128 devices in a mesh: pipe: 2 (over z_hi), dp: 32 (over y, x, z_lo), tensor: 2 (over core).
Axes of the slice: x: 4, y: 4, z: 4 (z_hi: 2, z_lo: 2; z = z_hi * 2 + z_lo), core: 2. Of those that a mesh axis runs over, the one named last changes fastest.
Arguments:
- tokens: bfloat16 [2, 8192, 1536], P(None, 'dp'), may hold values from -6 to 6
- cotangent: bfloat16 [2, 8192, 1536], P(None, 'dp'), may hold values from -6 to 6
- lengths: int32 [2, 32, 4], P(None, 'dp'), may hold values from 0 to 256, as said below
- norm_gain: float32 [2, 1536], P('pipe'), may hold values from 0.5 to 1.5
- w_zx: bfloat16 [2, 1536, 2, 3072], P('pipe', None, None, 'tensor'), may hold values from -0.15625 to 0.15625
- w_bc: bfloat16 [2, 1536, 256], P('pipe'), may hold values from -0.15625 to 0.15625
- w_dt: bfloat16 [2, 1536, 48], P('pipe', None, 'tensor'), may hold values from -0.15625 to 0.15625
- conv_x: float32 [2, 4, 3072], P('pipe', None, 'tensor'), may hold values from -3 to 3
- bias_x: float32 [2, 3072], P('pipe', 'tensor'), may hold values from -1.5 to 1.5
- conv_bc: float32 [2, 4, 256], P('pipe'), may hold values from -3 to 3
- bias_bc: float32 [2, 256], P('pipe'), may hold values from -1.5 to 1.5
- head_params: float32 [2, 3, 48], P('pipe', None, 'tensor'), may hold values from -5 to 2.7, as said below
- gate_gain: float32 [2, 3072], P('pipe', 'tensor'), may hold values from 0.5 to 1.5
- w_out: bfloat16 [2, 3072, 1536], P('pipe', 'tensor'), may hold values from -0.109375 to 0.109375
Outputs:
- section_out: float32 [2, 2, 8192, 1536], P('pipe', None, 'dp')
- section_grad: float32 [2, 2, 8192, 1536], P('pipe', None, 'dp')
- g_norm_gain: float32 [2, 1536], P('pipe')
- g_w_zx: float32 [2, 1536, 2, 3072], P('pipe', 'dp', None, 'tensor')
- g_w_bc: float32 [2, 1536, 256], P('pipe', ('dp', 'tensor'))
- g_w_dt: float32 [2, 1536, 48], P('pipe', 'dp', 'tensor')
- g_conv_x: float32 [2, 4, 3072], P('pipe', None, 'tensor')
- g_bias_x: float32 [2, 3072], P('pipe', 'tensor')
- g_conv_bc: float32 [2, 4, 256], P('pipe')
- g_bias_bc: float32 [2, 256], P('pipe')
- g_head_params: float32 [2, 3, 48], P('pipe', None, 'tensor')
- g_gate_gain: float32 [2, 3072], P('pipe', 'tensor')
- g_w_out: float32 [2, 3072, 1536], P('pipe', 'tensor', 'dp')
The draws below stay inside these ranges and needn't reach their ends.
Inputs may be any that keep to these rules, and one draw needn't show every extreme that they name: `lengths`: each row sums to at most 256; in every micro-batch one buffer is a single sequence of 256. `head_params`: row 0 shifts the step sizes, row 1 is the log of each head's decay rate, row 2 is the skip weight.
All inputs are finite; a program needn't handle non-finite values.
Results may differ from the reference program's by a relative error of at most 0.03.
Values may be sent and summed in bfloat16 or wider, within the bound.
No kernel may reach another device: no remote copies, remote signals or barrier semaphores. Data moves between devices by JAX's collectives and lax.ppermute only.
A program may use at most 256 MiB of HBM per device.

```python
import jax
import jax.numpy as jnp
from jax import lax

D = 1536
H = 48
NS = 128
K = 4
GROUP = 256
M = 2
SLOTS = 4
TOK_MB = 256
DI = 3072
TOKENS = 8192
N_DP = 32


def draw_lengths(key, part):
    key = jax.random.fold_in(key, 11)
    first, second, third = jax.random.split(key, 3)
    totals = jax.random.randint(first, (M, N_DP, 1), TOK_MB // 2, TOK_MB + 1).astype(jnp.int32)
    cuts = jnp.sort(jax.random.randint(second, (M, N_DP, SLOTS - 1), 0, TOK_MB + 1).astype(jnp.int32), axis=-1)
    cuts = jnp.minimum(cuts, totals)
    edges = jnp.concatenate([jnp.zeros((M, N_DP, 1), jnp.int32), cuts, totals], axis=-1)
    spans = edges[..., 1:] - edges[..., :-1]
    chosen_rank = jax.random.randint(third, (M, 1), 0, N_DP).astype(jnp.int32)
    single = jnp.zeros((SLOTS,), jnp.int32).at[0].set(TOK_MB)
    chosen = (jnp.arange(N_DP, dtype=jnp.int32)[None, :] == chosen_rank)[:, :, None]
    return jnp.where(chosen, single[None, None, :], spans).astype(jnp.int32)


def draw_head_params(key, part):
    key = jax.random.fold_in(key, 5)
    unit = jax.random.uniform(key, (2, 3, H), jnp.float32)
    lower_end = jnp.array([-5.0, 0.0, 0.5], jnp.float32)[None, :, None]
    upper_end = jnp.array([-2.0, 2.7, 1.5], jnp.float32)[None, :, None]
    return lower_end + (upper_end - lower_end) * unit


def shard_levels(stream_key, extent, cuts, smallest, high):
    def one(axis_at, parts):
        heights = jax.random.uniform(jax.random.fold_in(jax.random.fold_in(stream_key, 6), axis_at), (parts,), jnp.float32, smallest / len(cuts), high / len(cuts))
        return jnp.repeat(jnp.exp(heights), extent[axis_at] // parts).reshape((-1,) + (1,) * (len(extent) - axis_at - 1))

    gain = one(*cuts[0])
    for cut in cuts[1:]:
        gain = gain * one(*cut)
    return gain


def noise(stream_key, dims, scale, limit, cuts=(), held_as=jnp.bfloat16):
    level = shard_levels(stream_key, dims, cuts, -0.22, 0.18) if cuts else 1.0
    entries = jax.random.normal(stream_key, dims, jnp.float32) * scale * level
    return jnp.minimum(jnp.maximum(entries, -limit), limit).astype(held_as)


def setup_inputs(seed: int = 0) -> dict:
    arg_keys = jax.random.split(jax.random.key(seed), 15)
    return {
        "tokens": noise(arg_keys[0], (M, TOKENS, D), 1.0, 6.0, ((1, 32),)),
        "cotangent": noise(arg_keys[1], (M, TOKENS, D), 1.0, 6.0, ((1, 32),)),
        "lengths": draw_lengths(jax.random.fold_in(arg_keys[14], 71), 0),
        "norm_gain": jnp.clip(1.0 + 0.1 * jax.random.normal(arg_keys[3], (2, D), jnp.float32), 0.5, 1.5),
        "w_zx": noise(arg_keys[4], (2, D, 2, DI), D ** -0.5, 0.15625, ((0, 2), (3, 2))),
        "w_bc": noise(arg_keys[5], (2, D, 2 * NS), D ** -0.5, 0.15625, ((0, 2),)),
        "w_dt": noise(arg_keys[6], (2, D, H), D ** -0.5, 0.15625, ((0, 2), (2, 2))),
        "conv_x": noise(arg_keys[7], (2, K, DI), K ** -0.5, 3.0, ((0, 2), (2, 2)), jnp.float32),
        "bias_x": noise(arg_keys[8], (2, DI), 0.3, 1.5, ((0, 2), (1, 2)), jnp.float32),
        "conv_bc": noise(arg_keys[9], (2, K, 2 * NS), K ** -0.5, 3.0, ((0, 2),), jnp.float32),
        "bias_bc": noise(arg_keys[10], (2, 2 * NS), 0.3, 1.5, ((0, 2),), jnp.float32),
        "head_params": draw_head_params(jax.random.fold_in(arg_keys[14], 71), 0),
        "gate_gain": jnp.clip(1.0 + 0.1 * jax.random.normal(arg_keys[12], (2, DI), jnp.float32), 0.5, 1.5),
        "w_out": noise(arg_keys[13], (2, DI, D), DI ** -0.5, 0.109375, ((0, 2), (1, 2))),
    }


HIGH = lax.Precision.HIGHEST
EPS = 1e-05

@jax.custom_vjp
def low(v):
    return lax.optimization_barrier(v.astype(jnp.bfloat16)).astype(jnp.float32)

@jax.custom_vjp
def low_back(v):
    return v

def low_keep(v):
    return (low(v), None)

def low_pass(kept, grad):
    return (grad,)

def back_keep(v):
    return (v, None)

def back_low(kept, grad):
    return (low(grad),)
low.defvjp(low_keep, low_pass)
low_back.defvjp(back_keep, back_low)

def segment_ids(row, count):
    ends = jnp.cumsum(row).astype(jnp.int32)
    places = jnp.arange(count, dtype=jnp.int32)
    return lax.optimization_barrier(jnp.sum((places[:, None] >= ends[None, :]).astype(jnp.int32), axis=1)).astype(jnp.int32)

def causal_conv(values, kernel, bias, segs):
    taps = kernel.shape[0]
    count = values.shape[0]
    total = bias[None, :] + kernel[taps - 1][None, :] * values
    for back in range(1, taps):
        moved = jnp.pad(values, ((back, 0), (0, 0)))[:count]
        seg_moved = jnp.pad(segs, (back, 0), constant_values=-1)[:count]
        keep = (seg_moved == segs).astype(jnp.float32)
        total = total + kernel[taps - 1 - back][None, :] * moved * keep[:, None]
    return total

def ssd(values, steps, a_neg, bmat, cmat, segs, skip):
    count, nheads, width = values.shape
    blocks = count // GROUP
    rates = steps * a_neg[None, :]
    ends = segs[GROUP - 1::GROUP]
    prevs = jnp.concatenate([jnp.full((1,), -1, jnp.int32), ends[:-1].astype(jnp.int32)])
    rows = jnp.arange(GROUP, dtype=jnp.int32)

    def advance(state, pieces):
        vals, dts, rts, bs, cs, sg, prev = pieces
        cums = jnp.cumsum(rts, axis=0)
        cums_t = cums.T
        allowed = (rows[:, None] >= rows[None, :]) & (sg[:, None] == sg[None, :])
        decay = jnp.where(allowed[None, :, :], jnp.exp(jnp.minimum(cums_t[:, :, None] - cums_t[:, None, :], 0.0)), 0.0)
        scores = jnp.dot(cs, bs.T, precision=HIGH)
        mixing = scores[None, :, :] * decay * dts.T[:, None, :]
        inside = jnp.einsum('hij,jhp->ihp', mixing, vals, precision=HIGH)
        carried = jnp.where((sg == prev)[:, None], jnp.exp(cums), 0.0)
        before = jnp.einsum('in,hpn->ihp', cs, state, precision=HIGH) * carried[:, :, None]
        tails = jnp.where((sg == sg[-1])[:, None], jnp.exp(cums[-1][None, :] - cums), 0.0) * dts
        kept = jnp.where(sg[-1] == prev, jnp.exp(cums[-1]), 0.0)
        state = kept[:, None, None] * state + jnp.einsum('jhp,jn->hpn', tails[:, :, None] * vals, bs, precision=HIGH)
        return (state, inside + before + skip[None, :, None] * vals)
    pieces = (values.reshape(blocks, GROUP, nheads, width), steps.reshape(blocks, GROUP, nheads), rates.reshape(blocks, GROUP, nheads), bmat.reshape(blocks, GROUP, -1), cmat.reshape(blocks, GROUP, -1), segs.reshape(blocks, GROUP), prevs)
    start = jnp.zeros((nheads, width, bmat.shape[1]), jnp.float32)
    _, outs = lax.scan(advance, start, pieces)
    return outs.reshape(count, nheads, width)

def mid(zx, bcr, dtr, conv_x, bias_x, conv_bc, bias_bc, heads, segs):
    count = zx.shape[0]
    nheads = dtr.shape[1]
    nstate = bcr.shape[1] // 2
    xconv = jax.nn.silu(causal_conv(zx[:, 1], conv_x, bias_x, segs))
    bconv = jax.nn.silu(causal_conv(bcr, conv_bc, bias_bc, segs))
    steps = jax.nn.softplus(dtr + heads[0][None, :])
    a_neg = -jnp.exp(heads[1])
    y_out = ssd(xconv.reshape(count, nheads, -1), steps, a_neg, bconv[:, :nstate], bconv[:, nstate:], segs, heads[2])
    return y_out.reshape(count, -1) * jax.nn.silu(zx[:, 0])

def layer(u, params, segs):
    norm_gain, w_zx, w_bc, w_dt, conv_x, bias_x, conv_bc, bias_bc, heads, gate_gain, w_out = params
    s_zero = lax.rsqrt(lax.optimization_barrier(jnp.mean(u * u, axis=1, keepdims=True)) + EPS)
    r_low = low(u * s_zero * norm_gain[None, :])
    zx = low_back(jnp.einsum('td,dkc->tkc', r_low, w_zx, precision=HIGH))
    bcr = low_back(jnp.dot(r_low, w_bc, precision=HIGH))
    dtr = low_back(jnp.dot(r_low, w_dt, precision=HIGH))
    gated = mid(zx, bcr, dtr, conv_x, bias_x, conv_bc, bias_bc, heads, segs)
    scale = lax.rsqrt(lax.optimization_barrier(jnp.mean(gated * gated, axis=1, keepdims=True)) + EPS)
    n_low = low(gated * scale * gate_gain[None, :])
    out = low_back(jnp.dot(n_low, w_out, precision=HIGH))
    return u + out

def reference(tokens, cotangent, lengths, norm_gain, w_zx, w_bc, w_dt, conv_x, bias_x, conv_bc, bias_bc, head_params, gate_gain, w_out):
    count = TOK_MB
    batches = M * N_DP
    xf = tokens.astype(jnp.float32).reshape(batches, count, D)
    dyf = cotangent.astype(jnp.float32).reshape(batches, count, D)
    segs = jax.vmap(lambda row: segment_ids(row, count))(lengths.reshape(batches, SLOTS))
    weights = tuple((w.astype(jnp.float32) for w in (norm_gain, w_zx, w_bc, w_dt, conv_x, bias_x, conv_bc, bias_bc, head_params, gate_gain, w_out)))
    first = tuple((w[0] for w in weights))
    second = tuple((w[1] for w in weights))
    probe = jnp.zeros((batches, count, D), jnp.float32)

    def forward(inputs, probes, params_one, params_two):

        def one(carry, pieces):
            x_block, p_block, s_block = pieces
            kept = low(layer(x_block, params_one, s_block))
            return (carry, (layer(low_back(kept) + p_block, params_two, s_block), kept))
        _, (ys, hs) = lax.scan(jax.checkpoint(one), jnp.zeros((), jnp.float32), (inputs, probes, segs))
        return (ys, hs)
    ys, pull, hs = jax.vjp(forward, xf, probe, first, second, has_aux=True)
    dx, dh, grads_one, grads_two = pull(dyf)
    shape = (M, N_DP * count, D)
    section_out = jnp.stack([hs.reshape(shape), ys.reshape(shape)])
    section_grad = jnp.stack([dx.reshape(shape), dh.reshape(shape)])
    grads = tuple((jnp.stack([a, b]) for a, b in zip(grads_one, grads_two)))
    return (section_out, section_grad) + grads
```

```python
import functools

import jax
import jax.numpy as jnp
import numpy as np
from jax import lax
from jax.experimental import pallas as pl
from jax.experimental.pallas import tpu as pltpu
from jax.sharding import PartitionSpec as P

F32 = jnp.float32
BF16 = jnp.bfloat16
HIGH = lax.Precision.HIGHEST
EPS = 1e-05
T = 256
D = 1536
C = 1536
W = 256
STEPS = C // W
HEAD = 64
PER = W // HEAD
NS = 128
DI = 3072
LANES = 128
HALF = T // 2
NT = (((1,), (1,)), ((), ()))
VMEM_LIMIT = 56 * 1024 * 1024
SMALL_LIMIT = 16 * 1024 * 1024
COST = pl.CostEstimate(flops=1, bytes_accessed=1, transcendentals=0)


def dot(a, b):
    return jnp.dot(a, b, preferred_element_type=F32)


def dot_nt(a, b):
    return lax.dot_general(a, b, NT, preferred_element_type=F32)


def dot_exact(a, b):
    return jnp.dot(a, b, precision=HIGH, preferred_element_type=F32)


def params(steps):
    return pltpu.CompilerParams(
        dimension_semantics=("arbitrary",) * steps, vmem_limit_bytes=VMEM_LIMIT
    )


def sigmoid(v):
    return 1.0 / (1.0 + jnp.exp(-v))


def seg_ids(len_ref, micro, pos):
    end = jnp.int32(0)
    seg = jnp.zeros(pos.shape, jnp.int32)
    for k in range(4):
        end = end + len_ref[4 * micro + k]
        seg = seg + (pos >= end).astype(jnp.int32)
    return seg


def keep_masks(len_ref, micro):
    pos = lax.broadcasted_iota(jnp.int32, (T, LANES), 0)
    seg = seg_ids(len_ref, micro, pos)
    out = []
    for back in range(1, 4):
        same = (seg_ids(len_ref, micro, pos - back) == seg) & (pos >= back)
        out.append(same.astype(F32))
    return out


def wide(mask):
    return jnp.concatenate([mask] * (W // LANES), axis=1)


def conv(v, taps, bias, keeps):
    total = bias + taps[3] * v
    for back in range(1, 4):
        total = total + taps[3 - back] * (pltpu.roll(v, back, 0) * keeps[back - 1])
    return total


def conv_back(dtotal, v, taps, keeps):
    dv = taps[3] * dtotal
    grads = [None] * 4
    grads[3] = jnp.sum(dtotal * v, axis=0, keepdims=True)
    for back in range(1, 4):
        masked = dtotal * keeps[back - 1]
        grads[3 - back] = jnp.sum(masked * pltpu.roll(v, back, 0), axis=0, keepdims=True)
        dv = dv + taps[3 - back] * pltpu.roll(masked, T - back, 0)
    return dv, grads, jnp.sum(dtotal, axis=0, keepdims=True)


def rows_of(ref, count):
    return [ref[k : k + 1, :] for k in range(count)]


def tri_mask(len_ref, micro, transposed=False):
    first = lax.broadcasted_iota(jnp.int32, (T, T), 0)
    second = lax.broadcasted_iota(jnp.int32, (T, T), 1)
    same = seg_ids(len_ref, micro, first) == seg_ids(len_ref, micro, second)
    order = (second >= first) if transposed else (first >= second)
    return (same & order).astype(F32)


def lower_ones(transposed):
    first = lax.broadcasted_iota(jnp.int32, (T, T), 0)
    second = lax.broadcasted_iota(jnp.int32, (T, T), 1)
    return ((second >= first) if transposed else (first >= second)).astype(F32)


def softplus(v):
    return jnp.maximum(v, 0.0) + jnp.log1p(jnp.exp(-jnp.abs(v)))


def spread_steps(dt, cums, dt_s, cum_s, cumt_s):
    turned = cums.T
    for i in range(STEPS):
        shift = (LANES - PER * i) % LANES
        dt_s[i] = pltpu.roll(dt, shift, 1) if shift else dt
        cum_s[i] = pltpu.roll(cums, shift, 1) if shift else cums
        cumt_s[i, 0:PER, :] = turned[PER * i : PER * (i + 1), :]


def head_lanes(value, k):
    lane = lax.broadcasted_iota(jnp.int32, value.shape, 1)
    return jnp.where((lane >= k * HEAD) & (lane < (k + 1) * HEAD), value, jnp.zeros_like(value))


def per_channel(dt):
    lane = lax.broadcasted_iota(jnp.int32, (T, LANES), 1)
    tiles = []
    for p in range(PER // 2):
        tiles.append(
            jnp.where(
                lane < HEAD,
                jnp.broadcast_to(dt[:, 2 * p : 2 * p + 1], (T, LANES)),
                jnp.broadcast_to(dt[:, 2 * p + 1 : 2 * p + 2], (T, LANES)),
            )
        )
    return jnp.concatenate(tiles, axis=1)


def forward_kernel(
    micro,
    len_ref,
    u_ref,
    gain_ref,
    wzx_ref,
    wbc_ref,
    wdt_ref,
    cx_ref,
    bx_ref,
    cbc_ref,
    bbc_ref,
    hp_ref,
    skip_ref,
    gg_ref,
    wout_ref,
    _,
    rt_ref,
    z_ref,
    x_ref,
    y_ref,
    bcr_ref,
    dtr_ref,
    part0_ref,
    part1_ref,
    sq_ref,
    xt_ref,
    scoret_ref,
    cums_ref,
    r_s,
    keep_s,
    score_s,
    dt_s,
    cum_s,
    cumt_s,
    acc_s,
):
    step = pl.program_id(0)

    @pl.when(step == 0)
    def _():
        u = u_ref[...].astype(F32)
        s_zero = lax.rsqrt(jnp.mean(u * u, axis=1, keepdims=True) + EPS)
        r = u * s_zero * gain_ref[...]
        low = r.astype(BF16)
        r_s[...] = low
        rt_ref[...] = low.T
        keeps = keep_masks(len_ref, micro)
        for k in range(3):
            keep_s[k] = keeps[k]
        bcr = dot(low, wbc_ref[...])
        bcr_ref[...] = bcr
        dtr = dot_nt(low, wdt_ref[...])
        dtr_ref[...] = dtr
        total = conv(bcr, rows_of(cbc_ref, 4), bbc_ref[...], [wide(k) for k in keeps])
        act = total * sigmoid(total)
        score = dot_nt(act[:, NS:].astype(BF16), act[:, :NS].astype(BF16)) * tri_mask(
            len_ref, micro
        )
        score_s[...] = score
        scoret_ref[...] = score.T
        dt = softplus(dtr + hp_ref[0:1, :])
        rates = dt * (-jnp.exp(hp_ref[1:2, :]))
        cums = dot_exact(lower_ones(False), rates)
        cums_ref[...] = cums
        spread_steps(dt, cums, dt_s, cum_s, cumt_s)
        acc_s[...] = jnp.zeros_like(acc_s)
        sq_ref[...] = jnp.zeros_like(sq_ref)

    keeps = [wide(keep_s[k]) for k in range(3)]
    z = dot(r_s[...], wzx_ref[0])
    x = dot(r_s[...], wzx_ref[1])
    z_ref[...] = z
    x_ref[...] = x
    total = conv(x, rows_of(cx_ref, 4), bx_ref[...], keeps)
    xc = total * sigmoid(total)
    dt = dt_s[step]
    cums = cum_s[step]
    cumt = cumt_s[step]
    xt = (xc * per_channel(dt)).astype(BF16)
    xt_ref[...] = xt
    top = jnp.zeros((HALF, W), F32)
    bottom = jnp.zeros((HALF, W), F32)
    for k in range(PER):
        mine = head_lanes(xt, k)
        col = cums[:, k : k + 1]
        row = cumt[k : k + 1, :]
        mix = score_s[0:HALF, 0:HALF] * jnp.exp(jnp.minimum(col[:HALF] - row[:, :HALF], 0.0))
        top = top + dot(mix.astype(BF16), mine[:HALF])
        mix = score_s[HALF:T, :] * jnp.exp(jnp.minimum(col[HALF:] - row, 0.0))
        bottom = bottom + dot(mix.astype(BF16), mine)
    y = jnp.concatenate([top, bottom], axis=0) + skip_ref[...] * xc
    y_ref[...] = y
    g = y * (z * sigmoid(z))
    squares = g * g
    sq_ref[...] += squares[:, :LANES] + squares[:, LANES:]
    acc_s[...] += dot((g * gg_ref[...]).astype(BF16), wout_ref[...])

    @pl.when(step == STEPS - 1)
    def _():
        part0_ref[...] = acc_s[:HALF, :].astype(BF16)
        part1_ref[...] = acc_s[HALF:, :].astype(BF16)


def full(shape):
    return pl.BlockSpec(shape, lambda i: (0,) * len(shape))


def cols(rows):
    return pl.BlockSpec((rows, W), lambda i: (0, i))


def shape_of(shape, dtype):
    return jax.ShapeDtypeStruct(shape, dtype)


SMEM = pl.BlockSpec(memory_space=pltpu.SMEM)
VMEM = pl.BlockSpec(memory_space=pltpu.VMEM)
ANY = pl.BlockSpec(memory_space=pl.ANY)


def forward(micro, lens, u, wts, dep):
    outs = (
        shape_of((D, T), BF16),
        shape_of((T, C), F32),
        shape_of((T, C), F32),
        shape_of((T, C), F32),
        shape_of((T, 2 * NS), F32),
        shape_of((T, LANES), F32),
        shape_of((HALF, D), BF16),
        shape_of((HALF, D), BF16),
        shape_of((T, LANES), F32),
        shape_of((T, C), BF16),
        shape_of((T, T), F32),
        shape_of((T, LANES), F32),
    )
    return pl.pallas_call(
        functools.partial(forward_kernel, micro),
        grid=(STEPS,),
        in_specs=[
            SMEM,
            full((T, D)),
            full((1, D)),
            pl.BlockSpec((2, D, W), lambda i: (0, 0, i)),
            full((D, 2 * NS)),
            full((LANES, D)),
            cols(4),
            cols(1),
            full((4, 2 * NS)),
            full((1, 2 * NS)),
            full((8, LANES)),
            cols(1),
            cols(1),
            pl.BlockSpec((W, D), lambda i: (i, 0)),
            ANY,
        ],
        out_specs=[
            full((D, T)),
            cols(T),
            cols(T),
            cols(T),
            full((T, 2 * NS)),
            full((T, LANES)),
            full((HALF, D)),
            full((HALF, D)),
            full((T, LANES)),
            cols(T),
            full((T, T)),
            full((T, LANES)),
        ],
        out_shape=outs,
        scratch_shapes=[
            pltpu.VMEM((T, D), BF16),
            pltpu.VMEM((3, T, LANES), F32),
            pltpu.VMEM((T, T), F32),
            pltpu.VMEM((STEPS, T, LANES), F32),
            pltpu.VMEM((STEPS, T, LANES), F32),
            pltpu.VMEM((STEPS, 8, T), F32),
            pltpu.VMEM((T, D), F32),
        ],
        compiler_params=params(1),
        cost_estimate=COST,
        name="layer_forward",
    )(
        lens,
        u,
        wts["norm"],
        wts["zx"],
        wts["bc"],
        wts["dt"],
        wts["cx"],
        wts["bx"],
        wts["cbc"],
        wts["bbc"],
        wts["hp"],
        wts["skip"],
        wts["gate"],
        wts["out"],
        dep,
    )


def scale_of(sq0_ref, sq1_ref):
    squares = jnp.sum(sq0_ref[...] + sq1_ref[...], axis=1, keepdims=True)
    return lax.rsqrt(squares / DI + EPS)


def join_rows(mine, others):
    halves = [a[...].astype(F32) + b[...].astype(F32) for a, b in zip(mine, others)]
    return jnp.concatenate(halves, axis=0)


def join_kernel(u_ref, p0_ref, p1_ref, o0_ref, o1_ref, sq0_ref, sq1_ref, _, res_ref, low_ref):
    scale = scale_of(sq0_ref, sq1_ref)
    res = u_ref[...].astype(F32) + scale * join_rows((p0_ref, p1_ref), (o0_ref, o1_ref))
    res_ref[...] = res
    low_ref[...] = res.astype(BF16)


def join(u, part, other, sq, other_sq, dep):
    return pl.pallas_call(
        join_kernel,
        in_specs=[VMEM] * 7 + [ANY],
        out_specs=[VMEM] * 2,
        out_shape=(shape_of((T, D), F32), shape_of((T, D), BF16)),
        compiler_params=pltpu.CompilerParams(vmem_limit_bytes=SMALL_LIMIT),
        cost_estimate=COST,
        name="join_output",
    )(u, *part, *other, sq, other_sq, dep)


def gate_kernel(
    e_ref,
    p0_ref,
    p1_ref,
    o0_ref,
    o1_ref,
    sq0_ref,
    sq1_ref,
    z_ref,
    y_ref,
    gg_ref,
    wout_ref,
    _,
    et_ref,
    n_ref,
    dz_ref,
    dy_ref,
    ggrad_ref,
    scale_s,
    inner_s,
):
    step = pl.program_id(0)

    @pl.when(step == 0)
    def _():
        scale = scale_of(sq0_ref, sq1_ref)
        e = e_ref[...].astype(F32)
        total = join_rows((p0_ref, p1_ref), (o0_ref, o1_ref))
        inner = jnp.sum(e * total, axis=1, keepdims=True)
        scale_s[...] = jnp.broadcast_to(scale, (T, LANES))
        inner_s[...] = jnp.broadcast_to(inner * (scale * scale * scale) / DI, (T, LANES))
        et_ref[...] = e_ref[...].T

    scale = wide(scale_s[...])
    z = z_ref[...]
    y = y_ref[...]
    gg = gg_ref[...]
    dn = dot_nt(e_ref[...], wout_ref[...])
    sig = sigmoid(z)
    act = z * sig
    g = y * act
    normed = g * scale
    n_ref[...] = (normed * gg).astype(BF16)
    ggrad_ref[...] = jnp.sum(normed * dn, axis=0, keepdims=True)
    dg = scale * (gg * dn) - g * wide(inner_s[...])
    dy_ref[...] = dg * act
    dz_ref[...] = (dg * y * (sig * (1.0 + z * (1.0 - sig)))).astype(BF16)


def gate_back(e, part, other, sq, other_sq, z, y, wts, dep):
    return pl.pallas_call(
        gate_kernel,
        grid=(STEPS,),
        in_specs=[
            full((T, D)),
            full((HALF, D)),
            full((HALF, D)),
            full((HALF, D)),
            full((HALF, D)),
            full((T, LANES)),
            full((T, LANES)),
            cols(T),
            cols(T),
            cols(1),
            pl.BlockSpec((W, D), lambda i: (i, 0)),
            ANY,
        ],
        out_specs=[full((D, T)), cols(T), cols(T), cols(T), cols(1)],
        out_shape=(
            shape_of((D, T), BF16),
            shape_of((T, C), BF16),
            shape_of((T, C), BF16),
            shape_of((T, C), F32),
            shape_of((1, C), F32),
        ),
        scratch_shapes=[pltpu.VMEM((T, LANES), F32), pltpu.VMEM((T, LANES), F32)],
        compiler_params=params(1),
        cost_estimate=COST,
        name="gate_backward",
    )(e, *part, *other, sq, other_sq, z, y, wts["gate"], wts["out"], dep)


def scan_kernel(
    micro,
    len_ref,
    dz_ref,
    dy_ref,
    y_ref,
    x_ref,
    xt_ref,
    bcr_ref,
    dtr_ref,
    scoret_ref,
    cums_ref,
    wzx_ref,
    wbc_ref,
    wdt_ref,
    cx_ref,
    bx_ref,
    cbc_ref,
    bbc_ref,
    hp_ref,
    skip_ref,
    ggrad_ref,
    u_ref,
    _,
    dx_ref,
    bcdt_ref,
    dr0_ref,
    dr1_ref,
    pack_ref,
    keep_s,
    dt_s,
    cum_s,
    cumt_s,
    acc_s,
    dscore_s,
    dcum_s,
    ddt_s,
    dskip_s,
):
    step = pl.program_id(0)

    @pl.when(step == 0)
    def _():
        keeps = keep_masks(len_ref, micro)
        for k in range(3):
            keep_s[k] = keeps[k]
        dskip_s[...] = jnp.zeros_like(dskip_s)
        dt = softplus(dtr_ref[...] + hp_ref[0:1, :])
        cums = cums_ref[...]
        spread_steps(dt, cums, dt_s, cum_s, cumt_s)
        acc_s[...] = jnp.zeros_like(acc_s)
        dscore_s[...] = jnp.zeros_like(dscore_s)
        dcum_s[...] = jnp.zeros_like(dcum_s)
        ddt_s[...] = jnp.zeros_like(ddt_s)

    keeps = [wide(keep_s[k]) for k in range(3)]
    taps = rows_of(cx_ref, 4)
    x = x_ref[...]
    total = conv(x, taps, bx_ref[...], keeps)
    sig = sigmoid(total)
    xc = total * sig
    dt = dt_s[step]
    cums = cum_s[step]
    cumt = cumt_s[step]
    dtb = per_channel(dt)
    xt = xt_ref[...]
    dy = dy_ref[...]
    dyb = dy.astype(BF16)
    skip = skip_ref[...]
    inside = y_ref[...] - skip * xc
    top = jnp.zeros((HALF, W), F32)
    bottom = jnp.zeros((HALF, W), F32)
    for k in range(PER):
        my_dy = head_lanes(dyb, k)
        my_x = head_lanes(xt, k)
        col = cums[:, k : k + 1]
        row = cumt[k : k + 1, :]
        decay = jnp.exp(jnp.minimum(row - col[:HALF], 0.0))
        mix = scoret_ref[0:HALF, :] * decay
        top = top + dot(mix.astype(BF16), my_dy)
        dscore_s[0:HALF, :] += dot_nt(my_x[:HALF], dyb) * decay
        decay = jnp.exp(jnp.minimum(row[:, HALF:] - col[HALF:], 0.0))
        mix = scoret_ref[HALF:T, HALF:T] * decay
        bottom = bottom + dot(mix.astype(BF16), my_dy[HALF:])
        dscore_s[HALF:T, HALF:T] += dot_nt(my_x[HALF:], dyb[HALF:]) * decay
    dxt = jnp.concatenate([top, bottom], axis=0)
    chan = lax.broadcasted_iota(jnp.int32, (W, LANES), 0) // HEAD + PER * step
    lane = lax.broadcasted_iota(jnp.int32, (W, LANES), 1)
    group = (chan == lane).astype(F32)
    dcum_s[...] += dot_exact(dyb.astype(F32) * inside - xt.astype(F32) * dxt, group)
    ddt_s[...] += dot_exact(xc * dxt, group)
    dxc = dtb * dxt + skip * dy
    dskip = jnp.sum(dy * xc, axis=0, keepdims=True)
    dskip_s[...] += dot_exact(jnp.broadcast_to(dskip, (8, W)), group)
    dtotal = dxc * (sig * (1.0 + total * (1.0 - sig)))
    dx, grads, dbias = conv_back(dtotal, x, taps, keeps)
    here = pl.ds(pl.multiple_of(step * W, W), W)
    for k in range(4):
        pack_ref[k : k + 1, here] = grads[k]
    pack_ref[4:5, here] = dbias
    pack_ref[5:6, here] = ggrad_ref[...]
    low = dx.astype(BF16)
    dx_ref[...] = low
    acc_s[...] += dot_nt(dz_ref[...], wzx_ref[0]) + dot_nt(low, wzx_ref[1])

    @pl.when(step == STEPS - 1)
    def _():
        keeps = [wide(keep_s[k]) for k in range(3)]
        bcr = bcr_ref[...]
        taps = rows_of(cbc_ref, 4)
        total = conv(bcr, taps, bbc_ref[...], keeps)
        sig = sigmoid(total)
        act = total * sig
        dscore = dscore_s[...] * tri_mask(len_ref, micro, True)
        db = dot(dscore.astype(BF16), act[:, NS:].astype(BF16))
        dc = dot(dscore.T.astype(BF16), act[:, :NS].astype(BF16))
        dact = jnp.concatenate([db, dc], axis=1)
        dtotal = dact * (sig * (1.0 + total * (1.0 - sig)))
        dbc, grads, dbias = conv_back(dtotal, bcr, taps, keeps)
        for k, value in enumerate(grads + [dbias]):
            pack_ref[7:8, 2 * NS * k : 2 * NS * (k + 1)] = value
        pre = dtr_ref[...] + hp_ref[0:1, :]
        decay_rate = -jnp.exp(hp_ref[1:2, :])
        dt = softplus(pre)
        drates = dot_exact(lower_ones(True), dcum_s[...])
        lane = lax.broadcasted_iota(jnp.int32, (T, LANES), 1)
        ddt = (ddt_s[...] + drates * decay_rate) * sigmoid(pre)
        ddt = jnp.where(lane < C // HEAD, ddt, 0.0)
        shift = jnp.sum(ddt, axis=0, keepdims=True)
        decay = jnp.sum(drates * dt, axis=0, keepdims=True) * decay_rate
        decay = jnp.where(lane[0:1] < C // HEAD, decay, 0.0)
        both = jnp.concatenate([shift, decay, dskip_s[2:8, :]], axis=0)
        rolled = pltpu.roll(both, 32, 1)
        tile = both[0:1] + rolled[1:2] + pltpu.roll(both, 64, 1)[2:3]
        pack_ref[7:8, 10 * NS : 11 * NS] = tile
        pack_ref[7:8, 11 * NS :] = jnp.zeros((1, NS), F32)
        low_bc = dbc.astype(BF16)
        low_dt = ddt.astype(BF16)
        bcdt_ref[:, : 2 * NS] = low_bc
        bcdt_ref[:, 2 * NS :] = low_dt
        out = acc_s[...] + dot_nt(low_bc, wbc_ref[...]) + dot(low_dt, wdt_ref[...])
        dr0_ref[...] = out[:HALF].astype(BF16)
        dr1_ref[...] = out[HALF:].astype(BF16)
        u = u_ref[...].astype(F32)
        s_zero = lax.rsqrt(jnp.mean(u * u, axis=1, keepdims=True) + EPS)
        pack_ref[6:7, :] = jnp.sum(u * s_zero * out, axis=0, keepdims=True)


def scan_back(micro, lens, dz, dy, keep, wts, dep):
    return pl.pallas_call(
        functools.partial(scan_kernel, micro),
        grid=(STEPS,),
        in_specs=[
            SMEM,
            cols(T),
            cols(T),
            cols(T),
            cols(T),
            cols(T),
            full((T, 2 * NS)),
            full((T, LANES)),
            full((T, T)),
            full((T, LANES)),
            pl.BlockSpec((2, D, W), lambda i: (0, 0, i)),
            full((D, 2 * NS)),
            full((LANES, D)),
            cols(4),
            cols(1),
            full((4, 2 * NS)),
            full((1, 2 * NS)),
            full((8, LANES)),
            cols(1),
            cols(1),
            full((T, D)),
            ANY,
        ],
        out_specs=[
            cols(T),
            full((T, 3 * LANES)),
            full((HALF, D)),
            full((HALF, D)),
            full((8, C)),
        ],
        out_shape=(
            shape_of((T, C), BF16),
            shape_of((T, 3 * LANES), BF16),
            shape_of((HALF, D), BF16),
            shape_of((HALF, D), BF16),
            shape_of((8, C), F32),
        ),
        scratch_shapes=[
            pltpu.VMEM((3, T, LANES), F32),
            pltpu.VMEM((STEPS, T, LANES), F32),
            pltpu.VMEM((STEPS, T, LANES), F32),
            pltpu.VMEM((STEPS, 8, T), F32),
            pltpu.VMEM((T, D), F32),
            pltpu.VMEM((T, T), F32),
            pltpu.VMEM((T, LANES), F32),
            pltpu.VMEM((T, LANES), F32),
            pltpu.VMEM((8, LANES), F32),
        ],
        compiler_params=params(1),
        cost_estimate=COST,
        name="scan_backward",
    )(
        lens,
        dz,
        dy,
        keep["y"],
        keep["x"],
        keep["xt"],
        keep["bcr"],
        keep["dtr"],
        keep["scoret"],
        keep["cums"],
        wts["zx"],
        wts["bc"],
        wts["dt"],
        wts["cx"],
        wts["bx"],
        wts["cbc"],
        wts["bbc"],
        wts["hp"],
        wts["skip"],
        keep["ggrad"],
        keep["u"],
        dep,
    )


def input_kernel(e_ref, u_ref, gain_ref, d0_ref, d1_ref, o0_ref, o1_ref, _, du_ref, low_ref):
    u = u_ref[...].astype(F32)
    s_zero = lax.rsqrt(jnp.mean(u * u, axis=1, keepdims=True) + EPS)
    dr = join_rows((d0_ref, d1_ref), (o0_ref, o1_ref))
    gained = gain_ref[...] * dr
    shared = s_zero * s_zero * s_zero * jnp.mean(u * gained, axis=1, keepdims=True)
    du = e_ref[...].astype(F32) + s_zero * gained - u * shared
    du_ref[...] = du
    low_ref[...] = du.astype(BF16)


def input_back(e, u, dr, other, wts, dep):
    return pl.pallas_call(
        input_kernel,
        in_specs=[VMEM] * 7 + [ANY],
        out_specs=[VMEM] * 2,
        out_shape=(shape_of((T, D), F32), shape_of((T, D), BF16)),
        compiler_params=pltpu.CompilerParams(vmem_limit_bytes=SMALL_LIMIT),
        cost_estimate=COST,
        name="input_backward",
    )(e, u, wts["norm"], *dr, *other, dep)


def swap(value):
    return lax.ppermute(value, "tensor", [(0, 1), (1, 0)])


def relay(value, pairs):
    return lax.ppermute(value, "pipe", pairs)


def partners(count):
    if count == 32:

        def make(fn):
            return [fn(i // 8, (i // 2) % 4, i % 2) for i in range(count)]

        def pack(y, x, z):
            return y * 8 + x * 2 + z

        def wrap(v):
            return (v + 1) % 4 if v % 2 else (v - 1) % 4

        return [
            make(lambda y, x, z: pack(y, x ^ 1, z)),
            make(lambda y, x, z: pack(y ^ 1, x, z)),
            make(lambda y, x, z: pack(y, wrap(x), z)),
            make(lambda y, x, z: pack(wrap(y), x, z)),
            make(lambda y, x, z: pack(y, x, z ^ 1)),
        ]
    return [[i ^ (1 << k) for i in range(count)] for k in range(count.bit_length() - 1)]


STREAMS = 5


def stream_order(maps, stream):
    k = stream % len(maps)
    return maps[k:] + maps[:k]


def block_order(maps, stream, late=0):
    order = stream_order(maps, stream + late)
    count = len(order[0])
    table = np.zeros((count, count), np.int32)
    for me in range(count):
        for p in range(count):
            owner = me
            for k, step in enumerate(order):
                if (p >> (len(order) - 1 - k)) & 1:
                    owner = step[owner]
            table[me, owner] = p
    return table


TILES_EARLY = [("et", "n", LANES * k) for k in range(C // LANES)] + [
    ("rt", "dz", LANES * k) for k in range(C // LANES)
]
TILES_LATE = [("rt", "dx", LANES * k) for k in range(C // LANES)] + [
    ("rt", "bcdt", LANES * k) for k in range(3)
]


def deal(tiles):
    width = -(-len(tiles) // STREAMS)
    return [tiles[width * s : width * (s + 1)] for s in range(STREAMS)]


EARLY, LATE = deal(TILES_EARLY), deal(TILES_LATE)
PACK = 8
PACK_ROWS = 2 * PACK * (C // LANES)
PACK_STREAM = STREAMS - 1


def runs(tiles):
    out = []
    for at, (left, right, first) in enumerate(tiles):
        if out and out[-1][:2] == [left, right] and out[-1][2] + LANES * out[-1][3] == first:
            out[-1][3] += 1
        else:
            out.append([left, right, first, 1, at])
    return out


class Loader:
    def __init__(self, flag_ref, names, sources, held, sem):
        self.flag, self.names, self.sources, self.held, self.sem = flag_ref, names, sources, held, sem
        self.waited = set()

    def copy(self, k, m, early):
        span = pl.ds(m * T, T)
        ref = self.held[k]
        slot = ref.at[:, span] if ref.shape[0] == D else ref.at[span, :]
        return pltpu.make_async_copy(self.sources[4 * k + 2 * early + m], slot, self.sem.at[2 * k + m])

    def start(self, name):
        k = self.names.index(name)
        for m in range(2):
            pl.when(self.flag[0] == 1)(lambda: self.copy(k, m, 0).start())
            pl.when(self.flag[0] == 0)(lambda: self.copy(k, m, 1).start())

    def get(self, name):
        k = self.names.index(name)
        if name not in self.waited:
            self.waited.add(name)
            for m in range(2):
                self.copy(k, m, 0).wait()
        return self.held[k]


def held_shapes(arrays):
    shapes = []
    for a in arrays:
        rows, columns = a[0].shape
        shapes.append(pltpu.VMEM((rows, 2 * columns) if rows == D else (2 * rows, columns), BF16))
    return shapes


def products(loader, tiles, blocks, place):
    rows = D // blocks
    chunk = max(384, rows)
    for left, right, first, count, at in runs(tiles):
        lhs, rhs = loader.get(left), loader.get(right)
        for c in range(D // chunk):
            value = dot(
                lhs[c * chunk : (c + 1) * chunk, :], rhs[:, first : first + LANES * count]
            ).astype(BF16)
            for b in range(chunk // rows):
                for j in range(count):
                    place(
                        at + j,
                        c * (chunk // rows) + b,
                        value[b * rows : (b + 1) * rows, j * LANES : (j + 1) * LANES],
                    )


def early_kernel(blocks, flag_ref, table_ref, *refs):
    names = ["et", "n", "rt", "dz"]
    sources, refs = refs[:16], refs[16:]
    outs, (held, stage, in_sem, out_sem) = refs[: 2 * STREAMS], refs[2 * STREAMS :]
    loader = Loader(flag_ref, names, sources, held, in_sem)
    for name in names:
        loader.start(name)
    rows, half = D // blocks, D // 2

    def flush(s, side):
        source = stage[s % 2].at[pl.ds(0, len(EARLY[s])), pl.ds(side * half, half), :]
        return pltpu.make_async_copy(source, outs[2 * s + side], out_sem.at[2 * s + side])

    for s in range(STREAMS):
        if s >= 2:
            flush(s - 2, 0).wait()
            flush(s - 2, 1).wait()

        def place(tile, owner, value):
            start = pl.multiple_of(table_ref[s, owner] * rows, 16)
            stage[s % 2][tile, pl.ds(start, rows), :] = value

        products(loader, EARLY[s], blocks, place)
        flush(s, 0).start()
        flush(s, 1).start()
    for s in range(STREAMS - 2, STREAMS):
        flush(s, 0).wait()
        flush(s, 1).wait()


def early_grads(flag, table, arrays):
    out = []
    for s in range(STREAMS):
        out += [shape_of((len(EARLY[s]), D // 2, LANES), BF16)] * 2
    flat = pl.pallas_call(
        functools.partial(early_kernel, table.shape[1]),
        in_specs=[SMEM, SMEM] + [ANY] * 16,
        out_specs=[ANY] * len(out),
        out_shape=tuple(out),
        scratch_shapes=[
            held_shapes(arrays),
            [pltpu.VMEM((len(EARLY[0]), D, LANES), BF16) for _ in range(2)],
            pltpu.SemaphoreType.DMA((8,)),
            pltpu.SemaphoreType.DMA((2 * STREAMS,)),
        ],
        compiler_params=pltpu.CompilerParams(vmem_limit_bytes=VMEM_LIMIT),
        cost_estimate=COST,
        name="grad_early",
    )(flag, table, *[v for a in arrays for v in a])
    return list(flat[0::2]), list(flat[1::2])


def total_rows(s, early, late):
    return len(EARLY[s]) * early + len(LATE[s]) * late + (PACK_ROWS if s == PACK_STREAM else 0)


def split_pair(value):
    high = value.astype(BF16)
    return jnp.concatenate([high, (value - high.astype(F32)).astype(BF16)], axis=0)


def join_pair(pair):
    wide_pair = pair.astype(F32)
    return wide_pair[:PACK] + wide_pair[PACK:]


def late_kernel(blocks, flag_ref, table_ref, *refs):
    names = ["rt", "dx", "bcdt"]
    sources, refs = refs[:12], refs[12:]
    packs, refs = refs[:4], refs[4:]
    keeps, gots, refs = refs[:STREAMS], refs[STREAMS : 2 * STREAMS], refs[2 * STREAMS :]
    outs, (held, own, got, stage, in_sem, add_sem, out_sem) = refs[: 2 * STREAMS], refs[2 * STREAMS :]
    loader = Loader(flag_ref, names, sources, held, in_sem)
    for name in names:
        loader.start(name)
    rows, half = D // blocks, D // 2
    quarter = half // 2

    def fetch(s):
        span = pl.ds(0, len(EARLY[s]))
        return (
            pltpu.make_async_copy(keeps[s], own[s % 2].at[span], add_sem.at[2 * s]),
            pltpu.make_async_copy(gots[s], got[s % 2].at[span], add_sem.at[2 * s + 1]),
        )

    def flush(s, side):
        size = total_rows(s, quarter, half)
        source = stage[s % 2].at[pl.ds(side * size, size), :]
        return pltpu.make_async_copy(source, outs[2 * s + side], out_sem.at[2 * s + side])

    for s in range(2):
        for copy in fetch(s):
            copy.start()
    for s in range(STREAMS):
        size = total_rows(s, quarter, half)
        base = len(EARLY[s]) * quarter
        if s >= 2:
            flush(s - 2, 0).wait()
            flush(s - 2, 1).wait()

        def place(tile, owner, value):
            at = table_ref[s, owner] * rows
            at = at + jnp.where(at >= half, size - half, 0) + (base + tile * half)
            stage[s % 2][pl.ds(pl.multiple_of(at, 16), rows), :] = value

        products(loader, LATE[s], blocks, place)
        for copy in fetch(s):
            copy.wait()
        for j in range(len(EARLY[s])):
            total = (own[s % 2][j].astype(F32) + got[s % 2][j].astype(F32)).astype(BF16)
            stage[s % 2][j * quarter : (j + 1) * quarter, :] = total[:quarter]
            stage[s % 2][size + j * quarter : size + (j + 1) * quarter, :] = total[quarter:]
        if s + 2 < STREAMS:
            for copy in fetch(s + 2):
                copy.start()
        if s == PACK_STREAM:
            last = flag_ref[0] == 1
            total = jnp.where(last, packs[0][...] + packs[1][...], packs[2][...] + packs[3][...])
            for j in range(C // LANES):
                pair = split_pair(total[:, j * LANES : (j + 1) * LANES])
                at = size - PACK_ROWS + 2 * PACK * j
                stage[s % 2][at : at + 2 * PACK, :] = pair
                stage[s % 2][size + at : size + at + 2 * PACK, :] = pair
        flush(s, 0).start()
        flush(s, 1).start()
    for s in range(STREAMS - 2, STREAMS):
        flush(s, 0).wait()
        flush(s, 1).wait()


def late_grads(flag, table, arrays, packs, keeps, gots):
    out = []
    for s in range(STREAMS):
        out += [shape_of((total_rows(s, D // 4, D // 2), LANES), BF16)] * 2
    most = max(total_rows(s, D // 4, D // 2) for s in range(STREAMS))
    flat = pl.pallas_call(
        functools.partial(late_kernel, table.shape[1]),
        in_specs=[SMEM, SMEM] + [ANY] * 12 + [VMEM] * 4 + [ANY] * (2 * STREAMS),
        out_specs=[ANY] * len(out),
        out_shape=tuple(out),
        scratch_shapes=[
            held_shapes(arrays),
            [pltpu.VMEM((len(EARLY[0]), D // 2, LANES), BF16) for _ in range(2)],
            [pltpu.VMEM((len(EARLY[0]), D // 2, LANES), BF16) for _ in range(2)],
            [pltpu.VMEM((2 * most, LANES), BF16) for _ in range(2)],
            pltpu.SemaphoreType.DMA((6,)),
            pltpu.SemaphoreType.DMA((2 * STREAMS,)),
            pltpu.SemaphoreType.DMA((2 * STREAMS,)),
        ],
        compiler_params=pltpu.CompilerParams(vmem_limit_bytes=VMEM_LIMIT),
        cost_estimate=COST,
        name="grad_late",
    )(flag, table, *[v for a in arrays for v in a], *packs, *keeps, *gots)
    return list(flat[0::2]), list(flat[1::2])


def fold_kernel(early, late, *refs):
    ends = early * 32 == D
    keeps, gots = refs[:STREAMS], refs[STREAMS : 2 * STREAMS]
    outs = refs[2 * STREAMS :]
    for s in range(STREAMS):
        keep, got = keeps[s], gots[s]
        next_keep, next_send = outs[2 * s], outs[2 * s + 1]

        def add(at, rows):
            return keep[at : at + rows, :].astype(F32) + got[at : at + rows, :].astype(F32)

        at = to = 0
        for j in range(len(EARLY[s])):
            if ends:
                outs[2 * STREAMS + s][j * early : (j + 1) * early, :] = add(at, early)
            else:
                next_send[to : to + early // 2, :] = add(at + early // 2, early // 2).astype(BF16)
                next_keep[to : to + early // 2, :] = add(at, early // 2).astype(BF16)
                to += early // 2
            at += early
        for j in range(len(LATE[s])):
            next_send[to : to + late // 2, :] = add(at + late // 2, late // 2).astype(BF16)
            next_keep[to : to + late // 2, :] = add(at, late // 2).astype(BF16)
            at += late
            to += late // 2
        if s == PACK_STREAM:
            for j in range(C // LANES):
                span = slice(at + 2 * PACK * j, at + 2 * PACK * (j + 1))
                pair = split_pair(join_pair(keep[span, :]) + join_pair(got[span, :]))
                next_send[to + 2 * PACK * j : to + 2 * PACK * (j + 1), :] = pair
                next_keep[to + 2 * PACK * j : to + 2 * PACK * (j + 1), :] = pair


def fold(keeps, gots, early, late, ends):
    out = []
    for s in range(STREAMS):
        rows = total_rows(s, 0 if ends else early // 2, late // 2)
        out += [shape_of((rows, LANES), BF16)] * 2
    if ends:
        out += [shape_of((len(EARLY[s]) * early, LANES), F32) for s in range(STREAMS)]
    flat = pl.pallas_call(
        functools.partial(fold_kernel, early, late),
        in_specs=[VMEM] * (2 * STREAMS),
        out_specs=[VMEM] * len(out),
        out_shape=tuple(out),
        compiler_params=pltpu.CompilerParams(vmem_limit_bytes=SMALL_LIMIT),
        cost_estimate=COST,
        name="fold_grads",
    )(*keeps, *gots)
    return list(flat[0 : 2 * STREAMS : 2]), list(flat[1 : 2 * STREAMS : 2]), flat[2 * STREAMS :]


def end_kernel(early, late, *refs):
    dones, keeps, gots = refs[:STREAMS], refs[STREAMS : 2 * STREAMS], refs[2 * STREAMS : 3 * STREAMS]
    out_ref, zx_ref, bcdt_ref, pack_ref = refs[3 * STREAMS :]

    def place(right, first, value):
        if right == "n":
            out_ref[:, first : first + LANES] = value
        elif right == "bcdt":
            bcdt_ref[:, first : first + LANES] = value
        else:
            zx_ref[0 if right == "dz" else 1, :, first : first + LANES] = value

    for s in range(STREAMS):
        for j, (_, right, first) in enumerate(EARLY[s]):
            place(right, first, dones[s][j * early : (j + 1) * early, :])
        for j, (_, right, first) in enumerate(LATE[s]):
            span = slice(j * late, (j + 1) * late)
            place(right, first, keeps[s][span, :].astype(F32) + gots[s][span, :].astype(F32))
        if s == PACK_STREAM:
            at = len(LATE[s]) * late
            for j in range(C // LANES):
                span = slice(at + 2 * PACK * j, at + 2 * PACK * (j + 1))
                pack_ref[:, j * LANES : (j + 1) * LANES] = join_pair(keeps[s][span, :]) + join_pair(
                    gots[s][span, :]
                )


def end(dones, keeps, gots, rows):
    return pl.pallas_call(
        functools.partial(end_kernel, rows, rows),
        in_specs=[VMEM] * (3 * STREAMS),
        out_specs=[VMEM] * 4,
        out_shape=(
            shape_of((rows, C), F32),
            shape_of((2, rows, C), F32),
            shape_of((rows, 3 * LANES), F32),
            shape_of((PACK, C), F32),
        ),
        compiler_params=pltpu.CompilerParams(vmem_limit_bytes=SMALL_LIMIT),
        cost_estimate=COST,
        name="grad_end",
    )(*dones, *keeps, *gots)


def exchange(sends, maps, k):
    got = []
    for s in range(STREAMS):
        step = stream_order(maps, s)[k % len(maps)]
        got.append(lax.ppermute(sends[s], "dp", [(i, to) for i, to in enumerate(step)]))
    return got


def body(
    tokens,
    cotangent,
    lengths,
    norm_gain,
    w_zx,
    w_bc,
    w_dt,
    conv_x,
    bias_x,
    conv_bc,
    bias_bc,
    head_params,
    gate_gain,
    w_out,
):
    is_last = lax.axis_index("pipe") == 1
    core_at = lax.axis_index("tensor")
    lens = lengths.reshape(-1)
    heads = w_dt.shape[2]
    wts = {
        "norm": norm_gain,
        "zx": jnp.transpose(w_zx[0], (1, 0, 2)),
        "bc": w_bc[0],
        "dt": jnp.pad(w_dt[0].T, ((0, LANES - heads), (0, 0))),
        "cx": conv_x[0],
        "bx": bias_x,
        "cbc": conv_bc[0],
        "bbc": bias_bc,
        "hp": jnp.pad(head_params[0], ((0, 5), (0, LANES - heads))),
        "skip": jnp.repeat(head_params[0, 2], HEAD)[None],
        "gate": gate_gain,
        "out": w_out[0],
    }
    up = [(0, 1)]
    down = [(1, 0)]

    def run(m, u, dep):
        names = ("rt", "z", "x", "y", "bcr", "dtr", "part0", "part1", "sq", "xt", "scoret", "cums")
        keep = dict(zip(names, forward(m, lens, u, wts, dep)))
        keep["u"] = u
        keep["part"] = (keep["part0"], keep["part1"])
        keep["other"] = tuple(swap(v) for v in keep["part"])
        keep["other_sq"] = swap(keep["sq"])
        return keep

    def joined(keep, dep):
        return join(keep["u"], keep["part"], keep["other"], keep["sq"], keep["other_sq"], dep)

    def gate(keep, e, dep):
        names = ("et", "n", "dz", "dy", "ggrad")
        values = gate_back(
            e, keep["part"], keep["other"], keep["sq"], keep["other_sq"], keep["z"], keep["y"], wts, dep
        )
        keep["e"] = e
        keep.update(zip(names, values))

    def scan(m, keep, dep):
        names = ("dx", "bcdt", "dr0", "dr1", "pack")
        keep.update(zip(names, scan_back(m, lens, keep["dz"], keep["dy"], keep, wts, dep)))
        keep["dr"] = (keep["dr0"], keep["dr1"])
        keep["other_dr"] = tuple(swap(v) for v in keep["dr"])

    def finish(keep, dep):
        keep["du"], low = input_back(keep["e"], keep["u"], keep["dr"], keep["other_dr"], wts, dep)
        return low

    keep_a = run(0, tokens[0], lens)
    res_a, half_a = joined(keep_a, lens)
    sent_a = relay(half_a, up)
    keep_b = run(1, tokens[1], half_a)
    res_b, half_b = joined(keep_b, sent_a)
    sent_b = relay(half_b, up)
    keep_c = run(0, sent_a, half_b)
    keep_d = run(1, sent_b, keep_c["cums"])
    gate(keep_c, cotangent[0], keep_d["cums"])
    scan(0, keep_c, lens)
    back_c = finish(keep_c, lens)
    sent_c = relay(back_c, down)
    gate(keep_d, cotangent[1], back_c)
    scan(1, keep_d, lens)
    back_d = finish(keep_d, sent_c)
    sent_d = relay(back_d, down)
    gate(keep_a, sent_c, back_d)
    scan(0, keep_a, lens)
    gate(keep_b, sent_d, keep_a["dr0"])

    dp = lax.axis_size("dp")
    maps = partners(dp)
    me = lax.axis_index("dp")
    tables = np.stack([block_order(maps, s) for s in range(STREAMS)], axis=1)
    table = lax.dynamic_index_in_dim(jnp.asarray(tables), me, 0, keepdims=False)
    flag = is_last.astype(jnp.int32).reshape(1)

    def both(name):
        return (keep_c[name], keep_d[name], keep_a[name], keep_b[name])

    arrays = [both(k) for k in ("et", "n", "rt", "dz")]
    keeps, sends = early_grads(flag, table, arrays)
    gots = exchange(sends, maps, 0)
    scan(1, keep_b, keeps[0])
    late_table = lax.dynamic_index_in_dim(
        jnp.asarray(np.stack([block_order(maps, s, 1) for s in range(STREAMS)], axis=1)), me, 0, keepdims=False
    )
    arrays = [both(k) for k in ("rt", "dx", "bcdt")]
    keeps, sends = late_grads(flag, late_table, arrays, both("pack"), keeps, gots)
    first_late = keeps[0]
    early, late = D // 4, D // 2
    dones = None
    for k in range(1, len(maps)):
        gots = exchange(sends, maps, k)
        ends = k + 1 == len(maps)
        keeps, sends, dones = fold(keeps, gots, early, late, ends)
        early, late = early // 2, late // 2
    gots = exchange(sends, maps, len(maps))
    g_out, g_zx, bcdt, pack = end(dones, keeps, gots, D // dp)
    finish(keep_a, first_late)
    finish(keep_b, first_late)
    res_c, _ = joined(keep_c, first_late)
    res_d, _ = joined(keep_d, first_late)

    rows = D // dp // 2
    bc = bcdt[:, : 2 * NS]
    mine = lax.dynamic_slice_in_dim(bc, core_at * rows, rows, 0)
    theirs = lax.dynamic_slice_in_dim(bc, (1 - core_at) * rows, rows, 0)
    g_bc = mine + swap(theirs)
    g_dt = bcdt[:, 2 * NS : 2 * NS + heads]
    shared = pack[6:8] + swap(pack[6:8])
    g_norm = shared[0:1]
    g_shared = shared[1, : 10 * NS].reshape(5, 2 * NS)
    tile = pack[7, 10 * NS : 11 * NS]
    g_heads = jnp.stack([tile[32 * k : 32 * k + heads] for k in range(3)])

    section_out = jnp.stack(
        [
            jnp.where(is_last, res_c, res_a.astype(BF16).astype(F32)),
            jnp.where(is_last, res_d, res_b.astype(BF16).astype(F32)),
        ]
    )
    section_grad = jnp.stack(
        [
            jnp.where(is_last, keep_c["du"], keep_a["du"]),
            jnp.where(is_last, keep_d["du"], keep_b["du"]),
        ]
    )
    return (
        section_out[None],
        section_grad[None],
        g_norm,
        jnp.transpose(g_zx, (1, 0, 2))[None],
        g_bc[None],
        g_dt[None],
        pack[None, 0:4],
        pack[4:5],
        g_shared[None, :4],
        g_shared[4:5],
        g_heads[None],
        pack[5:6],
        g_out.T[None],
    )


def solution(mesh):
    in_specs = (
        P(None, "dp", None),
        P(None, "dp", None),
        P(None, "dp", None),
        P("pipe", None),
        P("pipe", None, None, "tensor"),
        P("pipe", None, None),
        P("pipe", None, "tensor"),
        P("pipe", None, "tensor"),
        P("pipe", "tensor"),
        P("pipe", None, None),
        P("pipe", None),
        P("pipe", None, "tensor"),
        P("pipe", "tensor"),
        P("pipe", "tensor", None),
    )
    out_specs = (
        P("pipe", None, "dp", None),
        P("pipe", None, "dp", None),
        P("pipe", None),
        P("pipe", "dp", None, "tensor"),
        P("pipe", ("dp", "tensor"), None),
        P("pipe", "dp", "tensor"),
        P("pipe", None, "tensor"),
        P("pipe", "tensor"),
        P("pipe", None, None),
        P("pipe", None),
        P("pipe", None, "tensor"),
        P("pipe", "tensor"),
        P("pipe", "tensor", "dp"),
    )
    return jax.shard_map(body, mesh=mesh, in_specs=in_specs, out_specs=out_specs, check_vma=False)
```

```python
import functools

import jax
import jax.numpy as jnp
import numpy as np
from jax import lax
from jax.experimental import pallas as pl
from jax.experimental.pallas import tpu as pltpu
from jax.sharding import PartitionSpec as P

F32 = jnp.float32
BF16 = jnp.bfloat16
HIGH = lax.Precision.HIGHEST
EPS = 1e-05
T = 256
D = 1536
C = 1536
W = 256
STEPS = C // W
HEAD = 64
PER = W // HEAD
NS = 128
DI = 3072
LANES = 128
HALF = T // 2
NT = (((1,), (1,)), ((), ()))
VMEM_LIMIT = 24 * 1024 * 1024
SMALL_LIMIT = 16 * 1024 * 1024
COST = pl.CostEstimate(flops=1, bytes_accessed=1, transcendentals=0)


def dot(a, b):
    return jnp.dot(a, b, preferred_element_type=F32)


def dot_nt(a, b):
    return lax.dot_general(a, b, NT, preferred_element_type=F32)


def dot_exact(a, b):
    return jnp.dot(a, b, precision=HIGH, preferred_element_type=F32)


def params(steps):
    return pltpu.CompilerParams(
        dimension_semantics=("arbitrary",) * steps, vmem_limit_bytes=VMEM_LIMIT
    )


def sigmoid(v):
    return 1.0 / (1.0 + jnp.exp(-v))


def seg_ids(len_ref, micro, pos):
    end = jnp.int32(0)
    seg = jnp.zeros(pos.shape, jnp.int32)
    for k in range(4):
        end = end + len_ref[4 * micro + k]
        seg = seg + (pos >= end).astype(jnp.int32)
    return seg


def keep_masks(len_ref, micro):
    pos = lax.broadcasted_iota(jnp.int32, (T, LANES), 0)
    seg = seg_ids(len_ref, micro, pos)
    out = []
    for back in range(1, 4):
        same = (seg_ids(len_ref, micro, pos - back) == seg) & (pos >= back)
        out.append(same.astype(F32))
    return out


def wide(mask, width=W):
    return jnp.concatenate([mask] * (width // LANES), axis=1)


def conv(v, taps, bias, keeps):
    total = bias + taps[3] * v
    for back in range(1, 4):
        total = total + taps[3 - back] * (pltpu.roll(v, back, 0) * keeps[back - 1])
    return total


def conv_back(dtotal, v, taps, keeps):
    dv = taps[3] * dtotal
    grads = [None] * 4
    grads[3] = jnp.sum(dtotal * v, axis=0, keepdims=True)
    for back in range(1, 4):
        masked = dtotal * keeps[back - 1]
        grads[3 - back] = jnp.sum(masked * pltpu.roll(v, back, 0), axis=0, keepdims=True)
        dv = dv + taps[3 - back] * pltpu.roll(masked, T - back, 0)
    return dv, grads, jnp.sum(dtotal, axis=0, keepdims=True)


def rows_of(ref, count):
    return [ref[k : k + 1, :] for k in range(count)]


def tri_mask(len_ref, micro, transposed=False):
    first = lax.broadcasted_iota(jnp.int32, (T, T), 0)
    second = lax.broadcasted_iota(jnp.int32, (T, T), 1)
    same = seg_ids(len_ref, micro, first) == seg_ids(len_ref, micro, second)
    order = (second >= first) if transposed else (first >= second)
    return (same & order).astype(F32)


def lower_ones(transposed):
    first = lax.broadcasted_iota(jnp.int32, (T, T), 0)
    second = lax.broadcasted_iota(jnp.int32, (T, T), 1)
    return ((second >= first) if transposed else (first >= second)).astype(F32)


def softplus(v):
    return jnp.maximum(v, 0.0) + jnp.log1p(jnp.exp(-jnp.abs(v)))


def spread_steps(dt, cums, dt_s, cum_s, cumt_s):
    turned = cums.T
    for i in range(STEPS):
        shift = (LANES - PER * i) % LANES
        dt_s[i] = pltpu.roll(dt, shift, 1) if shift else dt
        cum_s[i] = pltpu.roll(cums, shift, 1) if shift else cums
        cumt_s[i, 0:PER, :] = turned[PER * i : PER * (i + 1), :]


def head_lanes(value, k):
    lane = lax.broadcasted_iota(jnp.int32, value.shape, 1)
    return jnp.where((lane >= k * HEAD) & (lane < (k + 1) * HEAD), value, jnp.zeros_like(value))


def per_channel(dt):
    lane = lax.broadcasted_iota(jnp.int32, (T, LANES), 1)
    tiles = []
    for p in range(PER // 2):
        tiles.append(
            jnp.where(
                lane < HEAD,
                jnp.broadcast_to(dt[:, 2 * p : 2 * p + 1], (T, LANES)),
                jnp.broadcast_to(dt[:, 2 * p + 1 : 2 * p + 2], (T, LANES)),
            )
        )
    return jnp.concatenate(tiles, axis=1)


def forward_kernel(
    micro,
    len_ref,
    u_ref,
    gain_ref,
    wzx_ref,
    wbc_ref,
    wdt_ref,
    cx_ref,
    bx_ref,
    cbc_ref,
    bbc_ref,
    hp_ref,
    skip_ref,
    gg_ref,
    wout_ref,
    _,
    rt_ref,
    z_ref,
    x_ref,
    y_ref,
    bcr_ref,
    dtr_ref,
    part0_ref,
    part1_ref,
    sq_ref,
    xt_ref,
    scoret_ref,
    cums_ref,
    token_ref,
    r_s,
    keep_s,
    score_s,
    dt_s,
    cum_s,
    cumt_s,
    acc_s,
):
    step = pl.program_id(0)

    @pl.when(step == 0)
    def _():
        u = u_ref[...].astype(F32)
        s_zero = lax.rsqrt(jnp.mean(u * u, axis=1, keepdims=True) + EPS)
        r = u * s_zero * gain_ref[...]
        low = r.astype(BF16)
        r_s[...] = low
        rt_ref[...] = low.T
        keeps = keep_masks(len_ref, micro)
        for k in range(3):
            keep_s[k] = keeps[k]
        bcr = dot(low, wbc_ref[...])
        bcr_ref[...] = bcr
        dtr = dot_nt(low, wdt_ref[...])
        dtr_ref[...] = dtr
        total = conv(bcr, rows_of(cbc_ref, 4), bbc_ref[...], [wide(k, 2 * NS) for k in keeps])
        act = total * sigmoid(total)
        score = dot_nt(act[:, NS:].astype(BF16), act[:, :NS].astype(BF16)) * tri_mask(
            len_ref, micro
        )
        score_s[...] = score
        scoret_ref[...] = score.T
        dt = softplus(dtr + hp_ref[0:1, :])
        rates = dt * (-jnp.exp(hp_ref[1:2, :]))
        cums = dot_exact(lower_ones(False), rates)
        cums_ref[...] = cums
        spread_steps(dt, cums, dt_s, cum_s, cumt_s)
        acc_s[...] = jnp.zeros_like(acc_s)
        sq_ref[...] = jnp.zeros_like(sq_ref)

    here = pl.ds(pl.multiple_of(step * W, W), W)
    keeps = [wide(keep_s[k]) for k in range(3)]
    z = dot(r_s[...], wzx_ref[0, :, here])
    x = dot(r_s[...], wzx_ref[1, :, here])
    z_ref[...] = z
    x_ref[...] = x
    total = conv(x, rows_of(cx_ref, 4), bx_ref[...], keeps)
    xc = total * sigmoid(total)
    dt = dt_s[step]
    cums = cum_s[step]
    cumt = cumt_s[step]
    xt = (xc * per_channel(dt)).astype(BF16)
    xt_ref[...] = xt
    top = jnp.zeros((HALF, W), F32)
    bottom = jnp.zeros((HALF, W), F32)
    for k in range(PER):
        mine = head_lanes(xt, k)
        col = cums[:, k : k + 1]
        row = cumt[k : k + 1, :]
        mix = score_s[0:HALF, 0:HALF] * jnp.exp(jnp.minimum(col[:HALF] - row[:, :HALF], 0.0))
        top = top + dot(mix.astype(BF16), mine[:HALF])
        mix = score_s[HALF:T, :] * jnp.exp(jnp.minimum(col[HALF:] - row, 0.0))
        bottom = bottom + dot(mix.astype(BF16), mine)
    y = jnp.concatenate([top, bottom], axis=0) + skip_ref[...] * xc
    y_ref[...] = y
    g = y * (z * sigmoid(z))
    squares = g * g
    for k in range(W // LANES):
        sq_ref[...] += squares[:, k * LANES : (k + 1) * LANES]
    acc_s[...] += dot((g * gg_ref[...]).astype(BF16), wout_ref[here, :])

    @pl.when(step == STEPS - 1)
    def _():
        part0_ref[...] = acc_s[:HALF, :].astype(BF16)
        part1_ref[...] = acc_s[HALF:, :].astype(BF16)
        token_ref[...] = jnp.zeros(TOKEN, F32)


def full(shape):
    return pl.BlockSpec(shape, lambda i: (0,) * len(shape))


def cols(rows):
    return pl.BlockSpec((rows, W), lambda i: (0, i))


def shape_of(shape, dtype):
    return jax.ShapeDtypeStruct(shape, dtype)


def far(shape, dtype):
    return pltpu.HBM(shape, dtype)


def near(shape, dtype):
    return pltpu.VMEM(shape, dtype)


def to_near(value):
    return pltpu.with_memory_space_constraint(value, pltpu.VMEM)


class Rows:
    def __init__(self, array, m=None):
        self.array, self.m = array, m

    def spec(self):
        if self.m is None:
            return pl.BlockSpec((T, D), lambda *i: (0, 0))
        return pl.BlockSpec((None, T, D), lambda *i: (self.m, 0, 0))


def from_far(value):
    return pltpu.with_memory_space_constraint(value, pltpu.HBM)


TOKEN = (8, LANES)


SMEM = pl.BlockSpec(memory_space=pltpu.SMEM)
VMEM = pl.BlockSpec(memory_space=pltpu.VMEM)
ANY = pl.BlockSpec(memory_space=pl.ANY)
HBM = pl.BlockSpec(memory_space=pltpu.HBM)


def forward(micro, lens, u, wts, dep):
    outs = (
        far((D, T), BF16),
        far((T, C), F32),
        far((T, C), F32),
        far((T, C), F32),
        far((T, 2 * NS), F32),
        far((T, LANES), F32),
        shape_of((HALF, D), BF16),
        shape_of((HALF, D), BF16),
        shape_of((T, LANES), F32),
        far((T, C), BF16),
        far((T, T), F32),
        far((T, LANES), F32),
        shape_of(TOKEN, F32),
    )
    return pl.pallas_call(
        functools.partial(forward_kernel, micro),
        grid=(STEPS,),
        in_specs=[
            SMEM,
            u.spec(),
            full((1, D)),
            VMEM,
            full((D, 2 * NS)),
            full((LANES, D)),
            cols(4),
            cols(1),
            full((4, 2 * NS)),
            full((1, 2 * NS)),
            full((8, LANES)),
            cols(1),
            cols(1),
            VMEM,
            ANY,
        ],
        out_specs=[
            full((D, T)),
            cols(T),
            cols(T),
            cols(T),
            full((T, 2 * NS)),
            full((T, LANES)),
            full((HALF, D)),
            full((HALF, D)),
            full((T, LANES)),
            cols(T),
            full((T, T)),
            full((T, LANES)),
            full(TOKEN),
        ],
        out_shape=outs,
        scratch_shapes=[
            pltpu.VMEM((T, D), BF16),
            pltpu.VMEM((3, T, LANES), F32),
            pltpu.VMEM((T, T), F32),
            pltpu.VMEM((STEPS, T, LANES), F32),
            pltpu.VMEM((STEPS, T, LANES), F32),
            pltpu.VMEM((STEPS, 8, T), F32),
            pltpu.VMEM((T, D), F32),
        ],
        compiler_params=params(1),
        cost_estimate=COST,
        name="layer_forward",
    )(
        lens,
        u.array,
        wts["norm"],
        wts["zx"],
        wts["bc"],
        wts["dt"],
        wts["cx"],
        wts["bx"],
        wts["cbc"],
        wts["bbc"],
        wts["hp"],
        wts["skip"],
        wts["gate"],
        wts["out"],
        dep,
    )


def touch_kernel(*refs):
    refs[-1][...] = jnp.zeros(TOKEN, F32)


def touch(*values):
    return pl.pallas_call(
        touch_kernel,
        in_specs=[ANY] * len(values),
        out_specs=VMEM,
        out_shape=shape_of(TOKEN, F32),
        compiler_params=pltpu.CompilerParams(vmem_limit_bytes=SMALL_LIMIT),
        cost_estimate=COST,
        name="touch",
    )(*values)


def scale_of(sq0_ref, sq1_ref):
    squares = jnp.sum(sq0_ref[...] + sq1_ref[...], axis=1, keepdims=True)
    return lax.rsqrt(squares / DI + EPS)


def join_rows(mine, others):
    halves = [a[...].astype(F32) + b[...].astype(F32) for a, b in zip(mine, others)]
    return jnp.concatenate(halves, axis=0)


def join_kernel(round_out, u_ref, p0_ref, p1_ref, o0_ref, o1_ref, sq0_ref, sq1_ref, _, res_ref, low_ref, token_ref):
    scale = scale_of(sq0_ref, sq1_ref)
    res = u_ref[...].astype(F32) + scale * join_rows((p0_ref, p1_ref), (o0_ref, o1_ref))
    low = res.astype(BF16)
    res_ref[...] = low.astype(F32) if round_out else res
    low_ref[...] = low
    token_ref[...] = jnp.zeros(TOKEN, F32)


def join(round_out, u, part, other, sq, other_sq, dep):
    return pl.pallas_call(
        functools.partial(join_kernel, round_out),
        grid=(1,),
        in_specs=[u.spec()] + [VMEM] * 6 + [ANY],
        out_specs=[full((T, D)), VMEM, VMEM],
        out_shape=(far((T, D), F32), shape_of((T, D), BF16), shape_of(TOKEN, F32)),
        compiler_params=pltpu.CompilerParams(vmem_limit_bytes=SMALL_LIMIT),
        cost_estimate=COST,
        name="join_output",
    )(u.array, *part, *other, sq, other_sq, dep)


def gate_kernel(
    role,
    flag_ref,
    e_ref,
    p0_ref,
    p1_ref,
    o0_ref,
    o1_ref,
    sq0_ref,
    sq1_ref,
    z_ref,
    y_ref,
    gg_ref,
    wout_ref,
    _,
    et_ref,
    n_ref,
    dz_ref,
    dy_ref,
    ggrad_ref,
    scale_s,
    inner_s,
):
    step = pl.program_id(0)

    @pl.when((flag_ref[0] == 1) | (role == 0))
    def _():
        @pl.when(step == 0)
        def _():
            scale = scale_of(sq0_ref, sq1_ref)
            e = e_ref[...].astype(F32)
            total = join_rows((p0_ref, p1_ref), (o0_ref, o1_ref))
            inner = jnp.sum(e * total, axis=1, keepdims=True)
            scale_s[...] = jnp.broadcast_to(scale, (T, LANES))
            inner_s[...] = jnp.broadcast_to(inner * (scale * scale * scale) / DI, (T, LANES))
            et_ref[...] = e_ref[...].T

        scale = wide(scale_s[...])
        z = z_ref[...]
        y = y_ref[...]
        gg = gg_ref[...]
        dn = dot_nt(e_ref[...], wout_ref[...])
        sig = sigmoid(z)
        act = z * sig
        g = y * act
        normed = g * scale
        n_ref[...] = (normed * gg).astype(BF16)
        ggrad_ref[...] = jnp.sum(normed * dn, axis=0, keepdims=True)
        dg = scale * (gg * dn) - g * wide(inner_s[...])
        dy_ref[...] = dg * act
        dz_ref[...] = (dg * y * (sig * (1.0 + z * (1.0 - sig)))).astype(BF16)


def gate_back(role, flag, e, part, other, sq, other_sq, z, y, wts, dep):
    return pl.pallas_call(
        functools.partial(gate_kernel, role),
        grid=(STEPS,),
        in_specs=[
            SMEM,
            e.spec(),
            full((HALF, D)),
            full((HALF, D)),
            full((HALF, D)),
            full((HALF, D)),
            full((T, LANES)),
            full((T, LANES)),
            cols(T),
            cols(T),
            cols(1),
            pl.BlockSpec((W, D), lambda i: (i, 0)),
            ANY,
        ],
        out_specs=[full((D, T)), cols(T), cols(T), cols(T), cols(1)],
        out_shape=(
            far((D, T), BF16),
            far((T, C), BF16),
            far((T, C), BF16),
            far((T, C), F32),
            far((1, C), F32),
        ),
        scratch_shapes=[pltpu.VMEM((T, LANES), F32), pltpu.VMEM((T, LANES), F32)],
        compiler_params=params(1),
        cost_estimate=COST,
        name="gate_backward",
    )(
        flag,
        from_far(e.array),
        *[from_far(v) for v in (*part, *other, sq, other_sq, z, y)],
        wts["gate"],
        from_far(wts["far_out"]),
        dep,
    )


def scan_kernel(
    micro,
    role,
    flag_ref,
    len_ref,
    dz_ref,
    dy_ref,
    y_ref,
    x_ref,
    xt_ref,
    bcr_ref,
    dtr_ref,
    scoret_ref,
    cums_ref,
    wzx_ref,
    wbc_ref,
    wdt_ref,
    cx_ref,
    bx_ref,
    cbc_ref,
    bbc_ref,
    hp_ref,
    skip_ref,
    ggrad_ref,
    u_ref,
    _,
    dx_ref,
    bcdt_ref,
    dr0_ref,
    dr1_ref,
    pack_ref,
    token_ref,
    keep_s,
    dt_s,
    cum_s,
    cumt_s,
    acc_s,
    dscore_s,
    dcum_s,
    ddt_s,
    dskip_s,
):
    step = pl.program_id(0)

    @pl.when((flag_ref[0] == 0) & (role == 1))
    def _():
        dr0_ref[...] = jnp.zeros_like(dr0_ref)
        dr1_ref[...] = jnp.zeros_like(dr1_ref)
        token_ref[...] = jnp.zeros(TOKEN, F32)

    @pl.when((flag_ref[0] == 1) | (role == 0))
    def _():
        @pl.when(step == 0)
        def _():
            keeps = keep_masks(len_ref, micro)
            for k in range(3):
                keep_s[k] = keeps[k]
            dskip_s[...] = jnp.zeros_like(dskip_s)
            dt = softplus(dtr_ref[...] + hp_ref[0:1, :])
            cums = cums_ref[...]
            spread_steps(dt, cums, dt_s, cum_s, cumt_s)
            acc_s[...] = jnp.zeros_like(acc_s)
            dscore_s[...] = jnp.zeros_like(dscore_s)
            dcum_s[...] = jnp.zeros_like(dcum_s)
            ddt_s[...] = jnp.zeros_like(ddt_s)

        keeps = [wide(keep_s[k]) for k in range(3)]
        taps = rows_of(cx_ref, 4)
        x = x_ref[...]
        total = conv(x, taps, bx_ref[...], keeps)
        sig = sigmoid(total)
        xc = total * sig
        dt = dt_s[step]
        cums = cum_s[step]
        cumt = cumt_s[step]
        dtb = per_channel(dt)
        xt = xt_ref[...]
        dy = dy_ref[...]
        dyb = dy.astype(BF16)
        skip = skip_ref[...]
        inside = y_ref[...] - skip * xc
        top = jnp.zeros((HALF, W), F32)
        bottom = jnp.zeros((HALF, W), F32)
        for k in range(PER):
            my_dy = head_lanes(dyb, k)
            my_x = head_lanes(xt, k)
            col = cums[:, k : k + 1]
            row = cumt[k : k + 1, :]
            decay = jnp.exp(jnp.minimum(row - col[:HALF], 0.0))
            mix = scoret_ref[0:HALF, :] * decay
            top = top + dot(mix.astype(BF16), my_dy)
            dscore_s[0:HALF, :] += dot_nt(my_x[:HALF], dyb) * decay
            decay = jnp.exp(jnp.minimum(row[:, HALF:] - col[HALF:], 0.0))
            mix = scoret_ref[HALF:T, HALF:T] * decay
            bottom = bottom + dot(mix.astype(BF16), my_dy[HALF:])
            dscore_s[HALF:T, HALF:T] += dot_nt(my_x[HALF:], dyb[HALF:]) * decay
        dxt = jnp.concatenate([top, bottom], axis=0)
        chan = lax.broadcasted_iota(jnp.int32, (W, LANES), 0) // HEAD + PER * step
        lane = lax.broadcasted_iota(jnp.int32, (W, LANES), 1)
        group = (chan == lane).astype(F32)
        dcum_s[...] += dot_exact(dyb.astype(F32) * inside - xt.astype(F32) * dxt, group)
        ddt_s[...] += dot_exact(xc * dxt, group)
        dxc = dtb * dxt + skip * dy
        dskip = jnp.sum(dy * xc, axis=0, keepdims=True)
        dskip_s[...] += dot_exact(jnp.broadcast_to(dskip, (8, W)), group)
        dtotal = dxc * (sig * (1.0 + total * (1.0 - sig)))
        dx, grads, dbias = conv_back(dtotal, x, taps, keeps)
        here = pl.ds(pl.multiple_of(step * W, W), W)
        for k in range(4):
            pack_ref[k : k + 1, here] = grads[k]
        pack_ref[4:5, here] = dbias
        pack_ref[5:6, here] = ggrad_ref[...]
        low = dx.astype(BF16)
        dx_ref[...] = low
        acc_s[...] += dot_nt(dz_ref[...], wzx_ref[0]) + dot_nt(low, wzx_ref[1])

        @pl.when(step == STEPS - 1)
        def _():
            keeps = [wide(keep_s[k], 2 * NS) for k in range(3)]
            bcr = bcr_ref[...]
            taps = rows_of(cbc_ref, 4)
            total = conv(bcr, taps, bbc_ref[...], keeps)
            sig = sigmoid(total)
            act = total * sig
            dscore = dscore_s[...] * tri_mask(len_ref, micro, True)
            db = dot(dscore.astype(BF16), act[:, NS:].astype(BF16))
            dc = dot(dscore.T.astype(BF16), act[:, :NS].astype(BF16))
            dact = jnp.concatenate([db, dc], axis=1)
            dtotal = dact * (sig * (1.0 + total * (1.0 - sig)))
            dbc, grads, dbias = conv_back(dtotal, bcr, taps, keeps)
            for k, value in enumerate(grads + [dbias]):
                pack_ref[7:8, 2 * NS * k : 2 * NS * (k + 1)] = value
            pre = dtr_ref[...] + hp_ref[0:1, :]
            decay_rate = -jnp.exp(hp_ref[1:2, :])
            dt = softplus(pre)
            drates = dot_exact(lower_ones(True), dcum_s[...])
            lane = lax.broadcasted_iota(jnp.int32, (T, LANES), 1)
            ddt = (ddt_s[...] + drates * decay_rate) * sigmoid(pre)
            ddt = jnp.where(lane < C // HEAD, ddt, 0.0)
            shift = jnp.sum(ddt, axis=0, keepdims=True)
            decay = jnp.sum(drates * dt, axis=0, keepdims=True) * decay_rate
            decay = jnp.where(lane[0:1] < C // HEAD, decay, 0.0)
            both = jnp.concatenate([shift, decay, dskip_s[2:8, :]], axis=0)
            rolled = pltpu.roll(both, 32, 1)
            tile = both[0:1] + rolled[1:2] + pltpu.roll(both, 64, 1)[2:3]
            pack_ref[7:8, 10 * NS : 11 * NS] = tile
            pack_ref[7:8, 11 * NS :] = jnp.zeros((1, NS), F32)
            low_bc = dbc.astype(BF16)
            low_dt = ddt.astype(BF16)
            bcdt_ref[:, : 2 * NS] = low_bc
            bcdt_ref[:, 2 * NS :] = low_dt
            out = acc_s[...] + dot_nt(low_bc, wbc_ref[...]) + dot(low_dt, wdt_ref[...])
            dr0_ref[...] = out[:HALF].astype(BF16)
            dr1_ref[...] = out[HALF:].astype(BF16)
            u = u_ref[...].astype(F32)
            s_zero = lax.rsqrt(jnp.mean(u * u, axis=1, keepdims=True) + EPS)
            pack_ref[6:7, :] = jnp.sum(u * s_zero * out, axis=0, keepdims=True)
            token_ref[...] = jnp.zeros(TOKEN, F32)


def scan_back(micro, role, flag, lens, dz, dy, keep, wts, dep):
    return pl.pallas_call(
        functools.partial(scan_kernel, micro, role),
        grid=(STEPS,),
        in_specs=[
            SMEM,
            SMEM,
            cols(T),
            cols(T),
            cols(T),
            cols(T),
            cols(T),
            full((T, 2 * NS)),
            full((T, LANES)),
            full((T, T)),
            full((T, LANES)),
            pl.BlockSpec((2, D, W), lambda i: (0, 0, i)),
            full((D, 2 * NS)),
            full((LANES, D)),
            cols(4),
            cols(1),
            full((4, 2 * NS)),
            full((1, 2 * NS)),
            full((8, LANES)),
            cols(1),
            cols(1),
            keep["u"].spec(),
            ANY,
        ],
        out_specs=[
            cols(T),
            full((T, 3 * LANES)),
            full((HALF, D)),
            full((HALF, D)),
            full((8, C)),
            full(TOKEN),
        ],
        out_shape=(
            far((T, C), BF16),
            far((T, 3 * LANES), BF16),
            shape_of((HALF, D), BF16),
            shape_of((HALF, D), BF16),
            far((8, C), F32),
            shape_of(TOKEN, F32),
        ),
        scratch_shapes=[
            pltpu.VMEM((3, T, LANES), F32),
            pltpu.VMEM((STEPS, T, LANES), F32),
            pltpu.VMEM((STEPS, T, LANES), F32),
            pltpu.VMEM((STEPS, 8, T), F32),
            pltpu.VMEM((T, D), F32),
            pltpu.VMEM((T, T), F32),
            pltpu.VMEM((T, LANES), F32),
            pltpu.VMEM((T, LANES), F32),
            pltpu.VMEM((8, LANES), F32),
        ],
        compiler_params=params(1),
        cost_estimate=COST,
        name="scan_backward",
    )(
        flag,
        lens,
        from_far(dz),
        from_far(dy),
        from_far(keep["y"]),
        from_far(keep["x"]),
        from_far(keep["xt"]),
        from_far(keep["bcr"]),
        from_far(keep["dtr"]),
        from_far(keep["scoret"]),
        from_far(keep["cums"]),
        from_far(wts["far_zx"]),
        wts["bc"],
        wts["dt"],
        wts["cx"],
        wts["bx"],
        wts["cbc"],
        wts["bbc"],
        wts["hp"],
        wts["skip"],
        from_far(keep["ggrad"]),
        from_far(keep["u"].array),
        dep,
    )


def input_kernel(e_ref, u_ref, gain_ref, d0_ref, d1_ref, o0_ref, o1_ref, _, du_ref, low_ref, token_ref):
    u = u_ref[...].astype(F32)
    s_zero = lax.rsqrt(jnp.mean(u * u, axis=1, keepdims=True) + EPS)
    dr = join_rows((d0_ref, d1_ref), (o0_ref, o1_ref))
    gained = gain_ref[...] * dr
    shared = s_zero * s_zero * s_zero * jnp.mean(u * gained, axis=1, keepdims=True)
    du = e_ref[...].astype(F32) + s_zero * gained - u * shared
    du_ref[...] = du
    low_ref[...] = du.astype(BF16)
    token_ref[...] = jnp.zeros(TOKEN, F32)


def input_back(e, u, dr, other, wts, dep):
    return pl.pallas_call(
        input_kernel,
        grid=(1,),
        in_specs=[e.spec(), u.spec()] + [VMEM] * 5 + [ANY],
        out_specs=[full((T, D)), VMEM, VMEM],
        out_shape=(far((T, D), F32), shape_of((T, D), BF16), shape_of(TOKEN, F32)),
        compiler_params=pltpu.CompilerParams(vmem_limit_bytes=SMALL_LIMIT),
        cost_estimate=COST,
        name="input_backward",
    )(e.array, u.array, wts["norm"], *dr, *other, dep)


def swap(value):
    return lax.ppermute(value, "tensor", [(0, 1), (1, 0)])


def relay_up(value):
    return lax.ppermute(value, "pipe", [(0, 1), (1, 0)])


def relay_down(value):
    return lax.ppermute(value, "pipe", [(1, 0)])


def partners(count):
    if count == 32:

        def make(fn):
            return [fn(i // 8, (i // 2) % 4, i % 2) for i in range(count)]

        def pack(y, x, z):
            return y * 8 + x * 2 + z

        def wrap(v):
            return (v + 1) % 4 if v % 2 else (v - 1) % 4

        return [
            make(lambda y, x, z: pack(y, x ^ 1, z)),
            make(lambda y, x, z: pack(y ^ 1, x, z)),
            make(lambda y, x, z: pack(y, wrap(x), z)),
            make(lambda y, x, z: pack(wrap(y), x, z)),
            make(lambda y, x, z: pack(y, x, z ^ 1)),
        ]
    return [[i ^ (1 << k) for i in range(count)] for k in range(count.bit_length() - 1)]


STREAMS = 5


def stream_order(maps, stream):
    k = stream % len(maps)
    return maps[k:] + maps[:k]


def block_order(maps, stream, late=0):
    order = stream_order(maps, stream + late)
    count = len(order[0])
    table = np.zeros((count, count), np.int32)
    for me in range(count):
        for p in range(count):
            owner = me
            for k, step in enumerate(order):
                if (p >> (len(order) - 1 - k)) & 1:
                    owner = step[owner]
            table[me, p] = owner
    return table


TILES_EARLY = [("et", "n", LANES * k) for k in range(C // LANES)] + [
    ("rt", "dz", LANES * k) for k in range(C // LANES)
]
TILES_LATE = [("rt", "dx", LANES * k) for k in range(C // LANES)] + [
    ("rt", "bcdt", LANES * k) for k in range(3)
]


def deal(tiles):
    width = -(-len(tiles) // STREAMS)
    return [tiles[width * s : width * (s + 1)] for s in range(STREAMS)]


EARLY, LATE = deal(TILES_EARLY), deal(TILES_LATE)
PACK = 8
PACK_ROWS = 2 * PACK * (C // LANES)
PACK_STREAM = STREAMS - 1


def runs(tiles):
    out = []
    for at, (left, right, first) in enumerate(tiles):
        if out and out[-1][:2] == [left, right] and out[-1][2] + LANES * out[-1][3] == first:
            out[-1][3] += 1
        else:
            out.append([left, right, first, 1, at])
    return out


class Loader:
    def __init__(self, flag_ref, names, sources, held, sem):
        self.flag, self.names, self.sources, self.held, self.sem = flag_ref, names, sources, held, sem
        self.waited = set()

    def copy(self, k, m, early):
        span = pl.ds(m * T, T)
        ref = self.held[k]
        slot = ref.at[:, span] if ref.shape[0] == D else ref.at[span, :]
        return pltpu.make_async_copy(self.sources[4 * k + 2 * early + m], slot, self.sem.at[2 * k + m])

    def start(self, name):
        k = self.names.index(name)
        for m in range(2):
            pl.when(self.flag[0] == 1)(lambda: self.copy(k, m, 0).start())
            pl.when(self.flag[0] == 0)(lambda: self.copy(k, m, 1).start())

    def get(self, name):
        k = self.names.index(name)
        if name not in self.waited:
            self.waited.add(name)
            for m in range(2):
                self.copy(k, m, 0).wait()
        return self.held[k]


def held_shapes(arrays):
    shapes = []
    for a in arrays:
        rows, columns = a[0].shape
        shapes.append(pltpu.VMEM((rows, 2 * columns) if rows == D else (2 * rows, columns), BF16))
    return shapes


def products(loader, lefts, tiles, blocks, owner_of, place):
    rows = D // blocks
    chunk = max(384, rows)
    placed = []
    for left, right, first, count, at in runs(tiles):
        held, rhs = loader.get(left), loader.get(right)
        if left not in placed:
            placed.append(left)
            for p in range(blocks):
                start = pl.multiple_of(owner_of(p) * rows, 16)
                lefts[len(placed) - 1, p * rows : (p + 1) * rows, :] = held[pl.ds(start, rows), :]
        slot = placed.index(left)
        for c in range(D // chunk):
            span = slice(c * chunk, (c + 1) * chunk)
            value = dot(lefts[slot, span, :], rhs[:, first : first + LANES * count]).astype(BF16)
            for j in range(count):
                place(at + j, c * chunk, value[:, j * LANES : (j + 1) * LANES])


def early_kernel(blocks, flag_ref, table_ref, *refs):
    names = ["et", "n", "rt", "dz"]
    sources, refs = refs[:16], refs[16:]
    outs, token_ref = refs[: 2 * STREAMS], refs[2 * STREAMS]
    held, lefts, in_sem = refs[2 * STREAMS + 1 :]
    loader = Loader(flag_ref, names, sources, held, in_sem)
    for name in names:
        loader.start(name)
    half = D // 2
    for s in range(STREAMS):

        def place(tile, row, value):
            outs[2 * s + row // half][tile, row % half : row % half + value.shape[0], :] = value

        def owner_of(p):
            return table_ref[flag_ref[1] + s * blocks + p]

        products(loader, lefts, EARLY[s], blocks, owner_of, place)
    token_ref[...] = jnp.zeros(TOKEN, F32)


def early_grads(flag, table, arrays, blocks):
    out = []
    for s in range(STREAMS):
        out += [near((len(EARLY[s]), D // 2, LANES), BF16)] * 2
    flat = pl.pallas_call(
        functools.partial(early_kernel, blocks),
        in_specs=[SMEM, SMEM] + [HBM] * 16,
        out_specs=[VMEM] * (len(out) + 1),
        out_shape=tuple(out) + (shape_of(TOKEN, F32),),
        scratch_shapes=[
            held_shapes(arrays),
            pltpu.VMEM((2, D, 2 * T), BF16),
            pltpu.SemaphoreType.DMA((8,)),
        ],
        compiler_params=pltpu.CompilerParams(vmem_limit_bytes=VMEM_LIMIT),
        cost_estimate=COST,
        name="grad_early",
    )(flag, table, *[from_far(v) for a in arrays for v in a])
    return list(flat[0:-1:2]), list(flat[1:-1:2]), flat[-1]


def total_rows(s, early, late):
    return len(EARLY[s]) * early + len(LATE[s]) * late + (PACK_ROWS if s == PACK_STREAM else 0)


def split_pair(value):
    high = value.astype(BF16)
    return jnp.concatenate([high, (value - high.astype(F32)).astype(BF16)], axis=0)


def join_pair(pair):
    wide_pair = pair.astype(F32)
    return wide_pair[:PACK] + wide_pair[PACK:]


def late_kernel(blocks, flag_ref, table_ref, *refs):
    names = ["rt", "dx", "bcdt"]
    sources, refs = refs[:12], refs[12:]
    packs, refs = refs[:4], refs[4:]
    keeps, gots, refs = refs[:STREAMS], refs[STREAMS : 2 * STREAMS], refs[2 * STREAMS :]
    outs, token_ref = refs[: 2 * STREAMS], refs[2 * STREAMS]
    held, lefts, in_sem = refs[2 * STREAMS + 1 :]
    loader = Loader(flag_ref, names, sources, held, in_sem)
    for name in names:
        loader.start(name)
    half = D // 2
    quarter = half // 2
    for s in range(STREAMS):
        for j in range(len(EARLY[s])):
            for side in range(2):
                span = slice(side * quarter, (side + 1) * quarter)
                total = keeps[s][j, span, :].astype(F32) + gots[s][j, span, :].astype(F32)
                outs[2 * s + side][j * quarter : (j + 1) * quarter, :] = total.astype(BF16)
    last = flag_ref[0] == 1
    total = jnp.where(last, packs[0][...] + packs[1][...], packs[2][...] + packs[3][...])
    for j in range(C // LANES):
        pair = split_pair(total[:, j * LANES : (j + 1) * LANES])
        at = total_rows(PACK_STREAM, quarter, half) - PACK_ROWS + 2 * PACK * j
        for side in range(2):
            outs[2 * PACK_STREAM + side][at : at + 2 * PACK, :] = pair
    for s in range(STREAMS):
        base = len(EARLY[s]) * quarter

        def place(tile, row, value):
            at = base + tile * half + row % half
            outs[2 * s + row // half][at : at + value.shape[0], :] = value

        def owner_of(p):
            return table_ref[flag_ref[1] + s * blocks + p]

        products(loader, lefts, LATE[s], blocks, owner_of, place)
    token_ref[...] = jnp.zeros(TOKEN, F32)


def late_grads(flag, table, arrays, blocks, packs, keeps, gots):
    out = []
    for s in range(STREAMS):
        out += [near((total_rows(s, D // 4, D // 2), LANES), BF16)] * 2
    flat = pl.pallas_call(
        functools.partial(late_kernel, blocks),
        in_specs=[SMEM, SMEM] + [HBM] * 12 + [VMEM] * (4 + 2 * STREAMS),
        out_specs=[VMEM] * (len(out) + 1),
        out_shape=tuple(out) + (shape_of(TOKEN, F32),),
        scratch_shapes=[
            held_shapes(arrays),
            pltpu.VMEM((1, D, 2 * T), BF16),
            pltpu.SemaphoreType.DMA((6,)),
        ],
        compiler_params=pltpu.CompilerParams(vmem_limit_bytes=VMEM_LIMIT),
        cost_estimate=COST,
        name="grad_late",
    )(
        flag,
        table,
        *[from_far(v) for a in arrays for v in a],
        *packs,
        *keeps,
        *gots,
    )
    return list(flat[0:-1:2]), list(flat[1:-1:2]), flat[-1]


def fold_kernel(early, late, deps, *refs):
    ends = early * 32 == D
    keeps, gots = refs[:STREAMS], refs[STREAMS : 2 * STREAMS]
    outs = refs[2 * STREAMS + deps :]
    for s in range(STREAMS):
        keep, got = keeps[s], gots[s]
        next_keep, next_send = outs[2 * s], outs[2 * s + 1]

        def add(at, rows):
            return keep[at : at + rows, :].astype(F32) + got[at : at + rows, :].astype(F32)

        at = to = 0
        for j in range(len(EARLY[s])):
            if ends:
                outs[2 * STREAMS + s][j * early : (j + 1) * early, :] = add(at, early)
            else:
                next_send[to : to + early // 2, :] = add(at + early // 2, early // 2).astype(BF16)
                next_keep[to : to + early // 2, :] = add(at, early // 2).astype(BF16)
                to += early // 2
            at += early
        for j in range(len(LATE[s])):
            next_send[to : to + late // 2, :] = add(at + late // 2, late // 2).astype(BF16)
            next_keep[to : to + late // 2, :] = add(at, late // 2).astype(BF16)
            at += late
            to += late // 2
        if s == PACK_STREAM:
            for j in range(C // LANES):
                span = slice(at + 2 * PACK * j, at + 2 * PACK * (j + 1))
                pair = split_pair(join_pair(keep[span, :]) + join_pair(got[span, :]))
                next_send[to + 2 * PACK * j : to + 2 * PACK * (j + 1), :] = pair
                next_keep[to + 2 * PACK * j : to + 2 * PACK * (j + 1), :] = pair


def fold(keeps, gots, early, late, ends, deps):
    out = []
    for s in range(STREAMS):
        rows = total_rows(s, 0 if ends else early // 2, late // 2)
        out += [near((rows, LANES), BF16)] * 2
    if ends:
        out += [near((len(EARLY[s]) * early, LANES), F32) for s in range(STREAMS)]
    flat = pl.pallas_call(
        functools.partial(fold_kernel, early, late, len(deps)),
        in_specs=[VMEM] * (2 * STREAMS) + [ANY] * len(deps),
        out_specs=[VMEM] * len(out),
        out_shape=tuple(out),
        compiler_params=pltpu.CompilerParams(vmem_limit_bytes=SMALL_LIMIT),
        cost_estimate=COST,
        name="fold_grads",
    )(*keeps, *gots, *deps)
    return list(flat[0 : 2 * STREAMS : 2]), list(flat[1 : 2 * STREAMS : 2]), flat[2 * STREAMS :]


def end_kernel(rows, heads, core_ref, *refs):
    dones, keeps, gots = refs[:STREAMS], refs[STREAMS : 2 * STREAMS], refs[2 * STREAMS : 3 * STREAMS]
    refs = refs[3 * STREAMS :]
    out_ref, zx_ref, dt_ref, cx_ref, bx_ref, gate_ref, heads_ref = refs[:7]
    mine_ref, theirs_ref, shared_ref, bcdt_s = refs[7:]

    def place(right, first, value):
        if right == "n":
            out_ref[:, first : first + LANES] = value
        elif right == "bcdt":
            bcdt_s[:, first : first + LANES] = value
        else:
            zx_ref[:, 0 if right == "dz" else 1, first : first + LANES] = value

    for s in range(STREAMS):
        for j, (_, right, first) in enumerate(EARLY[s]):
            place(right, first, dones[s][j * rows : (j + 1) * rows, :])
        for j, (_, right, first) in enumerate(LATE[s]):
            span = slice(j * rows, (j + 1) * rows)
            place(right, first, keeps[s][span, :].astype(F32) + gots[s][span, :].astype(F32))
    keep, got = keeps[PACK_STREAM], gots[PACK_STREAM]
    at = len(LATE[PACK_STREAM]) * rows
    for j in range(C // LANES):
        span = slice(at + 2 * PACK * j, at + 2 * PACK * (j + 1))
        lanes = slice(j * LANES, (j + 1) * LANES)
        value = join_pair(keep[span, :]) + join_pair(got[span, :])
        cx_ref[:, lanes] = value[0:4]
        bx_ref[:, lanes] = value[4:5]
        gate_ref[:, lanes] = value[5:6]
        shared_ref[:, lanes] = value[6:8]
        if j == 10:
            for k in range(3):
                moved = pltpu.roll(value, (LANES - 32 * k) % LANES, 1) if k else value
                heads_ref[k : k + 1, :] = moved[7:8, :heads]
    part = rows // 2
    mine_ref[...] = bcdt_s[pl.ds(pl.multiple_of(core_ref[0] * part, 8), part), : 2 * NS]
    theirs_ref[...] = bcdt_s[pl.ds(pl.multiple_of((1 - core_ref[0]) * part, 8), part), : 2 * NS]
    dt_ref[...] = bcdt_s[:, 2 * NS :].T[:heads, :]


def end(core, dones, keeps, gots, rows, heads):
    return pl.pallas_call(
        functools.partial(end_kernel, rows, heads),
        in_specs=[SMEM] + [VMEM] * (3 * STREAMS),
        out_specs=[VMEM] * 10,
        out_shape=(
            shape_of((rows, C), F32),
            shape_of((rows, 2, C), F32),
            shape_of((heads, rows), F32),
            shape_of((4, C), F32),
            shape_of((1, C), F32),
            shape_of((1, C), F32),
            shape_of((3, heads), F32),
            shape_of((rows // 2, 2 * NS), F32),
            shape_of((rows // 2, 2 * NS), F32),
            shape_of((2, C), F32),
        ),
        scratch_shapes=[pltpu.VMEM((rows, 3 * LANES), F32)],
        compiler_params=pltpu.CompilerParams(vmem_limit_bytes=SMALL_LIMIT),
        cost_estimate=COST,
        name="grad_end",
    )(core, *dones, *keeps, *gots)


def last_kernel(mine_ref, other_ref, shared_ref, other_shared_ref, bc_ref, norm_ref, conv_ref, bias_ref):
    bc_ref[...] = mine_ref[...] + other_ref[...]
    total = shared_ref[...] + other_shared_ref[...]
    norm_ref[...] = total[0:1]
    for k in range(4):
        conv_ref[k : k + 1, :] = total[1:2, 2 * NS * k : 2 * NS * (k + 1)]
    bias_ref[...] = total[1:2, 8 * NS : 10 * NS]


def last_sums(mine, other, shared, other_shared):
    return pl.pallas_call(
        last_kernel,
        in_specs=[VMEM] * 4,
        out_specs=[VMEM] * 4,
        out_shape=(
            shape_of(mine.shape, F32),
            shape_of((1, C), F32),
            shape_of((4, 2 * NS), F32),
            shape_of((1, 2 * NS), F32),
        ),
        compiler_params=pltpu.CompilerParams(vmem_limit_bytes=SMALL_LIMIT),
        cost_estimate=COST,
        name="last_sums",
    )(mine, other, shared, other_shared)


def pick_kernel(flag_ref, late0, late1, early0, early1, _, out_ref, token_ref, held, sem):
    for m, (late, early) in enumerate(((late0, early0), (late1, early1))):

        def start(source):
            pltpu.make_async_copy(source, held.at[m], sem.at[m]).start()

        pl.when(flag_ref[0] == 1)(lambda: start(late))
        pl.when(flag_ref[0] == 0)(lambda: start(early))
    for m in range(2):
        pltpu.make_async_copy(early0, held.at[m], sem.at[m]).wait()
        pltpu.make_async_copy(held.at[m], out_ref.at[m], sem.at[2 + m]).start()
    for m in range(2):
        pltpu.make_async_copy(held.at[m], out_ref.at[m], sem.at[2 + m]).wait()
    token_ref[...] = jnp.zeros(TOKEN, F32)


def pick(flag, late, early, dep):
    return pl.pallas_call(
        pick_kernel,
        in_specs=[SMEM] + [HBM] * 4 + [ANY],
        out_specs=[HBM, VMEM],
        out_shape=(far((2, T, D), F32), shape_of(TOKEN, F32)),
        scratch_shapes=[pltpu.VMEM((2, T, D), F32), pltpu.SemaphoreType.DMA((4,))],
        compiler_params=pltpu.CompilerParams(vmem_limit_bytes=SMALL_LIMIT),
        cost_estimate=COST,
        name="pick_section",
    )(flag, *[from_far(v) for v in (*late, *early)], dep)


def exchange(sends, maps, k):
    got = []
    for s in range(STREAMS):
        step = stream_order(maps, s)[k % len(maps)]
        got.append(lax.ppermute(sends[s], "dp", [(i, to) for i, to in enumerate(step)]))
    return got


def body(
    tokens,
    cotangent,
    lengths,
    norm_gain,
    w_zx,
    w_bc,
    w_dt,
    conv_x,
    bias_x,
    conv_bc,
    bias_bc,
    head_params,
    gate_gain,
    w_out,
):
    is_last = lax.axis_index("pipe") == 1
    core_at = lax.axis_index("tensor")
    lens = lengths.reshape(-1)
    heads = w_dt.shape[2]
    far_zx = jnp.transpose(w_zx[0], (1, 0, 2))
    wts = {
        "norm": norm_gain,
        "far_zx": far_zx,
        "far_out": w_out[0],
        "zx": to_near(far_zx),
        "bc": w_bc[0],
        "dt": jnp.pad(w_dt[0].T, ((0, LANES - heads), (0, 0))),
        "cx": conv_x[0],
        "bx": bias_x,
        "cbc": conv_bc[0],
        "bbc": bias_bc,
        "hp": jnp.pad(head_params[0], ((0, 5), (0, LANES - heads))),
        "skip": jnp.repeat(head_params[0, 2], HEAD)[None],
        "gate": gate_gain,
        "out": to_near(w_out[0]),
    }

    flag = is_last.astype(jnp.int32).reshape(1)

    def run(m, u, dep):
        names = (
            "rt", "z", "x", "y", "bcr", "dtr", "part0", "part1", "sq", "xt", "scoret", "cums", "token"
        )
        keep = dict(zip(names, forward(m, lens, u, wts, dep)))
        keep["u"] = u
        keep["part"] = (keep["part0"], keep["part1"])
        keep["other"] = tuple(swap(v) for v in keep["part"])
        keep["other_sq"] = swap(keep["sq"])
        return keep

    def joined(keep, dep, round_out=False):
        return join(round_out, keep["u"], keep["part"], keep["other"], keep["sq"], keep["other_sq"], dep)

    def gate(role, keep, e, dep):
        names = ("et", "n", "dz", "dy", "ggrad")
        sums = (keep["part"], keep["other"], keep["sq"], keep["other_sq"])
        values = gate_back(role, flag, e, *sums, keep["z"], keep["y"], wts, dep)
        keep["e"] = e
        keep.update(zip(names, values))

    def scan(m, role, keep, dep):
        names = ("dx", "bcdt", "dr0", "dr1", "pack", "token")
        keep.update(zip(names, scan_back(m, role, flag, lens, keep["dz"], keep["dy"], keep, wts, dep)))
        keep["dr"] = (keep["dr0"], keep["dr1"])
        keep["other_dr"] = tuple(swap(v) for v in keep["dr"])

    def finish(keep, dep):
        keep["du"], low, token = input_back(keep["e"], keep["u"], keep["dr"], keep["other_dr"], wts, dep)
        return low, token

    keep_a = run(0, Rows(tokens, 0), lens)
    res_a, low_a, token = joined(keep_a, lens, True)
    sent_a = relay_up(low_a)
    keep_b = run(1, Rows(tokens, 1), token)
    res_b, low_b, token = joined(keep_b, sent_a, True)
    sent_b = relay_up(low_b)
    keep_c = run(0, Rows(sent_a), token)
    keep_d = run(1, Rows(sent_b), keep_c["token"])
    gate(1, keep_c, Rows(cotangent, 0), keep_d["token"])
    scan(0, 1, keep_c, touch(*keep_d["other"], keep_d["other_sq"]))
    back_c, token = finish(keep_c, lens)
    sent_c = relay_down(back_c)
    gate(1, keep_d, Rows(cotangent, 1), token)
    scan(1, 1, keep_d, lens)
    back_d, token = finish(keep_d, sent_c)
    sent_d = relay_down(back_d)
    gate(0, keep_a, Rows(sent_c), token)
    scan(0, 0, keep_a, lens)
    gate(0, keep_b, Rows(sent_d), keep_a["token"])

    dp = lax.axis_size("dp")
    maps = partners(dp)
    me = lax.axis_index("dp")
    tables = [
        jnp.asarray(np.stack([block_order(maps, s, late) for s in range(STREAMS)], axis=1).reshape(-1))
        for late in range(2)
    ]
    flag = jnp.stack([is_last.astype(jnp.int32), me.astype(jnp.int32) * (STREAMS * dp)])

    def both(name):
        return (keep_c[name], keep_d[name], keep_a[name], keep_b[name])

    arrays = [both(k) for k in ("et", "n", "rt", "dz")]
    keeps, sends, token = early_grads(flag, tables[0], arrays, dp)
    gots = exchange(sends, maps, 0)
    scan(1, 0, keep_b, token)
    arrays = [both(k) for k in ("rt", "dx", "bcdt")]
    keeps, sends, token = late_grads(flag, tables[1], arrays, dp, both("pack"), keeps, gots)
    _, token_a = finish(keep_a, token)
    _, token_b = finish(keep_b, token)
    res_c, _, token_c = joined(keep_c, token)
    res_d, _, token_d = joined(keep_d, token)
    deps = [[token_a, token_b, token_c, token_d]]
    section_out, token_a = pick(flag, (res_c, res_d), (res_a, res_b), token)
    section_grad, token_b = pick(flag, (keep_c["du"], keep_d["du"]), (keep_a["du"], keep_b["du"]), token)
    deps += [[token_a, token_b], [], []]
    early, late = D // 4, D // 2
    dones = None
    for k in range(1, len(maps)):
        gots = exchange(sends, maps, k)
        ends = k + 1 == len(maps)
        keeps, sends, dones = fold(keeps, gots, early, late, ends, deps[k - 1])
        early, late = early // 2, late // 2
    gots = exchange(sends, maps, len(maps))
    core = core_at.astype(jnp.int32).reshape(1)
    g_out, g_zx, g_dt, g_cx, g_bx, g_gate, g_heads, mine, theirs, shared = end(
        core, dones, keeps, gots, D // dp, heads
    )
    g_bc, g_norm, g_cbc, g_bbc = last_sums(mine, swap(theirs), shared, swap(shared))
    return (
        section_out[None],
        section_grad[None],
        g_norm,
        g_zx[None],
        g_bc[None],
        g_dt.T[None],
        g_cx[None],
        g_bx,
        g_cbc[None],
        g_bbc,
        g_heads[None],
        g_gate,
        g_out.T[None],
    )


def solution(mesh):
    in_specs = (
        P(None, "dp", None),
        P(None, "dp", None),
        P(None, "dp", None),
        P("pipe", None),
        P("pipe", None, None, "tensor"),
        P("pipe", None, None),
        P("pipe", None, "tensor"),
        P("pipe", None, "tensor"),
        P("pipe", "tensor"),
        P("pipe", None, None),
        P("pipe", None),
        P("pipe", None, "tensor"),
        P("pipe", "tensor"),
        P("pipe", "tensor", None),
    )
    out_specs = (
        P("pipe", None, "dp", None),
        P("pipe", None, "dp", None),
        P("pipe", None),
        P("pipe", "dp", None, "tensor"),
        P("pipe", ("dp", "tensor"), None),
        P("pipe", "dp", "tensor"),
        P("pipe", None, "tensor"),
        P("pipe", "tensor"),
        P("pipe", None, None),
        P("pipe", None),
        P("pipe", None, "tensor"),
        P("pipe", "tensor"),
        P("pipe", "tensor", "dp"),
    )
    return jax.shard_map(body, mesh=mesh, in_specs=in_specs, out_specs=out_specs, check_vma=False)
```

```python
import functools
from types import SimpleNamespace

import jax
import jax.numpy as jnp
import numpy as np
from jax import lax
from jax.experimental import pallas as pl
from jax.experimental.pallas import tpu as pltpu
from jax.sharding import PartitionSpec as P

F32 = jnp.float32
BF16 = jnp.bfloat16
HIGH = lax.Precision.HIGHEST
EPS = 1e-05
T = 256
D = 1536
C = 1536
W = 256
STEPS = C // W
HEAD = 64
PER = W // HEAD
NS = 128
DI = 3072
LANES = 128
HALF = T // 2
NT = (((1,), (1,)), ((), ()))
VMEM_LIMIT = 24 * 1024 * 1024
SMALL_LIMIT = 16 * 1024 * 1024
COST = pl.CostEstimate(flops=1, bytes_accessed=1, transcendentals=0)


def dot(a, b):
    return jnp.dot(a, b, preferred_element_type=F32)


def dot_nt(a, b):
    return lax.dot_general(a, b, NT, preferred_element_type=F32)


def dot_exact(a, b):
    return jnp.dot(a, b, precision=HIGH, preferred_element_type=F32)


def group_sums(values, group):
    terms = []
    for value in values:
        high = value.astype(BF16)
        terms += [high, (value - high.astype(F32)).astype(BF16)]
    out = dot(jnp.concatenate(terms, axis=0), group.astype(BF16))
    at, sums = 0, []
    for value in values:
        rows = value.shape[0]
        sums.append(out[at : at + rows] + out[at + rows : at + 2 * rows])
        at += 2 * rows
    return sums


def params(steps):
    return pltpu.CompilerParams(
        dimension_semantics=("arbitrary",) * steps, vmem_limit_bytes=VMEM_LIMIT
    )


def sigmoid(v):
    return 1.0 / (1.0 + jnp.exp(-v))


def seg_ids(len_ref, micro, pos):
    end = jnp.int32(0)
    seg = jnp.zeros(pos.shape, jnp.int32)
    for k in range(4):
        end = end + len_ref[micro, 0, k]
        seg = seg + (pos >= end).astype(jnp.int32)
    return seg


def keep_masks(len_ref, micro):
    pos = lax.broadcasted_iota(jnp.int32, (T, LANES), 0)
    seg = seg_ids(len_ref, micro, pos)
    out = []
    for back in range(1, 4):
        same = (seg_ids(len_ref, micro, pos - back) == seg) & (pos >= back)
        out.append(same.astype(F32))
    return out


def wide(mask, width=W):
    return jnp.concatenate([mask] * (width // LANES), axis=1)


def conv(v, taps, bias, keeps):
    total = bias + taps[3] * v
    for back in range(1, 4):
        total = total + taps[3 - back] * (pltpu.roll(v, back, 0) * keeps[back - 1])
    return total


def conv_back(dtotal, v, taps, keeps):
    dv = taps[3] * dtotal
    grads = [None] * 4
    grads[3] = jnp.sum(dtotal * v, axis=0, keepdims=True)
    for back in range(1, 4):
        masked = dtotal * keeps[back - 1]
        grads[3 - back] = jnp.sum(masked * pltpu.roll(v, back, 0), axis=0, keepdims=True)
        dv = dv + taps[3 - back] * pltpu.roll(masked, T - back, 0)
    return dv, grads, jnp.sum(dtotal, axis=0, keepdims=True)


def rows_of(ref, count):
    return [ref[k : k + 1, :] for k in range(count)]


def tri_mask(len_ref, micro, transposed=False):
    first = lax.broadcasted_iota(jnp.int32, (T, T), 0)
    second = lax.broadcasted_iota(jnp.int32, (T, T), 1)
    same = seg_ids(len_ref, micro, first) == seg_ids(len_ref, micro, second)
    order = (second >= first) if transposed else (first >= second)
    return (same & order).astype(F32)


def lower_ones(transposed):
    first = lax.broadcasted_iota(jnp.int32, (T, T), 0)
    second = lax.broadcasted_iota(jnp.int32, (T, T), 1)
    return ((second >= first) if transposed else (first >= second)).astype(F32)


def softplus(v):
    return jnp.maximum(v, 0.0) + jnp.log1p(jnp.exp(-jnp.abs(v)))


def spread_steps(dt, cums, dt_s, cum_s, cumt_s):
    turned = cums.T
    for i in range(STEPS):
        shift = (LANES - PER * i) % LANES
        dt_s[i] = pltpu.roll(dt, shift, 1) if shift else dt
        cum_s[i] = pltpu.roll(cums, shift, 1) if shift else cums
        cumt_s[i, 0:PER, :] = turned[PER * i : PER * (i + 1), :]


def head_lanes(value, k):
    lane = lax.broadcasted_iota(jnp.int32, value.shape, 1)
    return jnp.where((lane >= k * HEAD) & (lane < (k + 1) * HEAD), value, jnp.zeros_like(value))


def per_channel(dt):
    lane = lax.broadcasted_iota(jnp.int32, dt.shape, 1)
    tiles = []
    for p in range(PER // 2):
        tiles.append(
            jnp.where(
                lane < HEAD,
                jnp.broadcast_to(dt[:, 2 * p : 2 * p + 1], dt.shape),
                jnp.broadcast_to(dt[:, 2 * p + 1 : 2 * p + 2], dt.shape),
            )
        )
    return jnp.concatenate(tiles, axis=1)


def spread_heads(hp_ref, hp_s):
    count = hp_ref.shape[2]
    hp_s[STEPS] = jnp.zeros((8, LANES), F32)
    for k in range(3):
        hp_s[STEPS, k : k + 1, 0:count] = hp_ref[k]
    value = hp_s[STEPS]
    for i in range(STEPS):
        shift = (LANES - PER * i) % LANES
        hp_s[i] = pltpu.roll(value, shift, 1) if shift else value
    return value


def skip_row(hp_s, step):
    return per_channel(hp_s[step])[2:3, :]


def full(shape):
    return pl.BlockSpec(shape, lambda i: (0,) * len(shape))


def cols(rows):
    return pl.BlockSpec((rows, W), lambda i: (0, i))


def shape_of(shape, dtype):
    return jax.ShapeDtypeStruct(shape, dtype)


def far(shape, dtype):
    return pltpu.HBM(shape, dtype)


def near(shape, dtype):
    return pltpu.VMEM(shape, dtype)


class Rows:
    def __init__(self, array, m=None):
        self.array, self.m = array, m

    def spec(self):
        if self.m is None:
            return pl.BlockSpec((T, D), lambda *i: (0, 0))
        return pl.BlockSpec((None, T, D), lambda *i: (self.m, 0, 0))


def order(dep):
    if isinstance(dep, tuple):
        return dep[0], ANY
    return from_far(dep), HBM


class Halves:
    def __init__(self, mine, other):
        self.mine, self.other = mine, other


def rows_operands(source):
    if isinstance(source, Rows):
        return dict(e=(source.array, source.spec()))
    half = pl.BlockSpec((HALF, D), lambda *i: (0, 0))
    return dict(e_mine=(source.mine, half), e_other=(source.other, half))


def from_far(value):
    return pltpu.with_memory_space_constraint(value, pltpu.HBM)


TOKEN = (8, LANES)


SMEM = pl.BlockSpec(memory_space=pltpu.SMEM)
VMEM = pl.BlockSpec(memory_space=pltpu.VMEM)
ANY = pl.BlockSpec(memory_space=pl.ANY)
HBM = pl.BlockSpec(memory_space=pltpu.HBM)


def call(body, ins, outs, scratch, name, grid=(STEPS,), limit=VMEM_LIMIT):
    names = [*ins, *outs, *scratch]

    def kernel(*refs):
        body(SimpleNamespace(**dict(zip(names, refs))))

    values = pl.pallas_call(
        kernel,
        grid=grid,
        in_specs=[v[1] for v in ins.values()],
        out_specs=[v[1] for v in outs.values()],
        out_shape=tuple(v[0] for v in outs.values()),
        scratch_shapes=list(scratch.values()),
        compiler_params=pltpu.CompilerParams(
            dimension_semantics=("arbitrary",) * len(grid), vmem_limit_bytes=limit
        ),
        cost_estimate=COST,
        name=name,
    )(*[v[0] for v in ins.values()])
    return dict(zip(outs, values))


def scan_scratch():
    return dict(
        keep_s=pltpu.VMEM((3, T, LANES), F32),
        dt_s=pltpu.VMEM((STEPS, T, LANES), F32),
        cum_s=pltpu.VMEM((STEPS, T, LANES), F32),
        cumt_s=pltpu.VMEM((STEPS, 8, T), F32),
        hp_s=pltpu.VMEM((STEPS + 1, 8, LANES), F32),
        acc_s=pltpu.VMEM((T, D), F32),
    )


def forward_kernel(micro, R):
    step = pl.program_id(0)

    @pl.when(step == 0)
    def _():
        u = R.u[...].astype(F32)
        s_zero = lax.rsqrt(jnp.mean(u * u, axis=1, keepdims=True) + EPS)
        low = (u * s_zero * R.norm[...]).astype(BF16)
        R.r_s[...] = low
        R.rt[...] = low.T
        keeps = keep_masks(R.lens, micro)
        for k in range(3):
            R.keep_s[k] = keeps[k]
        bcr = dot(low, R.bc[...])
        R.bcr[...] = bcr
        dtr = dot_nt(low, R.dt[...])
        R.dtr[...] = dtr
        total = conv(bcr, rows_of(R.cbc, 4), R.bbc[...], [wide(k, 2 * NS) for k in keeps])
        act = total * sigmoid(total)
        score = dot_nt(act[:, NS:].astype(BF16), act[:, :NS].astype(BF16)) * tri_mask(R.lens, micro)
        R.score_s[...] = score
        R.scoret[...] = score.T
        hp = spread_heads(R.hp, R.hp_s)
        dt = softplus(dtr + hp[0:1, :])
        rates = dt * (-jnp.exp(hp[1:2, :]))
        cums = dot_exact(lower_ones(False), rates)
        R.cums[...] = cums
        spread_steps(dt, cums, R.dt_s, R.cum_s, R.cumt_s)
        R.acc_s[...] = jnp.zeros_like(R.acc_s)
        R.sq[...] = jnp.zeros_like(R.sq)

    keeps = [wide(R.keep_s[k]) for k in range(3)]
    low_z = dot(R.r_s[...], R.zx[0]).astype(BF16)
    low_x = dot(R.r_s[...], R.zx[1]).astype(BF16)
    R.z[...] = low_z
    R.x[...] = low_x
    z = low_z.astype(F32)
    x = low_x.astype(F32)
    total = conv(x, rows_of(R.cx, 4), R.bx[...], keeps)
    xc = total * sigmoid(total)
    cums = R.cum_s[step]
    cumt = R.cumt_s[step]
    xt = (xc * per_channel(R.dt_s[step])).astype(BF16)
    R.xt[...] = xt
    top = jnp.zeros((HALF, W), F32)
    bottom = jnp.zeros((HALF, W), F32)
    for k in range(PER):
        mine = head_lanes(xt, k)
        col = cums[:, k : k + 1]
        row = cumt[k : k + 1, :]
        mix = R.score_s[0:HALF, 0:HALF] * jnp.exp(jnp.minimum(col[:HALF] - row[:, :HALF], 0.0))
        top = top + dot(mix.astype(BF16), mine[:HALF])
        mix = R.score_s[HALF:T, :] * jnp.exp(jnp.minimum(col[HALF:] - row, 0.0))
        bottom = bottom + dot(mix.astype(BF16), mine)
    y = jnp.concatenate([top, bottom], axis=0) + skip_row(R.hp_s, step) * xc
    R.y[...] = y
    g = y * (z * sigmoid(z))
    squares = g * g
    for k in range(W // LANES):
        R.sq[...] += squares[:, k * LANES : (k + 1) * LANES]
    R.acc_s[...] += dot((g * R.gate[...]).astype(BF16), R.out[...])

    @pl.when(step == STEPS - 1)
    def _():
        R.part0[...] = R.acc_s[:HALF, :].astype(BF16)
        R.part1[...] = R.acc_s[HALF:, :].astype(BF16)
        R.token[...] = jnp.zeros(TOKEN, F32)


def small_operands(wts):
    return dict(
        bc=(wts.bc, full((D, 2 * NS))),
        dt=(wts.dt, full((LANES, D))),
        cx=(from_far(wts.cx), cols(4)),
        bx=(from_far(wts.bx), cols(1)),
        cbc=(from_far(wts.cbc), full((4, 2 * NS))),
        bbc=(from_far(wts.bbc), full((1, 2 * NS))),
        hp=(from_far(wts.hp), full(wts.hp.shape)),
    )


def forward(micro, lens, u, wts, dep):
    ins = dict(
        lens=(lens, SMEM),
        u=(u.array, u.spec()),
        norm=(from_far(wts.norm), full((1, D))),
        zx=(from_far(wts.zx), pl.BlockSpec((2, D, W), lambda i: (0, 0, i))),
        out=(from_far(wts.out), pl.BlockSpec((W, D), lambda i: (i, 0))),
        gate=(from_far(wts.gate), cols(1)),
        **small_operands(wts),
        dep=order(dep),
    )
    outs = dict(
        rt=(far((D, T), BF16), full((D, T))),
        z=(far((T, C), BF16), cols(T)),
        x=(far((T, C), BF16), cols(T)),
        y=(far((T, C), F32), cols(T)),
        bcr=(far((T, 2 * NS), F32), full((T, 2 * NS))),
        dtr=(far((T, LANES), F32), full((T, LANES))),
        part0=(shape_of((HALF, D), BF16), full((HALF, D))),
        part1=(shape_of((HALF, D), BF16), full((HALF, D))),
        sq=(shape_of((T, LANES), F32), full((T, LANES))),
        xt=(far((T, C), BF16), cols(T)),
        scoret=(far((T, T), F32), full((T, T))),
        cums=(far((T, LANES), F32), full((T, LANES))),
        token=(far(TOKEN, F32), full(TOKEN)),
    )
    scratch = scan_scratch() | dict(
        r_s=pltpu.VMEM((T, D), BF16),
        score_s=pltpu.VMEM((T, T), F32),
    )
    return call(functools.partial(forward_kernel, micro), ins, outs, scratch, "layer_forward")


def touch_kernel(*refs):
    refs[-1][...] = jnp.zeros(TOKEN, F32)


def touch(*values):
    return pl.pallas_call(
        touch_kernel,
        in_specs=[ANY] * len(values),
        out_specs=VMEM,
        out_shape=shape_of(TOKEN, F32),
        compiler_params=pltpu.CompilerParams(vmem_limit_bytes=SMALL_LIMIT),
        cost_estimate=COST,
        name="touch",
    )(*values)


def scale_of(sq0_ref, sq1_ref):
    squares = jnp.sum(sq0_ref[...] + sq1_ref[...], axis=1, keepdims=True)
    return lax.rsqrt(squares / DI + EPS)


def join_rows(mine, others):
    halves = [a[...].astype(F32) + b[...].astype(F32) for a, b in zip(mine, others)]
    return jnp.concatenate(halves, axis=0)


def join(keep, dep, first):
    def kernel(R):
        scale = scale_of(R.sq0, R.sq1)
        total = join_rows((R.p0, R.p1), (R.o0, R.o1))
        res = R.u[...].astype(F32) + scale * total
        low = res.astype(BF16)
        R.res[...] = low.astype(F32) if first else res
        if first:
            R.low[...] = low
            R.total[...] = total.astype(BF16)
            R.scale[...] = jnp.broadcast_to(scale, (T, LANES))
        R.token[...] = jnp.zeros(TOKEN, F32)

    ins = dict(
        u=(keep.u.array, keep.u.spec()),
        p0=(keep.part[0], VMEM),
        p1=(keep.part[1], VMEM),
        o0=(keep.other[0], VMEM),
        o1=(keep.other[1], VMEM),
        sq0=(keep.sq, VMEM),
        sq1=(keep.other_sq, VMEM),
        dep=order(dep),
    )
    outs = dict(res=(far((T, D), F32), full((T, D))), token=(far(TOKEN, F32), full(TOKEN)))
    if first:
        outs |= dict(
            low=(shape_of((T, D), BF16), VMEM),
            total=(far((T, D), BF16), full((T, D))),
            scale=(far((T, LANES), F32), full((T, LANES))),
        )
    return call(kernel, ins, outs, {}, "join_output", grid=(1,), limit=SMALL_LIMIT)


def gate_begin(R):
    if hasattr(R, "e_mine"):
        R.e_s[half_rows(R.core[0]), :] = R.e_mine[...]
        R.e_s[half_rows(1 - R.core[0]), :] = R.e_other[...]
    else:
        R.e_s[...] = R.e[...]
    e = R.e_s[...].astype(F32)
    if hasattr(R, "total"):
        scale = R.scale[:, 0:1]
        total = R.total[...].astype(F32)
    else:
        scale = scale_of(R.sq0, R.sq1)
        total = join_rows((R.p0, R.p1), (R.o0, R.o1))
    inner = jnp.sum(e * total, axis=1, keepdims=True)
    R.scale_s[...] = jnp.broadcast_to(scale, (T, LANES))
    R.inner_s[...] = jnp.broadcast_to(inner * (scale * scale * scale) / DI, (T, LANES))
    R.et[...] = R.e_s[...].T


def gate_block(R):
    scale = wide(R.scale_s[...])
    z = R.z[...].astype(F32)
    y = R.y[...]
    gg = R.gate[...]
    dn = dot_nt(R.e_s[...], R.out[...])
    sig = sigmoid(z)
    act = z * sig
    g = y * act
    normed = g * scale
    R.n[...] = (normed * gg).astype(BF16)
    dg = scale * (gg * dn) - g * wide(R.inner_s[...])
    R.dz[...] = (dg * y * (sig * (1.0 + z * (1.0 - sig)))).astype(BF16)
    return y, (dg * act).astype(BF16), jnp.sum(normed * dn, axis=0, keepdims=True)


def scan_begin(micro, R):
    keeps = keep_masks(R.lens, micro)
    for k in range(3):
        R.keep_s[k] = keeps[k]
    hp = spread_heads(R.hp, R.hp_s)
    spread_steps(softplus(R.dtr[...] + hp[0:1, :]), R.cums[...], R.dt_s, R.cum_s, R.cumt_s)
    for ref in (R.acc_s, R.dscore_s, R.dcum_s, R.ddt_s, R.dskip_s):
        ref[...] = jnp.zeros_like(ref)


def scan_block(R, step, y, dyb, ggrad):
    keeps = [wide(R.keep_s[k]) for k in range(3)]
    taps = rows_of(R.cx, 4)
    x = R.x[...].astype(F32)
    total = conv(x, taps, R.bx[...], keeps)
    sig = sigmoid(total)
    xc = total * sig
    cums = R.cum_s[step]
    cumt = R.cumt_s[step]
    dtb = per_channel(R.dt_s[step])
    xt = R.xt[...]
    skip = skip_row(R.hp_s, step)
    inside = y - skip * xc
    top = jnp.zeros((HALF, W), F32)
    bottom = jnp.zeros((HALF, W), F32)
    for k in range(PER):
        my_dy = head_lanes(dyb, k)
        my_x = head_lanes(xt, k)
        col = cums[:, k : k + 1]
        row = cumt[k : k + 1, :]
        decay = jnp.exp(jnp.minimum(row - col[:HALF], 0.0))
        mix = R.scoret[0:HALF, :] * decay
        top = top + dot(mix.astype(BF16), my_dy)
        R.dscore_s[0:HALF, :] += dot_nt(my_x[:HALF], dyb) * decay
        decay = jnp.exp(jnp.minimum(row[:, HALF:] - col[HALF:], 0.0))
        mix = R.scoret[HALF:T, HALF:T] * decay
        bottom = bottom + dot(mix.astype(BF16), my_dy[HALF:])
        R.dscore_s[HALF:T, HALF:T] += dot_nt(my_x[HALF:], dyb[HALF:]) * decay
    dxt = jnp.concatenate([top, bottom], axis=0)
    chan = lax.broadcasted_iota(jnp.int32, (W, LANES), 0) // HEAD + PER * step
    lane = lax.broadcasted_iota(jnp.int32, (W, LANES), 1)
    group = (chan == lane).astype(F32)
    dy = dyb.astype(F32)
    dxc = dtb * dxt + skip * dy
    dskip = jnp.broadcast_to(jnp.sum(dy * xc, axis=0, keepdims=True), (16, W))
    sums = group_sums([dy * inside - xt.astype(F32) * dxt, xc * dxt, dskip], group)
    R.dcum_s[...] += sums[0]
    R.ddt_s[...] += sums[1]
    R.dskip_s[...] += sums[2][:8]
    dtotal = dxc * (sig * (1.0 + total * (1.0 - sig)))
    dx, grads, dbias = conv_back(dtotal, x, taps, keeps)
    here = pl.ds(pl.multiple_of(step * W, W), W)
    for k, value in enumerate(grads + [dbias, ggrad]):
        R.pack[k : k + 1, here] = value
    low = dx.astype(BF16)
    R.dx[...] = low
    R.acc_s[...] += dot_nt(R.dz[...], R.zx[0]) + dot_nt(low, R.zx[1])


def half_rows(core):
    return pl.ds(pl.multiple_of(core * HALF, HALF), HALF)


def scan_end(micro, R):
    keeps = [wide(R.keep_s[k], 2 * NS) for k in range(3)]
    bcr = R.bcr[...]
    taps = rows_of(R.cbc, 4)
    total = conv(bcr, taps, R.bbc[...], keeps)
    sig = sigmoid(total)
    act = total * sig
    dscore = R.dscore_s[...] * tri_mask(R.lens, micro, True)
    db = dot(dscore.astype(BF16), act[:, NS:].astype(BF16))
    dc = dot(dscore.T.astype(BF16), act[:, :NS].astype(BF16))
    dact = jnp.concatenate([db, dc], axis=1)
    dtotal = dact * (sig * (1.0 + total * (1.0 - sig)))
    dbc, grads, dbias = conv_back(dtotal, bcr, taps, keeps)
    for k, value in enumerate(grads + [dbias]):
        R.pack[7:8, 2 * NS * k : 2 * NS * (k + 1)] = value
    hp = R.hp_s[STEPS]
    pre = R.dtr[...] + hp[0:1, :]
    decay_rate = -jnp.exp(hp[1:2, :])
    dt = softplus(pre)
    drates = dot_exact(lower_ones(True), R.dcum_s[...])
    heads = R.hp.shape[2]
    lane = lax.broadcasted_iota(jnp.int32, (T, LANES), 1)
    ddt = (R.ddt_s[...] + drates * decay_rate) * sigmoid(pre)
    ddt = jnp.where(lane < heads, ddt, 0.0)
    shift = jnp.sum(ddt, axis=0, keepdims=True)
    decay = jnp.sum(drates * dt, axis=0, keepdims=True) * decay_rate
    decay = jnp.where(lane[0:1] < heads, decay, 0.0)
    both = jnp.concatenate([shift, decay, R.dskip_s[2:8, :]], axis=0)
    tile = both[0:1] + pltpu.roll(both, 32, 1)[1:2] + pltpu.roll(both, 64, 1)[2:3]
    R.pack[7:8, 10 * NS : 11 * NS] = tile
    R.pack[7:8, 11 * NS :] = jnp.zeros((1, NS), F32)
    low_bc = dbc.astype(BF16)
    low_dt = ddt.astype(BF16)
    R.bcdt[:, : 2 * NS] = low_bc
    R.bcdt[:, 2 * NS :] = low_dt
    out = R.acc_s[...] + dot_nt(low_bc, R.bc[...]) + dot(low_dt, R.dt[...])
    R.acc_s[...] = out
    R.mine[...] = R.acc_s[half_rows(R.core[0]), :].astype(BF16)
    R.theirs[...] = R.acc_s[half_rows(1 - R.core[0]), :].astype(BF16)
    u = R.u[...].astype(F32)
    s_zero = lax.rsqrt(jnp.mean(u * u, axis=1, keepdims=True) + EPS)
    R.pack[6:7, :] = jnp.sum(u * s_zero * out, axis=0, keepdims=True)
    R.token[...] = jnp.zeros(TOKEN, F32)


def gate_operands(e, keep, wts):
    ins = rows_operands(e) | dict(
        z=(from_far(keep.z), cols(T)),
        y=(from_far(keep.y), cols(T)),
        gate=(from_far(wts.gate), cols(1)),
        out=(from_far(wts.out), pl.BlockSpec((W, D), lambda i: (i, 0))),
    )
    if hasattr(keep, "total"):
        return ins | dict(
            total=(from_far(keep.total), full((T, D))), scale=(from_far(keep.scale), full((T, LANES)))
        )
    part, other = keep.part, keep.other
    ins |= dict(
        p0=(part[0], full((HALF, D))),
        p1=(part[1], full((HALF, D))),
        o0=(other[0], full((HALF, D))),
        o1=(other[1], full((HALF, D))),
        sq0=(keep.sq, full((T, LANES))),
        sq1=(keep.other_sq, full((T, LANES))),
    )
    return ins


def gate_results():
    return dict(
        et=(far((D, T), BF16), full((D, T))),
        n=(far((T, C), BF16), cols(T)),
        dz=(far((T, C), BF16), cols(T)),
    )


GATE_SCRATCH = dict(
    e_s=pltpu.VMEM((T, D), BF16), scale_s=pltpu.VMEM((T, LANES), F32), inner_s=pltpu.VMEM((T, LANES), F32))


def scan_operands(lens, core, keep, wts):
    return dict(
        lens=(lens, SMEM),
        core=(core, SMEM),
        x=(from_far(keep.x), cols(T)),
        xt=(from_far(keep.xt), cols(T)),
        bcr=(from_far(keep.bcr), full((T, 2 * NS))),
        dtr=(from_far(keep.dtr), full((T, LANES))),
        scoret=(from_far(keep.scoret), full((T, T))),
        cums=(from_far(keep.cums), full((T, LANES))),
        zx=(from_far(wts.zx), pl.BlockSpec((2, D, W), lambda i: (0, 0, i))),
        **small_operands(wts),
        u=(keep.u.array, keep.u.spec()),
    )


def scan_results():
    return dict(
        dx=(far((T, C), BF16), cols(T)),
        bcdt=(far((T, 3 * LANES), BF16), full((T, 3 * LANES))),
        mine=(shape_of((HALF, D), BF16), full((HALF, D))),
        theirs=(shape_of((HALF, D), BF16), full((HALF, D))),
        pack=(far((PACK, C), F32), full((PACK, C))),
        token=(far(TOKEN, F32), full(TOKEN)),
    )


def back_scratch():
    return scan_scratch() | dict(
        dscore_s=pltpu.VMEM((T, T), F32),
        dcum_s=pltpu.VMEM((T, LANES), F32),
        ddt_s=pltpu.VMEM((T, LANES), F32),
        dskip_s=pltpu.VMEM((8, LANES), F32),
    )


def gate_back(core, e, keep, wts, dep):
    def kernel(R):
        pl.when(pl.program_id(0) == 0)(lambda: gate_begin(R))
        _, dy, ggrad = gate_block(R)
        R.dy[...] = dy
        R.ggrad[...] = ggrad

    ins = gate_operands(e, keep, wts) | dict(core=(core, SMEM), dep=order(dep))
    outs = gate_results() | dict(
        dy=(far((T, C), BF16), cols(T)),
        ggrad=(far((1, C), F32), cols(1)),
    )
    return call(kernel, ins, outs, GATE_SCRATCH, "gate_backward")


def scan_back(micro, lens, core, keep, wts, dep):
    def kernel(R):
        step = pl.program_id(0)
        pl.when(step == 0)(lambda: scan_begin(micro, R))
        scan_block(R, step, R.y[...], R.dy[...], R.ggrad[...])
        pl.when(step == STEPS - 1)(lambda: scan_end(micro, R))

    ins = scan_operands(lens, core, keep, wts) | dict(
        y=(from_far(keep.y), cols(T)),
        dy=(from_far(keep.dy), cols(T)),
        dz=(from_far(keep.dz), cols(T)),
        ggrad=(from_far(keep.ggrad), cols(1)),
        dep=order(dep),
    )
    return call(kernel, ins, scan_results(), back_scratch(), "scan_backward")


def layer_back(micro, role, flag, lens, core, e, keep, wts, dep):
    def kernel(R):
        step = pl.program_id(0)

        @pl.when((R.flag[0] == 0) & (role == 1))
        def _():
            R.mine[...] = jnp.zeros_like(R.mine)
            R.theirs[...] = jnp.zeros_like(R.theirs)
            R.token[...] = jnp.zeros(TOKEN, F32)

        @pl.when((R.flag[0] == 1) | (role == 0))
        def _():
            @pl.when(step == 0)
            def _():
                gate_begin(R)
                scan_begin(micro, R)

            y, dy, ggrad = gate_block(R)
            scan_block(R, step, y, dy, ggrad)
            pl.when(step == STEPS - 1)(lambda: scan_end(micro, R))

    ins = dict(flag=(flag, SMEM), **gate_operands(e, keep, wts), **scan_operands(lens, core, keep, wts))
    return call(
        kernel,
        ins | dict(dep=order(dep)),
        gate_results() | scan_results(),
        back_scratch() | GATE_SCRATCH,
        "layer_backward",
    )


def input_rows(R, e, u, dr):
    s_zero = lax.rsqrt(jnp.mean(u * u, axis=1, keepdims=True) + EPS)
    gained = R.norm[...] * dr
    shared = s_zero * s_zero * s_zero * jnp.mean(u * gained, axis=1, keepdims=True)
    return e + s_zero * gained - u * shared


def input_send(core, keep, wts):
    def kernel(R):
        mine = half_rows(R.core[0])
        dr = R.mine[...].astype(F32) + R.came[...].astype(F32)
        value = input_rows(R, R.e[mine, :].astype(F32), R.u[mine, :].astype(F32), dr)
        R.low[...] = value.astype(BF16)
        R.token[...] = jnp.zeros(TOKEN, F32)

    ins = rows_operands(keep.e) | dict(
        core=(core, SMEM),
        u=(keep.u.array, keep.u.spec()),
        norm=(from_far(wts.norm), full((1, D))),
        mine=(keep.mine, VMEM),
        came=(keep.came, VMEM),
    )
    outs = dict(low=(shape_of((HALF, D), BF16), VMEM), token=(far(TOKEN, F32), full(TOKEN)))
    return call(kernel, ins, outs, {}, "input_send", grid=(1,), limit=SMALL_LIMIT)


def input_back(core, keep, wts, dep):
    def kernel(R):
        mine, theirs = half_rows(R.core[0]), half_rows(1 - R.core[0])
        parts = ((mine, R.mine, R.came), (theirs, R.theirs, R.left))
        for k, (rows, ours, other) in enumerate(parts):
            if hasattr(R, "e"):
                e = R.e[rows, :]
            else:
                e = (R.e_other if k else R.e_mine)[...]
            dr = ours[...].astype(F32) + other[...].astype(F32)
            R.du[rows, :] = input_rows(R, e.astype(F32), R.u[rows, :].astype(F32), dr)
        R.token[...] = jnp.zeros(TOKEN, F32)

    ins = rows_operands(keep.e) | dict(
        core=(core, SMEM),
        u=(keep.u.array, keep.u.spec()),
        norm=(from_far(wts.norm), full((1, D))),
        mine=(keep.mine, full((HALF, D))),
        came=(keep.came, full((HALF, D))),
        theirs=(keep.theirs, full((HALF, D))),
        left=(keep.left, full((HALF, D))),
        dep=order(dep),
    )
    outs = dict(du=(far((T, D), F32), full((T, D))), token=(far(TOKEN, F32), full(TOKEN)))
    return call(kernel, ins, outs, {}, "input_backward", grid=(1,), limit=SMALL_LIMIT)


def hold(value, dep):
    def kernel(R):
        R.out[...] = R.value[...]

    ins = dict(value=(value, VMEM), dep=order(dep))
    outs = dict(out=(shape_of(value.shape, value.dtype), VMEM))
    return call(kernel, ins, outs, {}, "hold", grid=(1,), limit=SMALL_LIMIT)["out"]


def swap(value):
    return lax.ppermute(value, "tensor", [(0, 1), (1, 0)])


def relay_up(value):
    return lax.ppermute(value, "pipe", [(0, 1), (1, 0)])


def relay_down(value):
    return lax.ppermute(value, "pipe", [(1, 0)])


def partners():
    def make(fn):
        return [fn(i // 8, (i // 2) % 4, i % 2) for i in range(32)]

    def pack(y, x, z):
        return y * 8 + x * 2 + z

    def wrap(v):
        return (v + 1) % 4 if v % 2 else (v - 1) % 4

    return [
        make(lambda y, x, z: pack(y, x ^ 1, z)),
        make(lambda y, x, z: pack(y ^ 1, x, z)),
        make(lambda y, x, z: pack(y, wrap(x), z)),
        make(lambda y, x, z: pack(wrap(y), x, z)),
        make(lambda y, x, z: pack(y, x, z ^ 1)),
    ]


STREAMS = 5


LAST = ((0, 4), (0, 1), (2, 1), (2, 3), (3, 4))


def dims_of(stream, late):
    if late:
        return [(stream + k) % 5 for k in range(1, 4)] + list(LAST[stream])
    return [(stream + k) % 5 for k in range(5)]


def ends_first(s):
    return dims_of(s, 0)[4] == LAST[s][0]


def round_groups(which):
    dims = sorted({last[which] for last in LAST})
    return [(d, [s for s in range(5) if LAST[s][which] == d]) for d in dims]


def block_order(maps, stream, late=0):
    order = [maps[d] for d in dims_of(stream, late)]
    count = len(order[0])
    table = np.zeros((count, count), np.int32)
    for me in range(count):
        for p in range(count):
            owner = me
            for k, step in enumerate(order):
                if (p >> (len(order) - 1 - k)) & 1:
                    owner = step[owner]
            table[me, p] = owner
    return table


TILES_EARLY = [("et", "n", LANES * k) for k in range(C // LANES)] + [
    ("rt", "dz", LANES * k) for k in range(C // LANES)
]
TILES_LATE = [("rt", "dx", LANES * k) for k in range(C // LANES)] + [
    ("rt", "bcdt", LANES * k) for k in range(3)
]


def deal(tiles):
    width = -(-len(tiles) // STREAMS)
    return [tiles[width * s : width * (s + 1)] for s in range(STREAMS)]


EARLY, LATE = deal(TILES_EARLY), deal(TILES_LATE)
PACK = 8
PACK_ROWS = 2 * PACK * (C // LANES)
PACK_STREAM = STREAMS - 1


def runs(tiles):
    out = []
    for at, (left, right, first) in enumerate(tiles):
        if out and out[-1][:2] == [left, right] and out[-1][2] + LANES * out[-1][3] == first:
            out[-1][3] += 1
        else:
            out.append([left, right, first, 1, at])
    return out


class Loader:
    def __init__(self, flag_ref, names, sources, held, sem):
        self.flag, self.names, self.sources, self.held, self.sem = flag_ref, names, sources, held, sem
        self.waited = set()

    def copy(self, k, m, early):
        span = pl.ds(m * T, T)
        ref = self.held[k]
        slot = ref.at[:, span] if ref.shape[0] == D else ref.at[span, :]
        return pltpu.make_async_copy(self.sources[4 * k + 2 * early + m], slot, self.sem.at[2 * k + m])

    def start(self, name):
        k = self.names.index(name)
        for m in range(2):
            pl.when(self.flag[0] == 1)(lambda: self.copy(k, m, 0).start())
            pl.when(self.flag[0] == 0)(lambda: self.copy(k, m, 1).start())

    def get(self, name):
        k = self.names.index(name)
        if name not in self.waited:
            self.waited.add(name)
            for m in range(2):
                self.copy(k, m, 0).wait()
        return self.held[k]


def held_shapes(arrays):
    shapes = []
    for a in arrays:
        rows, columns = a[0].shape
        shapes.append(pltpu.VMEM((rows, 2 * columns) if rows == D else (2 * rows, columns), BF16))
    return shapes


def products(loader, lefts, tiles, blocks, owner_of, place):
    rows = D // blocks
    chunk = max(384, rows)
    placed = []
    for left, right, first, count, at in runs(tiles):
        held, rhs = loader.get(left), loader.get(right)
        if left not in placed:
            placed.append(left)
            for p in range(blocks):
                start = pl.multiple_of(owner_of(p) * rows, 16)
                lefts[len(placed) - 1, p * rows : (p + 1) * rows, :] = held[pl.ds(start, rows), :]
        slot = placed.index(left)
        for c in range(D // chunk):
            span = slice(c * chunk, (c + 1) * chunk)
            value = dot(lefts[slot, span, :], rhs[:, first : first + LANES * count]).astype(BF16)
            for j in range(count):
                place(at + j, c * chunk, value[:, j * LANES : (j + 1) * LANES])


def early_kernel(blocks, flag_ref, table_ref, *refs):
    names = ["et", "n", "rt", "dz"]
    sources, refs = refs[:16], refs[16:]
    outs, token_ref = refs[: 2 * STREAMS], refs[2 * STREAMS]
    held, lefts, in_sem = refs[2 * STREAMS + 1 :]
    loader = Loader(flag_ref, names, sources, held, in_sem)
    for name in names:
        loader.start(name)
    half = D // 2
    for s in range(STREAMS):

        def place(tile, row, value):
            outs[2 * s + row // half][tile, row % half : row % half + value.shape[0], :] = value

        def owner_of(p):
            return table_ref[flag_ref[1] + s * blocks + p]

        products(loader, lefts, EARLY[s], blocks, owner_of, place)
    token_ref[...] = jnp.zeros(TOKEN, F32)


def early_grads(flag, table, arrays, blocks):
    out = []
    for s in range(STREAMS):
        out += [near((len(EARLY[s]), D // 2, LANES), BF16)] * 2
    flat = pl.pallas_call(
        functools.partial(early_kernel, blocks),
        in_specs=[SMEM, SMEM] + [HBM] * 16,
        out_specs=[VMEM] * (len(out) + 1),
        out_shape=tuple(out) + (shape_of(TOKEN, F32),),
        scratch_shapes=[
            held_shapes(arrays),
            pltpu.VMEM((2, D, 2 * T), BF16),
            pltpu.SemaphoreType.DMA((8,)),
        ],
        compiler_params=pltpu.CompilerParams(vmem_limit_bytes=VMEM_LIMIT),
        cost_estimate=COST,
        name="grad_early",
    )(flag, table, *[from_far(v) for a in arrays for v in a])
    return list(flat[0:-1:2]), list(flat[1:-1:2]), flat[-1]


def total_rows(s, early, late):
    return len(EARLY[s]) * early + len(LATE[s]) * late + (PACK_ROWS if s == PACK_STREAM else 0)


def split_pair(value):
    high = value.astype(BF16)
    return jnp.concatenate([high, (value - high.astype(F32)).astype(BF16)], axis=0)


def join_pair(pair):
    wide_pair = pair.astype(F32)
    return wide_pair[:PACK] + wide_pair[PACK:]


def late_kernel(blocks, flag_ref, table_ref, *refs):
    names = ["rt", "dx", "bcdt"]
    sources, refs = refs[:12], refs[12:]
    packs, refs = refs[:4], refs[4:]
    keeps, gots, refs = refs[:STREAMS], refs[STREAMS : 2 * STREAMS], refs[2 * STREAMS :]
    outs, token_ref = refs[: 2 * STREAMS], refs[2 * STREAMS]
    held, lefts, in_sem = refs[2 * STREAMS + 1 :]
    loader = Loader(flag_ref, names, sources, held, in_sem)
    for name in names:
        loader.start(name)
    half = D // 2
    quarter = half // 2
    for s in range(STREAMS):
        for j in range(len(EARLY[s])):
            for side in range(2):
                span = slice(side * quarter, (side + 1) * quarter)
                total = keeps[s][j, span, :].astype(F32) + gots[s][j, span, :].astype(F32)
                outs[2 * s + side][j * quarter : (j + 1) * quarter, :] = total.astype(BF16)
    last = flag_ref[0] == 1
    total = jnp.where(last, packs[0][...] + packs[1][...], packs[2][...] + packs[3][...])
    for j in range(C // LANES):
        pair = split_pair(total[:, j * LANES : (j + 1) * LANES])
        at = total_rows(PACK_STREAM, quarter, half) - PACK_ROWS + 2 * PACK * j
        for side in range(2):
            outs[2 * PACK_STREAM + side][at : at + 2 * PACK, :] = pair
    for s in range(STREAMS):
        base = len(EARLY[s]) * quarter

        def place(tile, row, value):
            at = base + tile * half + row % half
            outs[2 * s + row // half][at : at + value.shape[0], :] = value

        def owner_of(p):
            return table_ref[flag_ref[1] + s * blocks + p]

        products(loader, lefts, LATE[s], blocks, owner_of, place)
    token_ref[...] = jnp.zeros(TOKEN, F32)


def late_grads(flag, table, arrays, blocks, packs, keeps, gots):
    out = []
    for s in range(STREAMS):
        out += [near((total_rows(s, D // 4, D // 2), LANES), BF16)] * 2
    flat = pl.pallas_call(
        functools.partial(late_kernel, blocks),
        in_specs=[SMEM, SMEM] + [HBM] * 12 + [VMEM] * (4 + 2 * STREAMS),
        out_specs=[VMEM] * (len(out) + 1),
        out_shape=tuple(out) + (shape_of(TOKEN, F32),),
        scratch_shapes=[
            held_shapes(arrays),
            pltpu.VMEM((1, D, 2 * T), BF16),
            pltpu.SemaphoreType.DMA((6,)),
        ],
        compiler_params=pltpu.CompilerParams(vmem_limit_bytes=VMEM_LIMIT),
        cost_estimate=COST,
        name="grad_late",
    )(
        flag,
        table,
        *[from_far(v) for a in arrays for v in a],
        *packs,
        *keeps,
        *gots,
    )
    return list(flat[0:-1:2]), list(flat[1:-1:2]), flat[-1]


def fold(s, keep, got, early, late, deps):
    def kernel(keep, got, *refs):
        next_keep, next_send, token = refs[len(deps) :]
        at = to = 0
        for rows, tiles in ((early, EARLY[s]), (late, LATE[s])):
            for _ in tiles:
                next_send[to : to + rows // 2, :] = add(keep, got, at + rows // 2, rows // 2).astype(BF16)
                next_keep[to : to + rows // 2, :] = add(keep, got, at, rows // 2).astype(BF16)
                at += rows
                to += rows // 2
        if s == PACK_STREAM:
            add_packs((keep, at), (got, at), ((next_keep, to), (next_send, to)))
        token[...] = jnp.zeros(TOKEN, F32)

    rows = total_rows(s, early // 2, late // 2)
    out = [near((rows, LANES), BF16), near((rows, LANES), BF16), near(TOKEN, F32)]
    return pl.pallas_call(
        kernel,
        in_specs=[VMEM] * 2 + [ANY] * len(deps),
        out_specs=[VMEM, VMEM, VMEM],
        out_shape=tuple(out),
        compiler_params=pltpu.CompilerParams(vmem_limit_bytes=SMALL_LIMIT),
        cost_estimate=COST,
        name="fold_grads",
    )(keep, got, *deps)


def add(keep, got, at, rows, got_at=None):
    got_at = at if got_at is None else got_at
    return keep[at : at + rows, :].astype(F32) + got[got_at : got_at + rows, :].astype(F32)


def pack_sum(keep, keep_at, got, got_at, j):
    a = keep[keep_at + 2 * PACK * j : keep_at + 2 * PACK * (j + 1), :]
    b = got[got_at + 2 * PACK * j : got_at + 2 * PACK * (j + 1), :]
    return join_pair(a) + join_pair(b)


def add_packs(keep, got, targets):
    for j in range(C // LANES):
        pair = split_pair(pack_sum(*keep, *got, j))
        for ref, at in targets:
            ref[at + 2 * PACK * j : at + 2 * PACK * (j + 1), :] = pair


BLOCK = 48


def payload(s, which):
    early = BLOCK if ends_first(s) != bool(which) else 0
    late = BLOCK if which else 2 * BLOCK
    return len(EARLY[s]) * early, len(LATE[s]) * late, PACK_ROWS if s == PACK_STREAM else 0


def places(which):
    where, sizes = {}, []
    for g, (_, streams) in enumerate(round_groups(which)):
        at = 0
        for s in streams:
            where[s] = (g, at)
            at += sum(payload(s, which))
        sizes.append(at)
    return where, sizes


def keep_rows(s):
    early = len(EARLY[s]) * BLOCK
    return early if ends_first(s) else 2 * early, len(LATE[s]) * 2 * BLOCK, payload(s, 0)[2]


def third_kernel(*refs):
    keeps, gots = refs[:STREAMS], refs[STREAMS : 2 * STREAMS]
    next_keeps, sends = refs[2 * STREAMS : 3 * STREAMS], refs[3 * STREAMS :]
    where, _ = places(0)
    for s in range(STREAMS):
        keep, got, out = keeps[s], gots[s], next_keeps[s]
        group, to = where[s]
        target = sends[group]
        early = len(EARLY[s]) * BLOCK
        at = 0
        for j in range(len(EARLY[s])):
            out[j * BLOCK : (j + 1) * BLOCK, :] = add(keep, got, at, BLOCK).astype(BF16)
            value = add(keep, got, at + BLOCK, BLOCK).astype(BF16)
            if ends_first(s):
                target[to + j * BLOCK : to + (j + 1) * BLOCK, :] = value
            else:
                out[early + j * BLOCK : early + (j + 1) * BLOCK, :] = value
            at += 2 * BLOCK
        base, to = keep_rows(s)[0], to + payload(s, 0)[0]
        half = 2 * BLOCK
        for j in range(len(LATE[s])):
            out[base + j * half : base + (j + 1) * half, :] = add(keep, got, at, half).astype(BF16)
            target[to + j * half : to + (j + 1) * half, :] = add(keep, got, at + half, half).astype(BF16)
            at += 2 * half
        if s == PACK_STREAM:
            spots = ((out, base + len(LATE[s]) * half), (target, to + len(LATE[s]) * half))
            add_packs((keep, at), (got, at), spots)


def fourth_kernel(*refs):
    groups = len(round_groups(0))
    keeps, gots = refs[:STREAMS], refs[STREAMS : STREAMS + groups]
    refs = refs[STREAMS + groups :]
    dones, next_keeps, sends = refs[:STREAMS], refs[STREAMS : 2 * STREAMS], refs[2 * STREAMS :]
    came, _ = places(0)
    where, _ = places(1)
    for s in range(STREAMS):
        keep, got, out = keeps[s], gots[came[s][0]], next_keeps[s]
        target, to = sends[where[s][0]], where[s][1]
        at = came[s][1]
        early = len(EARLY[s]) * BLOCK
        if ends_first(s):
            dones[s][...] = add(keep, got, 0, early, at)
        else:
            dones[s][...] = keep[:early, :].astype(F32)
            target[to : to + early, :] = keep[early : 2 * early, :]
        at, to, base = at + payload(s, 0)[0], to + payload(s, 1)[0], keep_rows(s)[0]
        for j in range(len(LATE[s])):
            first = base + 2 * BLOCK * j
            out[j * BLOCK : (j + 1) * BLOCK, :] = add(keep, got, first, BLOCK, at).astype(BF16)
            value = add(keep, got, first + BLOCK, BLOCK, at + BLOCK).astype(BF16)
            target[to + j * BLOCK : to + (j + 1) * BLOCK, :] = value
            at += 2 * BLOCK
        if s == PACK_STREAM:
            late = len(LATE[s]) * BLOCK
            add_packs((keep, base + 2 * late), (got, at), ((out, late), (target, to + late)))


def last_folds(kernel, operands, shapes, name):
    return pl.pallas_call(
        kernel,
        in_specs=[VMEM] * len(operands),
        out_specs=[VMEM] * len(shapes),
        out_shape=tuple(near((rows, LANES), dtype) for rows, dtype in shapes),
        compiler_params=pltpu.CompilerParams(vmem_limit_bytes=SMALL_LIMIT),
        cost_estimate=COST,
        name=name,
    )(*operands)


def fold_third(keeps, gots):
    shapes = [(sum(keep_rows(s)), BF16) for s in range(STREAMS)]
    shapes += [(rows, BF16) for rows in places(0)[1]]
    flat = last_folds(third_kernel, [*keeps, *gots], shapes, "fold_third")
    return flat[:STREAMS], flat[STREAMS:]


def fold_fourth(keeps, gots):
    shapes = [(len(EARLY[s]) * BLOCK, F32) for s in range(STREAMS)]
    shapes += [(sum(payload(s, 1)[1:]), BF16) for s in range(STREAMS)]
    shapes += [(rows, BF16) for rows in places(1)[1]]
    flat = last_folds(fourth_kernel, [*keeps, *gots], shapes, "fold_fourth")
    return flat[:STREAMS], flat[STREAMS : 2 * STREAMS], flat[2 * STREAMS :]


def end_kernel(rows, heads, core_ref, *refs):
    groups = len(round_groups(1))
    dones, keeps, gots = refs[:STREAMS], refs[STREAMS : 2 * STREAMS], refs[2 * STREAMS :][:groups]
    refs = refs[2 * STREAMS + groups :]
    out_ref, zx_ref, dt_ref, cx_ref, bx_ref, gate_ref, heads_ref = refs[:7]
    mine_ref, theirs_ref, shared_ref, bcdt_s = refs[7:]
    came, _ = places(1)

    def place(right, first, value):
        if right == "n":
            out_ref[:, first : first + LANES] = value
        elif right == "bcdt":
            bcdt_s[:, first : first + LANES] = value
        else:
            zx_ref[:, 0 if right == "dz" else 1, first : first + LANES] = value

    for s in range(STREAMS):
        got, at = gots[came[s][0]], came[s][1]
        for j, (_, right, first) in enumerate(EARLY[s]):
            value = dones[s][j * rows : (j + 1) * rows, :]
            if not ends_first(s):
                value = value + got[at : at + rows, :].astype(F32)
                at += rows
            place(right, first, value)
        for j, (_, right, first) in enumerate(LATE[s]):
            place(right, first, add(keeps[s], got, j * rows, rows, at))
            at += rows
        if s == PACK_STREAM:
            keep, keep_at = keeps[s], len(LATE[s]) * rows
            for j in range(C // LANES):
                lanes = slice(j * LANES, (j + 1) * LANES)
                value = pack_sum(keep, keep_at, got, at, j)
                cx_ref[:, lanes] = value[0:4]
                bx_ref[:, lanes] = value[4:5]
                gate_ref[:, lanes] = value[5:6]
                shared_ref[:, lanes] = value[6:8]
                if j == 10:
                    for k in range(3):
                        moved = pltpu.roll(value, (LANES - 32 * k) % LANES, 1) if k else value
                        heads_ref[k : k + 1, :] = moved[7:8, :heads]
    part = rows // 2
    mine_ref[...] = bcdt_s[pl.ds(pl.multiple_of(core_ref[0] * part, 8), part), : 2 * NS]
    theirs_ref[...] = bcdt_s[pl.ds(pl.multiple_of((1 - core_ref[0]) * part, 8), part), : 2 * NS]
    dt_ref[...] = bcdt_s[:, 2 * NS :].T[:heads, :]


def end(core, dones, keeps, gots, rows, heads):
    return pl.pallas_call(
        functools.partial(end_kernel, rows, heads),
        in_specs=[SMEM] + [VMEM] * (2 * STREAMS + len(gots)),
        out_specs=[VMEM] * 10,
        out_shape=(
            shape_of((rows, C), F32),
            shape_of((rows, 2, C), F32),
            shape_of((heads, rows), F32),
            shape_of((4, C), F32),
            shape_of((1, C), F32),
            shape_of((1, C), F32),
            shape_of((3, heads), F32),
            shape_of((rows // 2, 2 * NS), F32),
            shape_of((rows // 2, 2 * NS), F32),
            shape_of((2, C), F32),
        ),
        scratch_shapes=[pltpu.VMEM((rows, 3 * LANES), F32)],
        compiler_params=pltpu.CompilerParams(vmem_limit_bytes=SMALL_LIMIT),
        cost_estimate=COST,
        name="grad_end",
    )(core, *dones, *keeps, *gots)


def last_kernel(mine_ref, other_ref, shared_ref, other_shared_ref, bc_ref, norm_ref, conv_ref, bias_ref):
    bc_ref[...] = mine_ref[...] + other_ref[...]
    total = shared_ref[...] + other_shared_ref[...]
    norm_ref[...] = total[0:1]
    for k in range(4):
        conv_ref[k : k + 1, :] = total[1:2, 2 * NS * k : 2 * NS * (k + 1)]
    bias_ref[...] = total[1:2, 8 * NS : 10 * NS]


def last_sums(mine, other, shared, other_shared):
    return pl.pallas_call(
        last_kernel,
        in_specs=[VMEM] * 4,
        out_specs=[VMEM] * 4,
        out_shape=(
            shape_of(mine.shape, F32),
            shape_of((1, C), F32),
            shape_of((4, 2 * NS), F32),
            shape_of((1, 2 * NS), F32),
        ),
        compiler_params=pltpu.CompilerParams(vmem_limit_bytes=SMALL_LIMIT),
        cost_estimate=COST,
        name="last_sums",
    )(mine, other, shared, other_shared)


def pick_kernel(flag_ref, late0, late1, early0, early1, _, out_ref, token_ref, held, sem):
    for m, (late, early) in enumerate(((late0, early0), (late1, early1))):

        def start(source):
            pltpu.make_async_copy(source, held.at[m], sem.at[m]).start()

        pl.when(flag_ref[0] == 1)(lambda: start(late))
        pl.when(flag_ref[0] == 0)(lambda: start(early))
    for m in range(2):
        pltpu.make_async_copy(early0, held.at[m], sem.at[m]).wait()
        pltpu.make_async_copy(held.at[m], out_ref.at[m], sem.at[2 + m]).start()
    for m in range(2):
        pltpu.make_async_copy(held.at[m], out_ref.at[m], sem.at[2 + m]).wait()
    token_ref[...] = jnp.zeros(TOKEN, F32)


def pick(flag, late, early, dep):
    return pl.pallas_call(
        pick_kernel,
        in_specs=[SMEM] + [HBM] * 4 + [ANY],
        out_specs=[HBM, VMEM],
        out_shape=(far((2, T, D), F32), shape_of(TOKEN, F32)),
        scratch_shapes=[pltpu.VMEM((2, T, D), F32), pltpu.SemaphoreType.DMA((4,))],
        compiler_params=pltpu.CompilerParams(vmem_limit_bytes=SMALL_LIMIT),
        cost_estimate=COST,
        name="pick_section",
    )(flag, *[from_far(v) for v in (*late, *early)], dep)


def send(value, step):
    return lax.ppermute(value, "dp", [(i, to) for i, to in enumerate(step)])


def body(
    tokens,
    cotangent,
    lengths,
    norm_gain,
    w_zx,
    w_bc,
    w_dt,
    conv_x,
    bias_x,
    conv_bc,
    bias_bc,
    head_params,
    gate_gain,
    w_out,
):
    is_last = lax.axis_index("pipe") == 1
    core_at = lax.axis_index("tensor")
    heads = w_dt.shape[2]
    wts = SimpleNamespace(
        norm=norm_gain,
        zx=jnp.transpose(w_zx[0], (1, 0, 2)),
        bc=w_bc[0],
        dt=jnp.pad(w_dt[0].T, ((0, LANES - heads), (0, 0))),
        cx=conv_x[0],
        bx=bias_x,
        cbc=conv_bc[0],
        bbc=bias_bc,
        hp=jnp.transpose(head_params, (1, 0, 2)),
        gate=gate_gain,
        out=w_out[0],
    )

    flag = is_last.astype(jnp.int32).reshape(1)

    lens = lengths

    def run(m, u, dep):
        keep = SimpleNamespace(**forward(m, lens, u, wts, dep))
        keep.u = u
        keep.part = (keep.part0, keep.part1)
        keep.other = tuple(swap(v) for v in keep.part)
        keep.other_sq = swap(keep.sq)
        return keep

    core = core_at.astype(jnp.int32).reshape(1)

    def backward(m, role, keep, e, dep):
        keep.e = e
        vars(keep).update(layer_back(m, role, flag, lens, core, e, keep, wts, dep))
        share(keep)

    def share(keep):
        keep.came, keep.left = swap(keep.theirs), swap(keep.mine)

    def send_down(keep):
        result = input_send(core, keep, wts)
        return relay_down(result["low"]), result["token"]

    def finish(keep, dep):
        result = input_back(core, keep, wts, dep)
        keep.du = result["du"]
        return result["token"]

    keep_a = run(0, Rows(tokens, 0), (lens,))
    vars(keep_a).update(join(keep_a, (lens,), True))
    sent_a = relay_up(keep_a.low)
    keep_b = run(1, Rows(tokens, 1), keep_a.token)
    vars(keep_b).update(join(keep_b, (sent_a,), True))
    sent_b = relay_up(keep_b.low)
    keep_c = run(0, Rows(sent_a), keep_b.token)
    keep_d = run(1, Rows(sent_b), keep_c.token)
    backward(0, 1, keep_c, Rows(cotangent, 0), keep_d.token)
    sent_c, token = send_down(keep_c)
    backward(1, 1, keep_d, Rows(cotangent, 1), token)
    sent_d, token = send_down(keep_d)
    backward(0, 0, keep_a, Halves(sent_c, swap(sent_c)), token)
    sent_d = hold(sent_d, keep_a.token)
    keep_b.e = Halves(sent_d, swap(sent_d))
    vars(keep_b).update(gate_back(core, keep_b.e, keep_b, wts, (touch(keep_a.came, *[keep.left for keep in (keep_a, keep_c, keep_d)]),)))

    dp = lax.axis_size("dp")
    maps = partners()
    me = lax.axis_index("dp")
    tables = [
        jnp.asarray(np.stack([block_order(maps, s, late) for s in range(STREAMS)], axis=1).reshape(-1))
        for late in range(2)
    ]
    flag = jnp.stack([is_last.astype(jnp.int32), me.astype(jnp.int32) * (STREAMS * dp)])

    def both(name):
        return tuple(getattr(keep, name) for keep in (keep_c, keep_d, keep_a, keep_b))

    arrays = [both(k) for k in ("et", "n", "rt", "dz")]
    keeps, sends, token = early_grads(flag, tables[0], arrays, dp)
    gots = [send(sends[s], maps[dims_of(s, 0)[0]]) for s in range(STREAMS)]
    vars(keep_b).update(scan_back(1, lens, core, keep_b, wts, (token,)))
    share(keep_b)
    arrays = [both(k) for k in ("rt", "dx", "bcdt")]
    keeps, sends, token = late_grads(flag, tables[1], arrays, dp, both("pack"), keeps, gots)
    tokens_in = [finish(keep, (token,)) for keep in (keep_a, keep_b, keep_c, keep_d)]
    join_c = SimpleNamespace(**join(keep_c, (token,), False))
    join_d = SimpleNamespace(**join(keep_d, (token,), False))
    deps = [[*tokens_in, join_c.token, join_d.token]]
    section_out, token_a = pick(
        flag, (join_c.res, join_d.res), (keep_a.res, keep_b.res), token
    )
    section_grad, token_b = pick(flag, (keep_c.du, keep_d.du), (keep_a.du, keep_b.du), token)
    deps += [[token_a, token_b]]
    early, late = D // 4, D // 2
    gots = [send(sends[s], maps[dims_of(s, 1)[0]]) for s in range(STREAMS)]
    token = None
    for k in range(1, 3):
        for s in range(STREAMS):
            order = [token] if token is not None else []
            if s == 0:
                order += deps[k - 1]
            keeps[s], sends[s], token = fold(s, keeps[s], gots[s], early, late, order)
            gots[s] = send(sends[s], maps[dims_of(s, 1)[k]])
        early, late = early // 2, late // 2
    keeps, sends = fold_third(keeps, gots)
    gots = [send(v, maps[d]) for v, (d, _) in zip(sends, round_groups(0))]
    dones, keeps, sends = fold_fourth(keeps, gots)
    gots = [send(v, maps[d]) for v, (d, _) in zip(sends, round_groups(1))]
    g_out, g_zx, g_dt, g_cx, g_bx, g_gate, g_heads, mine, theirs, shared = end(
        core, dones, keeps, gots, D // dp, heads
    )
    g_bc, g_norm, g_cbc, g_bbc = last_sums(mine, swap(theirs), shared, swap(shared))
    return (
        section_out[None],
        section_grad[None],
        g_norm,
        g_zx[None],
        g_bc[None],
        g_dt.T[None],
        g_cx[None],
        g_bx,
        g_cbc[None],
        g_bbc,
        g_heads[None],
        g_gate,
        g_out.T[None],
    )


def solution(mesh):
    in_specs = (
        P(None, "dp", None),
        P(None, "dp", None),
        P(None, "dp", None),
        P("pipe", None),
        P("pipe", None, None, "tensor"),
        P("pipe", None, None),
        P("pipe", None, "tensor"),
        P("pipe", None, "tensor"),
        P("pipe", "tensor"),
        P("pipe", None, None),
        P("pipe", None),
        P("pipe", None, "tensor"),
        P("pipe", "tensor"),
        P("pipe", "tensor", None),
    )
    out_specs = (
        P("pipe", None, "dp", None),
        P("pipe", None, "dp", None),
        P("pipe", None),
        P("pipe", "dp", None, "tensor"),
        P("pipe", ("dp", "tensor"), None),
        P("pipe", "dp", "tensor"),
        P("pipe", None, "tensor"),
        P("pipe", "tensor"),
        P("pipe", None, None),
        P("pipe", None),
        P("pipe", None, "tensor"),
        P("pipe", "tensor"),
        P("pipe", "tensor", "dp"),
    )
    return jax.shard_map(body, mesh=mesh, in_specs=in_specs, out_specs=out_specs, check_vma=False)
```

```python
import functools
from types import SimpleNamespace

import jax
import jax.numpy as jnp
import numpy as np
from jax import lax
from jax.experimental import pallas as pl
from jax.experimental.pallas import tpu as pltpu
from jax.sharding import PartitionSpec as P

F32 = jnp.float32
BF16 = jnp.bfloat16
HIGH = lax.Precision.HIGHEST
EPS = 1e-05
T = 256
D = 1536
C = 1536
W = 256
STEPS = C // W
HEAD = 64
PER = W // HEAD
NS = 128
DI = 3072
LANES = 128
HALF = T // 2
NT = (((1,), (1,)), ((), ()))
VMEM_LIMIT = 24 * 1024 * 1024
SMALL_LIMIT = 16 * 1024 * 1024
COST = pl.CostEstimate(flops=1, bytes_accessed=1, transcendentals=0)


def dot(a, b):
    return jnp.dot(a, b, preferred_element_type=F32)


def dot_nt(a, b):
    return lax.dot_general(a, b, NT, preferred_element_type=F32)


def dot_exact(a, b):
    return jnp.dot(a, b, precision=HIGH, preferred_element_type=F32)


def group_sums(values, group):
    terms = []
    for value in values:
        high = value.astype(BF16)
        terms += [high, (value - high.astype(F32)).astype(BF16)]
    out = dot(jnp.concatenate(terms, axis=0), group.astype(BF16))
    at, sums = 0, []
    for value in values:
        rows = value.shape[0]
        sums.append(out[at : at + rows] + out[at + rows : at + 2 * rows])
        at += 2 * rows
    return sums


def params(steps):
    return pltpu.CompilerParams(
        dimension_semantics=("arbitrary",) * steps, vmem_limit_bytes=VMEM_LIMIT
    )


def sigmoid(v):
    return 1.0 / (1.0 + jnp.exp(-v))


def seg_ids(len_ref, micro, pos):
    end = jnp.int32(0)
    seg = jnp.zeros(pos.shape, jnp.int32)
    for k in range(4):
        end = end + len_ref[micro, 0, k]
        seg = seg + (pos >= end).astype(jnp.int32)
    return seg


def keep_masks(len_ref, micro):
    pos = lax.broadcasted_iota(jnp.int32, (T, LANES), 0)
    seg = seg_ids(len_ref, micro, pos)
    out = []
    for back in range(1, 4):
        same = (seg_ids(len_ref, micro, pos - back) == seg) & (pos >= back)
        out.append(same.astype(F32))
    return out


def wide(mask, width=W):
    return jnp.concatenate([mask] * (width // LANES), axis=1)


def conv(v, taps, bias, keeps):
    total = bias + taps[3] * v
    for back in range(1, 4):
        total = total + taps[3 - back] * (pltpu.roll(v, back, 0) * keeps[back - 1])
    return total


def conv_back(dtotal, v, taps, keeps):
    dv = taps[3] * dtotal
    grads = [None] * 4
    grads[3] = jnp.sum(dtotal * v, axis=0, keepdims=True)
    for back in range(1, 4):
        masked = dtotal * keeps[back - 1]
        grads[3 - back] = jnp.sum(masked * pltpu.roll(v, back, 0), axis=0, keepdims=True)
        dv = dv + taps[3 - back] * pltpu.roll(masked, T - back, 0)
    return dv, grads, jnp.sum(dtotal, axis=0, keepdims=True)


def rows_of(ref, count):
    return [ref[k : k + 1, :] for k in range(count)]


def tri_mask(len_ref, micro, transposed=False):
    first = lax.broadcasted_iota(jnp.int32, (T, T), 0)
    second = lax.broadcasted_iota(jnp.int32, (T, T), 1)
    same = seg_ids(len_ref, micro, first) == seg_ids(len_ref, micro, second)
    order = (second >= first) if transposed else (first >= second)
    return (same & order).astype(F32)


def lower_ones(transposed):
    first = lax.broadcasted_iota(jnp.int32, (T, T), 0)
    second = lax.broadcasted_iota(jnp.int32, (T, T), 1)
    return ((second >= first) if transposed else (first >= second)).astype(F32)


def softplus(v):
    return jnp.maximum(v, 0.0) + jnp.log1p(jnp.exp(-jnp.abs(v)))


def spread_steps(dt, cums, dt_s, cum_s, cumt_s):
    turned = cums.T
    for i in range(STEPS):
        shift = (LANES - PER * i) % LANES
        dt_s[i] = pltpu.roll(dt, shift, 1) if shift else dt
        cum_s[i] = pltpu.roll(cums, shift, 1) if shift else cums
        cumt_s[i, 0:PER, :] = turned[PER * i : PER * (i + 1), :]


def head_lanes(value, k):
    lane = lax.broadcasted_iota(jnp.int32, value.shape, 1)
    return jnp.where((lane >= k * HEAD) & (lane < (k + 1) * HEAD), value, jnp.zeros_like(value))


def per_channel(dt):
    lane = lax.broadcasted_iota(jnp.int32, dt.shape, 1)
    tiles = []
    for p in range(PER // 2):
        tiles.append(
            jnp.where(
                lane < HEAD,
                jnp.broadcast_to(dt[:, 2 * p : 2 * p + 1], dt.shape),
                jnp.broadcast_to(dt[:, 2 * p + 1 : 2 * p + 2], dt.shape),
            )
        )
    return jnp.concatenate(tiles, axis=1)


def spread_heads(hp_ref, hp_s):
    count = hp_ref.shape[2]
    hp_s[STEPS] = jnp.zeros((8, LANES), F32)
    for k in range(3):
        hp_s[STEPS, k : k + 1, 0:count] = hp_ref[k]
    value = hp_s[STEPS]
    for i in range(STEPS):
        shift = (LANES - PER * i) % LANES
        hp_s[i] = pltpu.roll(value, shift, 1) if shift else value
    return value


def skip_row(hp_s, step):
    return per_channel(hp_s[step])[2:3, :]


def full(shape):
    return pl.BlockSpec(shape, lambda i: (0,) * len(shape))


def cols(rows):
    return pl.BlockSpec((rows, W), lambda i: (0, i))


def shape_of(shape, dtype):
    return jax.ShapeDtypeStruct(shape, dtype)


def far(shape, dtype):
    return pltpu.HBM(shape, dtype)


def near(shape, dtype):
    return pltpu.VMEM(shape, dtype)


class Rows:
    def __init__(self, array, m=None):
        self.array, self.m = array, m

    def spec(self):
        if self.m is None:
            return pl.BlockSpec((T, D), lambda *i: (0, 0))
        return pl.BlockSpec((None, T, D), lambda *i: (self.m, 0, 0))


def order(dep):
    if isinstance(dep, tuple):
        return dep[0], ANY
    return from_far(dep), HBM


class Halves:
    def __init__(self, mine, other):
        self.mine, self.other = mine, other


def rows_operands(source, name="e"):
    if isinstance(source, Rows):
        return {name: (source.array, source.spec())}
    half = pl.BlockSpec((HALF, D), lambda *i: (0, 0))
    return {name + MINE: (source.mine, half), name + OTHER: (source.other, half)}


MINE, OTHER = "_mine", "_other"


def half_rows(core):
    return pl.ds(pl.multiple_of(core * HALF, HALF), HALF)


def gather_rows(R, name, target):
    if hasattr(R, name):
        target[...] = getattr(R, name)[...].astype(target.dtype)
    else:
        target[half_rows(R.core[0]), :] = getattr(R, name + MINE)[...].astype(target.dtype)
        target[half_rows(1 - R.core[0]), :] = getattr(R, name + OTHER)[...].astype(target.dtype)


def part_rows(R, name, k, at=0, count=HALF):
    if hasattr(R, name):
        first = (1 - R.core[0] if k else R.core[0]) * HALF + at
        return getattr(R, name)[pl.ds(pl.multiple_of(first, STRIP), count), :].astype(F32)
    return getattr(R, name + (OTHER if k else MINE))[pl.ds(at, count), :].astype(F32)


STRIP = 32


def strips(rows, body):
    def step(c, _):
        body(pl.multiple_of(c * STRIP, STRIP))
        return 0

    lax.fori_loop(0, rows // STRIP, step, 0)


def ours(R, role):
    return R.flag[0] == role


def from_far(value):
    return pltpu.with_memory_space_constraint(value, pltpu.HBM)


TOKEN = (8, LANES)


SMEM = pl.BlockSpec(memory_space=pltpu.SMEM)
VMEM = pl.BlockSpec(memory_space=pltpu.VMEM)
ANY = pl.BlockSpec(memory_space=pl.ANY)
HBM = pl.BlockSpec(memory_space=pltpu.HBM)


def call(body, ins, outs, scratch, name, grid=(STEPS,), limit=VMEM_LIMIT):
    names = [*ins, *outs, *scratch]

    def kernel(*refs):
        body(SimpleNamespace(**dict(zip(names, refs))))

    values = pl.pallas_call(
        kernel,
        grid=grid,
        in_specs=[v[1] for v in ins.values()],
        out_specs=[v[1] for v in outs.values()],
        out_shape=tuple(v[0] for v in outs.values()),
        scratch_shapes=list(scratch.values()),
        compiler_params=pltpu.CompilerParams(
            dimension_semantics=("arbitrary",) * len(grid), vmem_limit_bytes=limit
        ),
        cost_estimate=COST,
        name=name,
    )(*[v[0] for v in ins.values()])
    return dict(zip(outs, values))


def scan_scratch():
    return dict(
        keep_s=pltpu.VMEM((3, T, LANES), F32),
        dt_s=pltpu.VMEM((STEPS, T, LANES), F32),
        cum_s=pltpu.VMEM((STEPS, T, LANES), F32),
        cumt_s=pltpu.VMEM((STEPS, 8, T), F32),
        hp_s=pltpu.VMEM((STEPS + 1, 8, LANES), F32),
        acc_s=pltpu.VMEM((T, D), F32),
    )


def forward_kernel(micro, R):
    step = pl.program_id(0)

    @pl.when(step == 0)
    def _():
        gather_rows(R, "u", R.u_s)
        u = R.u_s[...].astype(F32)
        s_zero = lax.rsqrt(jnp.mean(u * u, axis=1, keepdims=True) + EPS)
        low = (u * s_zero * R.norm[...]).astype(BF16)
        R.r_s[...] = low
        R.rt[...] = low.T
        keeps = keep_masks(R.lens, micro)
        for k in range(3):
            R.keep_s[k] = keeps[k]
        bcr = dot(low, R.bc[...])
        R.bcr[...] = bcr
        dtr = dot_nt(low, R.dt[...])
        R.dtr[...] = dtr
        total = conv(bcr, rows_of(R.cbc, 4), R.bbc[...], [wide(k, 2 * NS) for k in keeps])
        act = total * sigmoid(total)
        score = dot_nt(act[:, NS:].astype(BF16), act[:, :NS].astype(BF16)) * tri_mask(R.lens, micro)
        R.score_s[...] = score
        R.scoret[...] = score.T
        hp = spread_heads(R.hp, R.hp_s)
        dt = softplus(dtr + hp[0:1, :])
        rates = dt * (-jnp.exp(hp[1:2, :]))
        cums = dot_exact(lower_ones(False), rates)
        R.cums[...] = cums
        spread_steps(dt, cums, R.dt_s, R.cum_s, R.cumt_s)
        R.acc_s[...] = jnp.zeros_like(R.acc_s)
        R.sq[...] = jnp.zeros_like(R.sq)

    keeps = [wide(R.keep_s[k]) for k in range(3)]
    low_z = dot(R.r_s[...], R.zx[0]).astype(BF16)
    low_x = dot(R.r_s[...], R.zx[1]).astype(BF16)
    R.z[...] = low_z
    R.x[...] = low_x
    z = low_z.astype(F32)
    x = low_x.astype(F32)
    total = conv(x, rows_of(R.cx, 4), R.bx[...], keeps)
    xc = total * sigmoid(total)
    cums = R.cum_s[step]
    cumt = R.cumt_s[step]
    xt = (xc * per_channel(R.dt_s[step])).astype(BF16)
    R.xt[...] = xt
    top = jnp.zeros((HALF, W), F32)
    bottom = jnp.zeros((HALF, W), F32)
    for k in range(PER):
        mine = head_lanes(xt, k)
        col = cums[:, k : k + 1]
        row = cumt[k : k + 1, :]
        mix = R.score_s[0:HALF, 0:HALF] * jnp.exp(jnp.minimum(col[:HALF] - row[:, :HALF], 0.0))
        top = top + dot(mix.astype(BF16), mine[:HALF])
        mix = R.score_s[HALF:T, :] * jnp.exp(jnp.minimum(col[HALF:] - row, 0.0))
        bottom = bottom + dot(mix.astype(BF16), mine)
    y = jnp.concatenate([top, bottom], axis=0) + skip_row(R.hp_s, step) * xc
    R.y[...] = y
    g = y * (z * sigmoid(z))
    squares = g * g
    for k in range(W // LANES):
        R.sq[...] += squares[:, k * LANES : (k + 1) * LANES]
    R.acc_s[...] += dot((g * R.gate[...]).astype(BF16), R.out[...])

    @pl.when(step == STEPS - 1)
    def _():
        R.part0[...] = R.acc_s[:HALF, :].astype(BF16)
        R.part1[...] = R.acc_s[HALF:, :].astype(BF16)
        R.token[...] = jnp.zeros(TOKEN, F32)


def small_operands(wts):
    return dict(
        bc=(wts.bc, full((D, 2 * NS))),
        dt=(wts.dt, full((LANES, D))),
        cx=(from_far(wts.cx), cols(4)),
        bx=(from_far(wts.bx), cols(1)),
        cbc=(from_far(wts.cbc), full((4, 2 * NS))),
        bbc=(from_far(wts.bbc), full((1, 2 * NS))),
        hp=(from_far(wts.hp), full(wts.hp.shape)),
    )


def forward(micro, role, flag, lens, core, u, wts, dep):
    def kernel(R):
        @pl.when(R.flag[0] != role)
        def _():
            for ref in (R.part0, R.part1, R.sq, R.token):
                ref[...] = jnp.zeros_like(ref)

        pl.when(ours(R, role))(lambda: forward_kernel(micro, R))

    ins = rows_operands(u, "u") | dict(
        flag=(flag, SMEM),
        core=(core, SMEM),
        lens=(lens, SMEM),
        norm=(from_far(wts.norm), full((1, D))),
        zx=(from_far(wts.zx), pl.BlockSpec((2, D, W), lambda i: (0, 0, i))),
        out=(from_far(wts.out), pl.BlockSpec((W, D), lambda i: (i, 0))),
        gate=(from_far(wts.gate), cols(1)),
        **small_operands(wts),
        dep=order(dep),
    )
    outs = dict(
        rt=(far((D, T), BF16), full((D, T))),
        z=(far((T, C), BF16), cols(T)),
        x=(far((T, C), BF16), cols(T)),
        y=(far((T, C), F32), cols(T)),
        bcr=(far((T, 2 * NS), F32), full((T, 2 * NS))),
        dtr=(far((T, LANES), F32), full((T, LANES))),
        part0=(shape_of((HALF, D), BF16), full((HALF, D))),
        part1=(shape_of((HALF, D), BF16), full((HALF, D))),
        sq=(shape_of((T, LANES), F32), full((T, LANES))),
        xt=(far((T, C), BF16), cols(T)),
        scoret=(far((T, T), F32), full((T, T))),
        cums=(far((T, LANES), F32), full((T, LANES))),
        token=(far(TOKEN, F32), full(TOKEN)),
    )
    scratch = scan_scratch() | dict(
        r_s=pltpu.VMEM((T, D), BF16),
        u_s=pltpu.VMEM((T, D), BF16),
        score_s=pltpu.VMEM((T, T), F32),
    )
    return call(kernel, ins, outs, scratch, "layer_forward")


def touch_kernel(*refs):
    refs[-1][...] = jnp.zeros(TOKEN, F32)


def touch(*values):
    return pl.pallas_call(
        touch_kernel,
        in_specs=[ANY] * len(values),
        out_specs=VMEM,
        out_shape=shape_of(TOKEN, F32),
        compiler_params=pltpu.CompilerParams(vmem_limit_bytes=SMALL_LIMIT),
        cost_estimate=COST,
        name="touch",
    )(*values)


def scale_of(sq0_ref, sq1_ref):
    squares = jnp.sum(sq0_ref[...] + sq1_ref[...], axis=1, keepdims=True)
    return lax.rsqrt(squares / DI + EPS)


def join_rows(mine, others):
    halves = [a[...].astype(F32) + b[...].astype(F32) for a, b in zip(mine, others)]
    return jnp.concatenate(halves, axis=0)


def join(flag, core, keep, dep, first):
    def second(R):
        gather_rows(R, "u", R.res)
        for k, (own, other) in enumerate(((R.p0, R.o0), (R.p1, R.o1))):

            def strip(at):
                here, span = pl.ds(at, STRIP), pl.ds(pl.multiple_of(k * HALF + at, STRIP), STRIP)
                squares = jnp.sum(R.sq0[span, :] + R.sq1[span, :], axis=1, keepdims=True)
                scale = lax.rsqrt(squares / DI + EPS)
                total = own[here, :].astype(F32) + other[here, :].astype(F32)
                R.res[span, :] = R.res[span, :] + scale * total

            strips(HALF, strip)

    def body(R):
        if not first:
            return second(R)
        scale = scale_of(R.sq0, R.sq1)
        total = join_rows((R.p0, R.p1), (R.o0, R.o1))
        gather_rows(R, "u", R.res)
        res = R.res[...] + scale * total
        R.res[...] = res.astype(BF16).astype(F32)
        R.low[...] = R.res[half_rows(R.core[0]), :].astype(BF16)
        R.total[...] = total.astype(BF16)
        R.scale[...] = jnp.broadcast_to(scale, (T, LANES))

    def kernel(R):
        R.token[...] = jnp.zeros(TOKEN, F32)
        pl.when(ours(R, 0 if first else 1))(lambda: body(R))

    ins = rows_operands(keep.u, "u") | dict(
        flag=(flag, SMEM),
        core=(core, SMEM),
        p0=(keep.part[0], VMEM),
        p1=(keep.part[1], VMEM),
        o0=(keep.other[0], VMEM),
        o1=(keep.other[1], VMEM),
        sq0=(keep.sq, VMEM),
        sq1=(keep.other_sq, VMEM),
        dep=order(dep),
    )
    outs = dict(res=(far((T, D), F32), full((T, D))), token=(far(TOKEN, F32), full(TOKEN)))
    if first:
        outs |= dict(
            low=(shape_of((HALF, D), BF16), VMEM),
            total=(far((T, D), BF16), full((T, D))),
            scale=(far((T, LANES), F32), full((T, LANES))),
        )
    return call(kernel, ins, outs, {}, "join_output", grid=(1,), limit=SMALL_LIMIT)


def gate_begin(R):
    gather_rows(R, "e", R.e_s)
    e = R.e_s[...].astype(F32)
    if hasattr(R, "total"):
        scale = R.scale[:, 0:1]
        total = R.total[...].astype(F32)
    else:
        scale = scale_of(R.sq0, R.sq1)
        total = join_rows((R.p0, R.p1), (R.o0, R.o1))
    inner = jnp.sum(e * total, axis=1, keepdims=True)
    R.scale_s[...] = jnp.broadcast_to(scale, (T, LANES))
    R.inner_s[...] = jnp.broadcast_to(inner * (scale * scale * scale) / DI, (T, LANES))
    R.et[...] = R.e_s[...].T


def gate_block(R):
    scale = wide(R.scale_s[...])
    z = R.z[...].astype(F32)
    y = R.y[...]
    gg = R.gate[...]
    dn = dot_nt(R.e_s[...], R.out[...])
    sig = sigmoid(z)
    act = z * sig
    g = y * act
    normed = g * scale
    R.n[...] = (normed * gg).astype(BF16)
    dg = scale * (gg * dn) - g * wide(R.inner_s[...])
    R.dz[...] = (dg * y * (sig * (1.0 + z * (1.0 - sig)))).astype(BF16)
    return y, (dg * act).astype(BF16), jnp.sum(normed * dn, axis=0, keepdims=True)


def scan_begin(micro, R):
    keeps = keep_masks(R.lens, micro)
    for k in range(3):
        R.keep_s[k] = keeps[k]
    hp = spread_heads(R.hp, R.hp_s)
    spread_steps(softplus(R.dtr[...] + hp[0:1, :]), R.cums[...], R.dt_s, R.cum_s, R.cumt_s)
    for ref in (R.acc_s, R.dscore_s, R.dcum_s, R.ddt_s, R.dskip_s):
        ref[...] = jnp.zeros_like(ref)


def scan_block(R, step, y, dyb, ggrad):
    keeps = [wide(R.keep_s[k]) for k in range(3)]
    taps = rows_of(R.cx, 4)
    x = R.x[...].astype(F32)
    total = conv(x, taps, R.bx[...], keeps)
    sig = sigmoid(total)
    xc = total * sig
    cums = R.cum_s[step]
    cumt = R.cumt_s[step]
    dtb = per_channel(R.dt_s[step])
    xt = R.xt[...]
    skip = skip_row(R.hp_s, step)
    inside = y - skip * xc
    top = jnp.zeros((HALF, W), F32)
    bottom = jnp.zeros((HALF, W), F32)
    for k in range(PER):
        my_dy = head_lanes(dyb, k)
        my_x = head_lanes(xt, k)
        col = cums[:, k : k + 1]
        row = cumt[k : k + 1, :]
        decay = jnp.exp(jnp.minimum(row - col[:HALF], 0.0))
        mix = R.scoret[0:HALF, :] * decay
        top = top + dot(mix.astype(BF16), my_dy)
        R.dscore_s[0:HALF, :] += dot_nt(my_x[:HALF], dyb) * decay
        decay = jnp.exp(jnp.minimum(row[:, HALF:] - col[HALF:], 0.0))
        mix = R.scoret[HALF:T, HALF:T] * decay
        bottom = bottom + dot(mix.astype(BF16), my_dy[HALF:])
        R.dscore_s[HALF:T, HALF:T] += dot_nt(my_x[HALF:], dyb[HALF:]) * decay
    dxt = jnp.concatenate([top, bottom], axis=0)
    chan = (lax.broadcasted_iota(jnp.int32, (W, LANES), 0) >> 6) + PER * step
    lane = lax.broadcasted_iota(jnp.int32, (W, LANES), 1)
    group = (chan == lane).astype(F32)
    dy = dyb.astype(F32)
    dxc = dtb * dxt + skip * dy
    dskip = jnp.broadcast_to(jnp.sum(dy * xc, axis=0, keepdims=True), (16, W))
    sums = group_sums([dy * inside - xt.astype(F32) * dxt, xc * dxt, dskip], group)
    R.dcum_s[...] += sums[0]
    R.ddt_s[...] += sums[1]
    R.dskip_s[...] += sums[2][:8]
    dtotal = dxc * (sig * (1.0 + total * (1.0 - sig)))
    dx, grads, dbias = conv_back(dtotal, x, taps, keeps)
    here = pl.ds(pl.multiple_of(step * W, W), W)
    for k, value in enumerate(grads + [dbias, ggrad]):
        R.pack[k : k + 1, here] = value
    low = dx.astype(BF16)
    R.dx[...] = low
    R.acc_s[...] += dot_nt(R.dz[...], R.zx[0]) + dot_nt(low, R.zx[1])


def scan_end(micro, R):
    keeps = [wide(R.keep_s[k], 2 * NS) for k in range(3)]
    bcr = R.bcr[...]
    taps = rows_of(R.cbc, 4)
    total = conv(bcr, taps, R.bbc[...], keeps)
    sig = sigmoid(total)
    act = total * sig
    dscore = R.dscore_s[...] * tri_mask(R.lens, micro, True)
    db = dot(dscore.astype(BF16), act[:, NS:].astype(BF16))
    dc = dot(dscore.T.astype(BF16), act[:, :NS].astype(BF16))
    dact = jnp.concatenate([db, dc], axis=1)
    dtotal = dact * (sig * (1.0 + total * (1.0 - sig)))
    dbc, grads, dbias = conv_back(dtotal, bcr, taps, keeps)
    for k, value in enumerate(grads + [dbias]):
        R.pack[7:8, 2 * NS * k : 2 * NS * (k + 1)] = value
    hp = R.hp_s[STEPS]
    pre = R.dtr[...] + hp[0:1, :]
    decay_rate = -jnp.exp(hp[1:2, :])
    dt = softplus(pre)
    drates = dot_exact(lower_ones(True), R.dcum_s[...])
    heads = R.hp.shape[2]
    lane = lax.broadcasted_iota(jnp.int32, (T, LANES), 1)
    ddt = (R.ddt_s[...] + drates * decay_rate) * sigmoid(pre)
    ddt = jnp.where(lane < heads, ddt, 0.0)
    shift = jnp.sum(ddt, axis=0, keepdims=True)
    decay = jnp.sum(drates * dt, axis=0, keepdims=True) * decay_rate
    decay = jnp.where(lane[0:1] < heads, decay, 0.0)
    both = jnp.concatenate([shift, decay, R.dskip_s[2:8, :]], axis=0)
    tile = both[0:1] + pltpu.roll(both, 32, 1)[1:2] + pltpu.roll(both, 64, 1)[2:3]
    R.pack[7:8, 10 * NS : 11 * NS] = tile
    R.pack[7:8, 11 * NS :] = jnp.zeros((1, NS), F32)
    low_bc = dbc.astype(BF16)
    low_dt = ddt.astype(BF16)
    R.bcdt[:, : 2 * NS] = low_bc
    R.bcdt[:, 2 * NS :] = low_dt
    out = R.acc_s[...] + dot_nt(low_bc, R.bc[...]) + dot(low_dt, R.dt[...])
    R.acc_s[...] = out
    R.mine[...] = R.acc_s[half_rows(R.core[0]), :].astype(BF16)
    R.theirs[...] = R.acc_s[half_rows(1 - R.core[0]), :].astype(BF16)
    gather_rows(R, "u", R.u_s)
    u = R.u_s[...].astype(F32)
    s_zero = lax.rsqrt(jnp.mean(u * u, axis=1, keepdims=True) + EPS)
    R.pack[6:7, :] = jnp.sum(u * s_zero * out, axis=0, keepdims=True)
    R.token[...] = jnp.zeros(TOKEN, F32)


def gate_operands(e, keep, wts):
    ins = rows_operands(e) | dict(
        z=(from_far(keep.z), cols(T)),
        y=(from_far(keep.y), cols(T)),
        gate=(from_far(wts.gate), cols(1)),
        out=(from_far(wts.out), pl.BlockSpec((W, D), lambda i: (i, 0))),
    )
    if hasattr(keep, "total"):
        return ins | dict(
            total=(from_far(keep.total), full((T, D))), scale=(from_far(keep.scale), full((T, LANES)))
        )
    part, other = keep.part, keep.other
    ins |= dict(
        p0=(part[0], full((HALF, D))),
        p1=(part[1], full((HALF, D))),
        o0=(other[0], full((HALF, D))),
        o1=(other[1], full((HALF, D))),
        sq0=(keep.sq, full((T, LANES))),
        sq1=(keep.other_sq, full((T, LANES))),
    )
    return ins


def gate_results():
    return dict(
        et=(far((D, T), BF16), full((D, T))),
        n=(far((T, C), BF16), cols(T)),
        dz=(far((T, C), BF16), cols(T)),
    )


GATE_SCRATCH = dict(
    e_s=pltpu.VMEM((T, D), BF16), scale_s=pltpu.VMEM((T, LANES), F32), inner_s=pltpu.VMEM((T, LANES), F32))


def scan_operands(lens, core, keep, wts):
    return rows_operands(keep.u, "u") | dict(
        lens=(lens, SMEM),
        core=(core, SMEM),
        x=(from_far(keep.x), cols(T)),
        xt=(from_far(keep.xt), cols(T)),
        bcr=(from_far(keep.bcr), full((T, 2 * NS))),
        dtr=(from_far(keep.dtr), full((T, LANES))),
        scoret=(from_far(keep.scoret), full((T, T))),
        cums=(from_far(keep.cums), full((T, LANES))),
        zx=(from_far(wts.zx), pl.BlockSpec((2, D, W), lambda i: (0, 0, i))),
        **small_operands(wts),
    )


def scan_results():
    return dict(
        dx=(far((T, C), BF16), cols(T)),
        bcdt=(far((T, 3 * LANES), BF16), full((T, 3 * LANES))),
        mine=(shape_of((HALF, D), BF16), full((HALF, D))),
        theirs=(shape_of((HALF, D), BF16), full((HALF, D))),
        pack=(far((PACK, C), F32), full((PACK, C))),
        token=(far(TOKEN, F32), full(TOKEN)),
    )


def back_scratch():
    return scan_scratch() | dict(
        dscore_s=pltpu.VMEM((T, T), F32),
        dcum_s=pltpu.VMEM((T, LANES), F32),
        ddt_s=pltpu.VMEM((T, LANES), F32),
        dskip_s=pltpu.VMEM((8, LANES), F32),
        u_s=pltpu.VMEM((T, D), BF16),
    )


def gate_back(flag, core, e, keep, wts, dep):
    def body(R):
        pl.when(pl.program_id(0) == 0)(lambda: gate_begin(R))
        _, R.dy[...], R.ggrad[...] = gate_block(R)

    ins = gate_operands(e, keep, wts) | dict(flag=(flag, SMEM), core=(core, SMEM), dep=order(dep))
    outs = gate_results() | dict(dy=(far((T, C), BF16), cols(T)), ggrad=(far((1, C), F32), cols(1)))
    return call(
        lambda R: pl.when(ours(R, 0))(lambda: body(R)), ins, outs, GATE_SCRATCH, "gate_backward"
    )


def no_rows(R):
    for ref in (R.mine, R.theirs, R.token):
        ref[...] = jnp.zeros_like(ref)


def scan_back(micro, flag, lens, core, keep, wts, dep):
    def body(R):
        step = pl.program_id(0)
        pl.when(step == 0)(lambda: scan_begin(micro, R))
        scan_block(R, step, R.y[...], R.dy[...], R.ggrad[...])
        pl.when(step == STEPS - 1)(lambda: scan_end(micro, R))

    def kernel(R):
        pl.when(R.flag[0] != 0)(lambda: no_rows(R))
        pl.when(ours(R, 0))(lambda: body(R))

    ins = scan_operands(lens, core, keep, wts) | dict(
        flag=(flag, SMEM),
        y=(from_far(keep.y), cols(T)),
        dy=(from_far(keep.dy), cols(T)),
        dz=(from_far(keep.dz), cols(T)),
        ggrad=(from_far(keep.ggrad), cols(1)),
        dep=order(dep),
    )
    return call(kernel, ins, scan_results(), back_scratch(), "scan_backward")


def layer_back(micro, role, flag, lens, core, e, keep, wts, dep):
    def body(R):
        step = pl.program_id(0)

        @pl.when(step == 0)
        def _():
            gate_begin(R)
            scan_begin(micro, R)

        scan_block(R, step, *gate_block(R))
        pl.when(step == STEPS - 1)(lambda: scan_end(micro, R))

    def kernel(R):
        pl.when(R.flag[0] != role)(lambda: no_rows(R))
        pl.when(ours(R, role))(lambda: body(R))

    ins = dict(flag=(flag, SMEM), **gate_operands(e, keep, wts), **scan_operands(lens, core, keep, wts))
    return call(
        kernel,
        ins | dict(dep=order(dep)),
        gate_results() | scan_results(),
        back_scratch() | GATE_SCRATCH,
        "layer_backward",
    )


def input_rows(R, e, u, dr):
    s_zero = lax.rsqrt(jnp.mean(u * u, axis=1, keepdims=True) + EPS)
    gained = R.norm[...] * dr
    shared = s_zero * s_zero * s_zero * jnp.mean(u * gained, axis=1, keepdims=True)
    return e + s_zero * gained - u * shared


def input_send(core, keep, wts):
    def kernel(R):
        dr = R.mine[...].astype(F32) + R.came[...].astype(F32)
        R.low[...] = input_rows(R, part_rows(R, "e", 0), part_rows(R, "u", 0), dr).astype(BF16)
        R.token[...] = jnp.zeros(TOKEN, F32)

    ins = rows_operands(keep.e) | rows_operands(keep.u, "u") | dict(
        core=(core, SMEM),
        norm=(from_far(wts.norm), full((1, D))),
        mine=(keep.mine, VMEM),
        came=(keep.came, VMEM),
    )
    outs = dict(low=(shape_of((HALF, D), BF16), VMEM), token=(far(TOKEN, F32), full(TOKEN)))
    return call(kernel, ins, outs, {}, "input_send", grid=(1,), limit=SMALL_LIMIT)


def input_back(core, keep, wts, dep):
    def kernel(R):
        for k, (own, other) in enumerate(((R.mine, R.came), (R.theirs, R.left))):

            def strip(at):
                span = pl.ds(at, STRIP)
                dr = own[span, :].astype(F32) + other[span, :].astype(F32)
                e, u = part_rows(R, "e", k, at, STRIP), part_rows(R, "u", k, at, STRIP)
                first = (1 - R.core[0] if k else R.core[0]) * HALF + at
                R.du[pl.ds(pl.multiple_of(first, STRIP), STRIP), :] = input_rows(R, e, u, dr)

            strips(HALF, strip)
        R.token[...] = jnp.zeros(TOKEN, F32)

    ins = rows_operands(keep.e) | rows_operands(keep.u, "u") | dict(
        core=(core, SMEM),
        norm=(from_far(wts.norm), full((1, D))),
        mine=(keep.mine, full((HALF, D))),
        came=(keep.came, full((HALF, D))),
        theirs=(keep.theirs, full((HALF, D))),
        left=(keep.left, full((HALF, D))),
        dep=order(dep),
    )
    outs = dict(du=(far((T, D), F32), full((T, D))), token=(far(TOKEN, F32), full(TOKEN)))
    return call(kernel, ins, outs, {}, "input_backward", grid=(1,), limit=SMALL_LIMIT)


def hold(value, dep):
    def kernel(R):
        R.out[...] = R.value[...]

    ins = dict(value=(value, VMEM), dep=order(dep))
    outs = dict(out=(shape_of(value.shape, value.dtype), VMEM))
    return call(kernel, ins, outs, {}, "hold", grid=(1,), limit=SMALL_LIMIT)["out"]


def swap(value):
    return lax.ppermute(value, "tensor", [(0, 1), (1, 0)])


def relay_up(value):
    return lax.ppermute(value, "pipe", [(0, 1)])


def relay_down(value):
    return lax.ppermute(value, "pipe", [(1, 0)])


def partners():
    def make(fn):
        return [fn(i // 8, (i // 2) % 4, i % 2) for i in range(32)]

    def pack(y, x, z):
        return y * 8 + x * 2 + z

    def wrap(v):
        return (v + 1) % 4 if v % 2 else (v - 1) % 4

    return [
        make(lambda y, x, z: pack(y, x ^ 1, z)),
        make(lambda y, x, z: pack(y ^ 1, x, z)),
        make(lambda y, x, z: pack(y, wrap(x), z)),
        make(lambda y, x, z: pack(wrap(y), x, z)),
        make(lambda y, x, z: pack(y, x, z ^ 1)),
    ]


STREAMS = 5


LAST = ((0, 4), (0, 1), (2, 1), (2, 3), (3, 4))


def dims_of(stream, late):
    if late:
        return [(stream + k) % 5 for k in range(1, 4)] + list(LAST[stream])
    return [(stream + k) % 5 for k in range(5)]


def ends_first(s):
    return dims_of(s, 0)[4] == LAST[s][0]


def round_groups(which):
    dims = sorted({last[which] for last in LAST})
    return [(d, [s for s in range(5) if LAST[s][which] == d]) for d in dims]


def block_order(maps, stream, late=0):
    order = [maps[d] for d in dims_of(stream, late)]
    count = len(order[0])
    table = np.zeros((count, count), np.int32)
    for me in range(count):
        for p in range(count):
            owner = me
            for k, step in enumerate(order):
                if (p >> (len(order) - 1 - k)) & 1:
                    owner = step[owner]
            table[me, p] = owner
    return table


TILES_EARLY = [("et", "n", LANES * k) for k in range(C // LANES)] + [
    ("rt", "dz", LANES * k) for k in range(C // LANES)
]
TILES_LATE = [("rt", "dx", LANES * k) for k in range(C // LANES)] + [
    ("rt", "bcdt", LANES * k) for k in range(3)
]


def deal(tiles):
    width = -(-len(tiles) // STREAMS)
    return [tiles[width * s : width * (s + 1)] for s in range(STREAMS)]


EARLY, LATE = deal(TILES_EARLY), deal(TILES_LATE)
PACK = 8
PACK_ROWS = 2 * PACK * (C // LANES)
PACK_STREAM = STREAMS - 1


def runs(tiles):
    out = []
    for at, (left, right, first) in enumerate(tiles):
        if out and out[-1][:2] == [left, right] and out[-1][2] + LANES * out[-1][3] == first:
            out[-1][3] += 1
        else:
            out.append([left, right, first, 1, at])
    return out


class Loader:
    def __init__(self, flag_ref, names, sources, held, sem):
        self.flag, self.names, self.sources, self.held, self.sem = flag_ref, names, sources, held, sem
        self.waited = set()

    def copy(self, k, m, early):
        span = pl.ds(m * T, T)
        ref = self.held[k]
        slot = ref.at[:, span] if ref.shape[0] == D else ref.at[span, :]
        return pltpu.make_async_copy(self.sources[4 * k + 2 * early + m], slot, self.sem.at[2 * k + m])

    def start(self, name):
        k = self.names.index(name)
        for m in range(2):
            pl.when(self.flag[0] == 1)(lambda: self.copy(k, m, 0).start())
            pl.when(self.flag[0] == 0)(lambda: self.copy(k, m, 1).start())

    def get(self, name):
        k = self.names.index(name)
        if name not in self.waited:
            self.waited.add(name)
            for m in range(2):
                self.copy(k, m, 0).wait()
        return self.held[k]


def held_shapes(arrays):
    shapes = []
    for a in arrays:
        rows, columns = a[0].shape
        shapes.append(pltpu.VMEM((rows, 2 * columns) if rows == D else (2 * rows, columns), BF16))
    return shapes


def products(loader, lefts, tiles, blocks, owner_of, place):
    rows, half, chunk = D // blocks, D // 2, 384
    placed = []
    for left, right, first, count, at in runs(tiles):
        held, rhs = loader.get(left), loader.get(right)
        if left not in placed:
            placed.append(left)
            for p in range(blocks):
                start = pl.multiple_of(owner_of(p) * rows, 16)
                lefts[len(placed) - 1, p * rows : (p + 1) * rows, :] = held[pl.ds(start, rows), :]
        slot = placed.index(left)
        for side in range(2):
            for row in range(0, half, chunk):
                span = slice(side * half + row, side * half + row + chunk)
                value = dot(lefts[slot, span, :], rhs[:, first : first + LANES * count]).astype(BF16)
                for j in range(count):
                    place(side, at + j, row, value[:, j * LANES : (j + 1) * LANES])


def early_kernel(blocks, flag_ref, table_ref, *refs):
    names = ["et", "n", "rt", "dz"]
    sources, refs = refs[:16], refs[16:]
    outs, token_ref = refs[: 2 * STREAMS], refs[2 * STREAMS]
    held, lefts, in_sem = refs[2 * STREAMS + 1 :]
    loader = Loader(flag_ref, names, sources, held, in_sem)
    for name in names:
        loader.start(name)
    for s in range(STREAMS):

        def place(side, tile, row, value):
            outs[2 * s + side][tile, row : row + value.shape[0], :] = value

        def owner_of(p):
            return table_ref[flag_ref[1] + s * blocks + p]

        products(loader, lefts, EARLY[s], blocks, owner_of, place)
    token_ref[...] = jnp.zeros(TOKEN, F32)


def early_grads(flag, table, arrays, blocks):
    out = []
    for s in range(STREAMS):
        out += [near((len(EARLY[s]), D // 2, LANES), BF16)] * 2
    flat = pl.pallas_call(
        functools.partial(early_kernel, blocks),
        in_specs=[SMEM, SMEM] + [HBM] * 16,
        out_specs=[VMEM] * (len(out) + 1),
        out_shape=tuple(out) + (shape_of(TOKEN, F32),),
        scratch_shapes=[
            held_shapes(arrays),
            pltpu.VMEM((2, D, 2 * T), BF16),
            pltpu.SemaphoreType.DMA((8,)),
        ],
        compiler_params=pltpu.CompilerParams(vmem_limit_bytes=VMEM_LIMIT),
        cost_estimate=COST,
        name="grad_early",
    )(flag, table, *[from_far(v) for a in arrays for v in a])
    return list(flat[0:-1:2]), list(flat[1:-1:2]), flat[-1]


def total_rows(s, early, late):
    return len(EARLY[s]) * early + len(LATE[s]) * late + (PACK_ROWS if s == PACK_STREAM else 0)


def split_pair(value):
    high = value.astype(BF16)
    return jnp.concatenate([high, (value - high.astype(F32)).astype(BF16)], axis=0)


def join_pair(pair):
    wide_pair = pair.astype(F32)
    return wide_pair[:PACK] + wide_pair[PACK:]


def late_kernel(blocks, flag_ref, table_ref, *refs):
    names = ["rt", "dx", "bcdt"]
    sources, refs = refs[:12], refs[12:]
    packs, refs = refs[:4], refs[4:]
    keeps, gots, refs = refs[:STREAMS], refs[STREAMS : 2 * STREAMS], refs[2 * STREAMS :]
    outs, token_ref = refs[: 2 * STREAMS], refs[2 * STREAMS]
    held, lefts, in_sem = refs[2 * STREAMS + 1 :]
    loader = Loader(flag_ref, names, sources, held, in_sem)
    for name in names:
        loader.start(name)
    half = D // 2
    quarter = half // 2
    for s in range(STREAMS):
        for j in range(len(EARLY[s])):
            for side in range(2):
                span = slice(side * quarter, (side + 1) * quarter)
                total = keeps[s][j, span, :].astype(F32) + gots[s][j, span, :].astype(F32)
                outs[2 * s + side][j * quarter : (j + 1) * quarter, :] = total.astype(BF16)
    last = flag_ref[0] == 1
    total = jnp.where(last, packs[0][...] + packs[1][...], packs[2][...] + packs[3][...])
    for j in range(C // LANES):
        pair = split_pair(total[:, j * LANES : (j + 1) * LANES])
        at = total_rows(PACK_STREAM, quarter, half) - PACK_ROWS + 2 * PACK * j
        for side in range(2):
            outs[2 * PACK_STREAM + side][at : at + 2 * PACK, :] = pair
    for s in range(STREAMS):
        base = len(EARLY[s]) * quarter

        def place(side, tile, row, value):
            at = base + tile * half + row
            outs[2 * s + side][at : at + value.shape[0], :] = value

        def owner_of(p):
            return table_ref[flag_ref[1] + s * blocks + p]

        products(loader, lefts, LATE[s], blocks, owner_of, place)
    token_ref[...] = jnp.zeros(TOKEN, F32)


def late_grads(flag, table, arrays, blocks, packs, keeps, gots):
    out = []
    for s in range(STREAMS):
        out += [near((total_rows(s, D // 4, D // 2), LANES), BF16)] * 2
    flat = pl.pallas_call(
        functools.partial(late_kernel, blocks),
        in_specs=[SMEM, SMEM] + [HBM] * 12 + [VMEM] * (4 + 2 * STREAMS),
        out_specs=[VMEM] * (len(out) + 1),
        out_shape=tuple(out) + (shape_of(TOKEN, F32),),
        scratch_shapes=[
            held_shapes(arrays),
            pltpu.VMEM((1, D, 2 * T), BF16),
            pltpu.SemaphoreType.DMA((6,)),
        ],
        compiler_params=pltpu.CompilerParams(vmem_limit_bytes=VMEM_LIMIT),
        cost_estimate=COST,
        name="grad_late",
    )(
        flag,
        table,
        *[from_far(v) for a in arrays for v in a],
        *packs,
        *keeps,
        *gots,
    )
    return list(flat[0:-1:2]), list(flat[1:-1:2]), flat[-1]


def fold(s, keep, got, early, late, deps):
    def kernel(keep, got, *refs):
        next_keep, next_send, token = refs[len(deps) :]
        at = to = 0
        for rows, tiles in ((early, EARLY[s]), (late, LATE[s])):
            for _ in tiles:
                next_send[to : to + rows // 2, :] = add(keep, got, at + rows // 2, rows // 2).astype(BF16)
                next_keep[to : to + rows // 2, :] = add(keep, got, at, rows // 2).astype(BF16)
                at += rows
                to += rows // 2
        if s == PACK_STREAM:
            add_packs((keep, at), (got, at), ((next_keep, to), (next_send, to)))
        token[...] = jnp.zeros(TOKEN, F32)

    rows = total_rows(s, early // 2, late // 2)
    out = [near((rows, LANES), BF16), near((rows, LANES), BF16), near(TOKEN, F32)]
    return pl.pallas_call(
        kernel,
        in_specs=[VMEM] * 2 + [ANY] * len(deps),
        out_specs=[VMEM, VMEM, VMEM],
        out_shape=tuple(out),
        compiler_params=pltpu.CompilerParams(vmem_limit_bytes=SMALL_LIMIT),
        cost_estimate=COST,
        name="fold_grads",
    )(keep, got, *deps)


def add(keep, got, at, rows, got_at=None):
    got_at = at if got_at is None else got_at
    return keep[at : at + rows, :].astype(F32) + got[got_at : got_at + rows, :].astype(F32)


def pack_sum(keep, keep_at, got, got_at, j):
    a = keep[keep_at + 2 * PACK * j : keep_at + 2 * PACK * (j + 1), :]
    b = got[got_at + 2 * PACK * j : got_at + 2 * PACK * (j + 1), :]
    return join_pair(a) + join_pair(b)


def add_packs(keep, got, targets):
    for j in range(C // LANES):
        pair = split_pair(pack_sum(*keep, *got, j))
        for ref, at in targets:
            ref[at + 2 * PACK * j : at + 2 * PACK * (j + 1), :] = pair


BLOCK = 48


def payload(s, which):
    early = BLOCK if ends_first(s) != bool(which) else 0
    late = BLOCK if which else 2 * BLOCK
    return len(EARLY[s]) * early, len(LATE[s]) * late, PACK_ROWS if s == PACK_STREAM else 0


def places(which):
    where, sizes = {}, []
    for g, (_, streams) in enumerate(round_groups(which)):
        at = 0
        for s in streams:
            where[s] = (g, at)
            at += sum(payload(s, which))
        sizes.append(at)
    return where, sizes


def keep_rows(s):
    early = len(EARLY[s]) * BLOCK
    return early if ends_first(s) else 2 * early, len(LATE[s]) * 2 * BLOCK, payload(s, 0)[2]


def third_kernel(*refs):
    keeps, gots = refs[:STREAMS], refs[STREAMS : 2 * STREAMS]
    next_keeps, sends = refs[2 * STREAMS : 3 * STREAMS], refs[3 * STREAMS :]
    where, _ = places(0)
    for s in range(STREAMS):
        keep, got, out = keeps[s], gots[s], next_keeps[s]
        group, to = where[s]
        target = sends[group]
        early = len(EARLY[s]) * BLOCK
        at = 0
        for j in range(len(EARLY[s])):
            out[j * BLOCK : (j + 1) * BLOCK, :] = add(keep, got, at, BLOCK).astype(BF16)
            value = add(keep, got, at + BLOCK, BLOCK).astype(BF16)
            if ends_first(s):
                target[to + j * BLOCK : to + (j + 1) * BLOCK, :] = value
            else:
                out[early + j * BLOCK : early + (j + 1) * BLOCK, :] = value
            at += 2 * BLOCK
        base, to = keep_rows(s)[0], to + payload(s, 0)[0]
        half = 2 * BLOCK
        for j in range(len(LATE[s])):
            out[base + j * half : base + (j + 1) * half, :] = add(keep, got, at, half).astype(BF16)
            target[to + j * half : to + (j + 1) * half, :] = add(keep, got, at + half, half).astype(BF16)
            at += 2 * half
        if s == PACK_STREAM:
            spots = ((out, base + len(LATE[s]) * half), (target, to + len(LATE[s]) * half))
            add_packs((keep, at), (got, at), spots)


def fourth_kernel(*refs):
    groups = len(round_groups(0))
    keeps, gots = refs[:STREAMS], refs[STREAMS : STREAMS + groups]
    refs = refs[STREAMS + groups :]
    dones, next_keeps, sends = refs[:STREAMS], refs[STREAMS : 2 * STREAMS], refs[2 * STREAMS :]
    came, _ = places(0)
    where, _ = places(1)
    for s in range(STREAMS):
        keep, got, out = keeps[s], gots[came[s][0]], next_keeps[s]
        target, to = sends[where[s][0]], where[s][1]
        at = came[s][1]
        early = len(EARLY[s]) * BLOCK
        if ends_first(s):
            dones[s][...] = add(keep, got, 0, early, at)
        else:
            dones[s][...] = keep[:early, :].astype(F32)
            target[to : to + early, :] = keep[early : 2 * early, :]
        at, to, base = at + payload(s, 0)[0], to + payload(s, 1)[0], keep_rows(s)[0]
        for j in range(len(LATE[s])):
            first = base + 2 * BLOCK * j
            out[j * BLOCK : (j + 1) * BLOCK, :] = add(keep, got, first, BLOCK, at).astype(BF16)
            value = add(keep, got, first + BLOCK, BLOCK, at + BLOCK).astype(BF16)
            target[to + j * BLOCK : to + (j + 1) * BLOCK, :] = value
            at += 2 * BLOCK
        if s == PACK_STREAM:
            late = len(LATE[s]) * BLOCK
            add_packs((keep, base + 2 * late), (got, at), ((out, late), (target, to + late)))


def last_folds(kernel, operands, shapes, name):
    return pl.pallas_call(
        kernel,
        in_specs=[VMEM] * len(operands),
        out_specs=[VMEM] * len(shapes),
        out_shape=tuple(near((rows, LANES), dtype) for rows, dtype in shapes),
        compiler_params=pltpu.CompilerParams(vmem_limit_bytes=SMALL_LIMIT),
        cost_estimate=COST,
        name=name,
    )(*operands)


def fold_third(keeps, gots):
    shapes = [(sum(keep_rows(s)), BF16) for s in range(STREAMS)]
    shapes += [(rows, BF16) for rows in places(0)[1]]
    flat = last_folds(third_kernel, [*keeps, *gots], shapes, "fold_third")
    return flat[:STREAMS], flat[STREAMS:]


def fold_fourth(keeps, gots):
    shapes = [(len(EARLY[s]) * BLOCK, F32) for s in range(STREAMS)]
    shapes += [(sum(payload(s, 1)[1:]), BF16) for s in range(STREAMS)]
    shapes += [(rows, BF16) for rows in places(1)[1]]
    flat = last_folds(fourth_kernel, [*keeps, *gots], shapes, "fold_fourth")
    return flat[:STREAMS], flat[STREAMS : 2 * STREAMS], flat[2 * STREAMS :]


def end_kernel(rows, heads, core_ref, *refs):
    groups = len(round_groups(1))
    dones, keeps, gots = refs[:STREAMS], refs[STREAMS : 2 * STREAMS], refs[2 * STREAMS :][:groups]
    refs = refs[2 * STREAMS + groups :]
    out_ref, zx_ref, dt_ref, cx_ref, bx_ref, gate_ref, heads_ref = refs[:7]
    mine_ref, theirs_ref, shared_ref, bcdt_s = refs[7:]
    came, _ = places(1)

    def place(right, first, value):
        if right == "n":
            out_ref[:, first : first + LANES] = value
        elif right == "bcdt":
            bcdt_s[:, first : first + LANES] = value
        else:
            zx_ref[:, 0 if right == "dz" else 1, first : first + LANES] = value

    for s in range(STREAMS):
        got, at = gots[came[s][0]], came[s][1]
        for j, (_, right, first) in enumerate(EARLY[s]):
            value = dones[s][j * rows : (j + 1) * rows, :]
            if not ends_first(s):
                value = value + got[at : at + rows, :].astype(F32)
                at += rows
            place(right, first, value)
        for j, (_, right, first) in enumerate(LATE[s]):
            place(right, first, add(keeps[s], got, j * rows, rows, at))
            at += rows
        if s == PACK_STREAM:
            keep, keep_at = keeps[s], len(LATE[s]) * rows
            for j in range(C // LANES):
                lanes = slice(j * LANES, (j + 1) * LANES)
                value = pack_sum(keep, keep_at, got, at, j)
                cx_ref[:, lanes] = value[0:4]
                bx_ref[:, lanes] = value[4:5]
                gate_ref[:, lanes] = value[5:6]
                shared_ref[:, lanes] = value[6:8]
                if j == 10:
                    for k in range(3):
                        moved = pltpu.roll(value, (LANES - 32 * k) % LANES, 1) if k else value
                        heads_ref[k : k + 1, :] = moved[7:8, :heads]
    part = rows // 2
    mine_ref[...] = bcdt_s[pl.ds(pl.multiple_of(core_ref[0] * part, 8), part), : 2 * NS]
    theirs_ref[...] = bcdt_s[pl.ds(pl.multiple_of((1 - core_ref[0]) * part, 8), part), : 2 * NS]
    dt_ref[...] = bcdt_s[:, 2 * NS :].T[:heads, :]


def end(core, dones, keeps, gots, rows, heads):
    return pl.pallas_call(
        functools.partial(end_kernel, rows, heads),
        in_specs=[SMEM] + [VMEM] * (2 * STREAMS + len(gots)),
        out_specs=[VMEM] * 10,
        out_shape=(
            shape_of((rows, C), F32),
            shape_of((rows, 2, C), F32),
            shape_of((heads, rows), F32),
            shape_of((4, C), F32),
            shape_of((1, C), F32),
            shape_of((1, C), F32),
            shape_of((3, heads), F32),
            shape_of((rows // 2, 2 * NS), F32),
            shape_of((rows // 2, 2 * NS), F32),
            shape_of((2, C), F32),
        ),
        scratch_shapes=[pltpu.VMEM((rows, 3 * LANES), F32)],
        compiler_params=pltpu.CompilerParams(vmem_limit_bytes=SMALL_LIMIT),
        cost_estimate=COST,
        name="grad_end",
    )(core, *dones, *keeps, *gots)


def last_kernel(mine_ref, other_ref, shared_ref, other_shared_ref, bc_ref, norm_ref, conv_ref, bias_ref):
    bc_ref[...] = mine_ref[...] + other_ref[...]
    total = shared_ref[...] + other_shared_ref[...]
    norm_ref[...] = total[0:1]
    for k in range(4):
        conv_ref[k : k + 1, :] = total[1:2, 2 * NS * k : 2 * NS * (k + 1)]
    bias_ref[...] = total[1:2, 8 * NS : 10 * NS]


def last_sums(mine, other, shared, other_shared):
    return pl.pallas_call(
        last_kernel,
        in_specs=[VMEM] * 4,
        out_specs=[VMEM] * 4,
        out_shape=(
            shape_of(mine.shape, F32),
            shape_of((1, C), F32),
            shape_of((4, 2 * NS), F32),
            shape_of((1, 2 * NS), F32),
        ),
        compiler_params=pltpu.CompilerParams(vmem_limit_bytes=SMALL_LIMIT),
        cost_estimate=COST,
        name="last_sums",
    )(mine, other, shared, other_shared)


def pick_kernel(flag_ref, late0, late1, early0, early1, _, out_ref, token_ref, held, sem):
    for m, (late, early) in enumerate(((late0, early0), (late1, early1))):

        def start(source):
            pltpu.make_async_copy(source, held.at[m], sem.at[m]).start()

        pl.when(flag_ref[0] == 1)(lambda: start(late))
        pl.when(flag_ref[0] == 0)(lambda: start(early))
    for m in range(2):
        pltpu.make_async_copy(early0, held.at[m], sem.at[m]).wait()
        pltpu.make_async_copy(held.at[m], out_ref.at[m], sem.at[2 + m]).start()
    for m in range(2):
        pltpu.make_async_copy(held.at[m], out_ref.at[m], sem.at[2 + m]).wait()
    token_ref[...] = jnp.zeros(TOKEN, F32)


def pick(flag, late, early, dep):
    return pl.pallas_call(
        pick_kernel,
        in_specs=[SMEM] + [HBM] * 4 + [ANY],
        out_specs=[HBM, VMEM],
        out_shape=(far((2, T, D), F32), shape_of(TOKEN, F32)),
        scratch_shapes=[pltpu.VMEM((2, T, D), F32), pltpu.SemaphoreType.DMA((4,))],
        compiler_params=pltpu.CompilerParams(vmem_limit_bytes=SMALL_LIMIT),
        cost_estimate=COST,
        name="pick_section",
    )(flag, *[from_far(v) for v in (*late, *early)], dep)


def send(value, step):
    return lax.ppermute(value, "dp", [(i, to) for i, to in enumerate(step)])


def body(
    tokens,
    cotangent,
    lengths,
    norm_gain,
    w_zx,
    w_bc,
    w_dt,
    conv_x,
    bias_x,
    conv_bc,
    bias_bc,
    head_params,
    gate_gain,
    w_out,
):
    is_last = lax.axis_index("pipe") == 1
    core_at = lax.axis_index("tensor")
    heads = w_dt.shape[2]
    wts = SimpleNamespace(
        norm=norm_gain,
        zx=jnp.transpose(w_zx[0], (1, 0, 2)),
        bc=w_bc[0],
        dt=jnp.pad(w_dt[0].T, ((0, LANES - heads), (0, 0))),
        cx=conv_x[0],
        bx=bias_x,
        cbc=conv_bc[0],
        bbc=bias_bc,
        hp=jnp.transpose(head_params, (1, 0, 2)),
        gate=gate_gain,
        out=w_out[0],
    )

    flag = is_last.astype(jnp.int32).reshape(1)
    core = core_at.astype(jnp.int32).reshape(1)

    lens = lengths

    def run(m, role, u, dep):
        keep = SimpleNamespace(**forward(m, role, flag, lens, core, u, wts, dep))
        keep.u = u
        keep.part = (keep.part0, keep.part1)
        keep.other = tuple(swap(v) for v in keep.part)
        keep.other_sq = swap(keep.sq)
        return keep

    def backward(m, role, keep, e, dep):
        keep.e = e
        vars(keep).update(layer_back(m, role, flag, lens, core, e, keep, wts, dep))
        share(keep)

    def share(keep):
        keep.came, keep.left = swap(keep.theirs), swap(keep.mine)

    def send_down(keep):
        result = input_send(core, keep, wts)
        return relay_down(result["low"]), result["token"]

    def finish(keep, dep):
        result = input_back(core, keep, wts, dep)
        keep.du = result["du"]
        return result["token"]

    keep_a = run(0, 0, Rows(tokens, 0), (lens,))
    vars(keep_a).update(join(flag, core, keep_a, (lens,), True))
    sent_a = relay_up(keep_a.low)
    keep_b = run(1, 0, Rows(tokens, 1), keep_a.token)
    vars(keep_b).update(join(flag, core, keep_b, (sent_a,), True))
    sent_b = relay_up(keep_b.low)
    keep_c = run(0, 1, Halves(sent_a, swap(sent_a)), keep_b.token)
    sent_b = hold(sent_b, keep_c.token)
    keep_d = run(1, 1, Halves(sent_b, swap(sent_b)), keep_c.token)
    backward(0, 1, keep_c, Rows(cotangent, 0), keep_d.token)
    sent_c, token = send_down(keep_c)
    backward(1, 1, keep_d, Rows(cotangent, 1), token)
    sent_d, token = send_down(keep_d)
    backward(0, 0, keep_a, Halves(sent_c, swap(sent_c)), token)
    sent_d = hold(sent_d, keep_a.token)
    keep_b.e = Halves(sent_d, swap(sent_d))
    vars(keep_b).update(gate_back(flag, core, keep_b.e, keep_b, wts, (touch(keep_a.came, *[keep.left for keep in (keep_a, keep_c, keep_d)]),)))

    dp = lax.axis_size("dp")
    maps = partners()
    me = lax.axis_index("dp")
    tables = [
        jnp.asarray(np.stack([block_order(maps, s, late) for s in range(STREAMS)], axis=1).reshape(-1))
        for late in range(2)
    ]
    flag = jnp.stack([is_last.astype(jnp.int32), me.astype(jnp.int32) * (STREAMS * dp)])

    def both(name):
        return tuple(getattr(keep, name) for keep in (keep_c, keep_d, keep_a, keep_b))

    arrays = [both(k) for k in ("et", "n", "rt", "dz")]
    keeps, sends, token = early_grads(flag, tables[0], arrays, dp)
    gots = [send(sends[s], maps[dims_of(s, 0)[0]]) for s in range(STREAMS)]
    vars(keep_b).update(scan_back(1, flag, lens, core, keep_b, wts, (token,)))
    share(keep_b)
    arrays = [both(k) for k in ("rt", "dx", "bcdt")]
    keeps, sends, token = late_grads(flag, tables[1], arrays, dp, both("pack"), keeps, gots)
    tokens_in = [finish(keep, (token,)) for keep in (keep_a, keep_b, keep_c, keep_d)]
    join_c = SimpleNamespace(**join(flag, core, keep_c, (token,), False))
    join_d = SimpleNamespace(**join(flag, core, keep_d, (token,), False))
    deps = [[*tokens_in, join_c.token, join_d.token]]
    section_out, token_a = pick(
        flag, (join_c.res, join_d.res), (keep_a.res, keep_b.res), token
    )
    section_grad, token_b = pick(flag, (keep_c.du, keep_d.du), (keep_a.du, keep_b.du), token)
    deps += [[token_a, token_b]]
    early, late = D // 4, D // 2
    gots = [send(sends[s], maps[dims_of(s, 1)[0]]) for s in range(STREAMS)]
    token = None
    for k in range(1, 3):
        for s in range(STREAMS):
            order = [token] if token is not None else []
            if s == 0:
                order += deps[k - 1]
            keeps[s], sends[s], token = fold(s, keeps[s], gots[s], early, late, order)
            gots[s] = send(sends[s], maps[dims_of(s, 1)[k]])
        early, late = early // 2, late // 2
    keeps, sends = fold_third(keeps, gots)
    gots = [send(v, maps[d]) for v, (d, _) in zip(sends, round_groups(0))]
    dones, keeps, sends = fold_fourth(keeps, gots)
    gots = [send(v, maps[d]) for v, (d, _) in zip(sends, round_groups(1))]
    g_out, g_zx, g_dt, g_cx, g_bx, g_gate, g_heads, mine, theirs, shared = end(
        core, dones, keeps, gots, D // dp, heads
    )
    g_bc, g_norm, g_cbc, g_bbc = last_sums(mine, swap(theirs), shared, swap(shared))
    return (
        section_out[None],
        section_grad[None],
        g_norm,
        g_zx[None],
        g_bc[None],
        g_dt.T[None],
        g_cx[None],
        g_bx,
        g_cbc[None],
        g_bbc,
        g_heads[None],
        g_gate,
        g_out.T[None],
    )


def solution(mesh):
    in_specs = (
        P(None, "dp", None),
        P(None, "dp", None),
        P(None, "dp", None),
        P("pipe", None),
        P("pipe", None, None, "tensor"),
        P("pipe", None, None),
        P("pipe", None, "tensor"),
        P("pipe", None, "tensor"),
        P("pipe", "tensor"),
        P("pipe", None, None),
        P("pipe", None),
        P("pipe", None, "tensor"),
        P("pipe", "tensor"),
        P("pipe", "tensor", None),
    )
    out_specs = (
        P("pipe", None, "dp", None),
        P("pipe", None, "dp", None),
        P("pipe", None),
        P("pipe", "dp", None, "tensor"),
        P("pipe", ("dp", "tensor"), None),
        P("pipe", "dp", "tensor"),
        P("pipe", None, "tensor"),
        P("pipe", "tensor"),
        P("pipe", None, None),
        P("pipe", None),
        P("pipe", None, "tensor"),
        P("pipe", "tensor"),
        P("pipe", "tensor", "dp"),
    )
    return jax.shard_map(body, mesh=mesh, in_specs=in_specs, out_specs=out_specs, check_vma=False)
```

```python
import functools
from types import SimpleNamespace

import jax
import jax.numpy as jnp
import numpy as np
from jax import lax
from jax.experimental import pallas as pl
from jax.experimental.pallas import tpu as pltpu
from jax.sharding import PartitionSpec as P

F32 = jnp.float32
BF16 = jnp.bfloat16
EPS = 1e-05
T = 256
D = 1536
C = 1536
W = 256
STEPS = C // W
HEAD = 64
PER = W // HEAD
NS = 128
DI = 3072
LANES = 128
HALF = T // 2
NT = (((1,), (1,)), ((), ()))
VMEM_LIMIT = 24 * 1024 * 1024
SMALL_LIMIT = 16 * 1024 * 1024
COST = pl.CostEstimate(flops=1, bytes_accessed=1, transcendentals=0)


def dot(a, b):
    return jnp.dot(a, b, preferred_element_type=F32)


def dot_nt(a, b):
    return lax.dot_general(a, b, NT, preferred_element_type=F32)


def group_sums(values, group):
    terms = []
    for value in values:
        high = value.astype(BF16)
        terms += [high, (value - high.astype(F32)).astype(BF16)]
    out = dot(jnp.concatenate(terms, axis=0), group.astype(BF16))
    at, sums = 0, []
    for value in values:
        rows = value.shape[0]
        sums.append(out[at : at + rows] + out[at + rows : at + 2 * rows])
        at += 2 * rows
    return sums


def position_sums(ones, value):
    high = value.astype(BF16)
    rest = value - high.astype(F32)
    middle = rest.astype(BF16)
    low = (rest - middle.astype(F32)).astype(BF16)
    out = dot(ones.astype(BF16), jnp.concatenate([high, middle, low], axis=1))
    width = value.shape[1]
    return out[:, :width] + (out[:, width : 2 * width] + out[:, 2 * width :])


def params(steps):
    return pltpu.CompilerParams(
        dimension_semantics=("arbitrary",) * steps, vmem_limit_bytes=VMEM_LIMIT
    )


def sigmoid(v):
    return 1.0 / (1.0 + jnp.exp(-v))


def seg_ids(len_ref, micro, pos):
    end = jnp.int32(0)
    seg = jnp.zeros(pos.shape, jnp.int32)
    for k in range(4):
        end = end + len_ref[micro, 0, k]
        seg = seg + (pos >= end).astype(jnp.int32)
    return seg


def keep_masks(len_ref, micro):
    pos = lax.broadcasted_iota(jnp.int32, (T, LANES), 0)
    seg = seg_ids(len_ref, micro, pos)
    out = []
    for back in range(1, 4):
        same = (seg_ids(len_ref, micro, pos - back) == seg) & (pos >= back)
        out.append(same.astype(F32))
    return out


def wide(mask, width=W):
    return jnp.concatenate([mask] * (width // LANES), axis=1)


def conv(v, taps, bias, keeps):
    total = bias + taps[3] * v
    for back in range(1, 4):
        total = total + taps[3 - back] * (pltpu.roll(v, back, 0) * keeps[back - 1])
    return total


def conv_back(dtotal, v, taps, keeps):
    dv = taps[3] * dtotal
    grads = [None] * 4
    grads[3] = jnp.sum(dtotal * v, axis=0, keepdims=True)
    for back in range(1, 4):
        masked = dtotal * keeps[back - 1]
        grads[3 - back] = jnp.sum(masked * pltpu.roll(v, back, 0), axis=0, keepdims=True)
        dv = dv + taps[3 - back] * pltpu.roll(masked, T - back, 0)
    return dv, grads, jnp.sum(dtotal, axis=0, keepdims=True)


def rows_of(ref, count):
    return [ref[k : k + 1, :] for k in range(count)]


def tri_mask(len_ref, micro, transposed=False):
    first = lax.broadcasted_iota(jnp.int32, (T, T), 0)
    second = lax.broadcasted_iota(jnp.int32, (T, T), 1)
    same = seg_ids(len_ref, micro, first) == seg_ids(len_ref, micro, second)
    order = (second >= first) if transposed else (first >= second)
    return (same & order).astype(F32)


def lower_ones(transposed):
    first = lax.broadcasted_iota(jnp.int32, (T, T), 0)
    second = lax.broadcasted_iota(jnp.int32, (T, T), 1)
    return ((second >= first) if transposed else (first >= second)).astype(F32)


def softplus(v):
    return jnp.maximum(v, 0.0) + jnp.log1p(jnp.exp(-jnp.abs(v)))


def spread_steps(dt, cums, dt_s, cum_s, cumt_s):
    turned = cums.T
    for i in range(STEPS):
        shift = (LANES - PER * i) % LANES
        dt_s[i] = pltpu.roll(dt, shift, 1) if shift else dt
        cum_s[i] = pltpu.roll(cums, shift, 1) if shift else cums
        cumt_s[i, 0:PER, :] = turned[PER * i : PER * (i + 1), :]


def head_lanes(value, k):
    lane = lax.broadcasted_iota(jnp.int32, value.shape, 1)
    return jnp.where((lane >= k * HEAD) & (lane < (k + 1) * HEAD), value, jnp.zeros_like(value))


def per_channel(dt):
    lane = lax.broadcasted_iota(jnp.int32, dt.shape, 1)
    tiles = []
    for p in range(PER // 2):
        tiles.append(
            jnp.where(
                lane < HEAD,
                jnp.broadcast_to(dt[:, 2 * p : 2 * p + 1], dt.shape),
                jnp.broadcast_to(dt[:, 2 * p + 1 : 2 * p + 2], dt.shape),
            )
        )
    return jnp.concatenate(tiles, axis=1)


def spread_heads(hp_ref, hp_s):
    count = hp_ref.shape[2]
    hp_s[STEPS] = jnp.zeros((8, LANES), F32)
    for k in range(3):
        hp_s[STEPS, k : k + 1, 0:count] = hp_ref[k]
    value = hp_s[STEPS]
    for i in range(STEPS):
        shift = (LANES - PER * i) % LANES
        hp_s[i] = pltpu.roll(value, shift, 1) if shift else value
    return value


def skip_row(hp_s, step):
    return per_channel(hp_s[step])[2:3, :]


def full(shape):
    return pl.BlockSpec(shape, lambda i: (0,) * len(shape))


def cols(rows):
    return pl.BlockSpec((rows, W), lambda i: (0, i))


def shape_of(shape, dtype):
    return jax.ShapeDtypeStruct(shape, dtype)


def far(shape, dtype):
    return pltpu.HBM(shape, dtype)


def near(shape, dtype):
    return pltpu.VMEM(shape, dtype)


class Rows:
    def __init__(self, array, m=None):
        self.array, self.m = array, m

    def spec(self):
        if self.m is None:
            return pl.BlockSpec((T, D), lambda *i: (0, 0))
        return pl.BlockSpec((None, T, D), lambda *i: (self.m, 0, 0))


def order(dep):
    if isinstance(dep, tuple):
        return dep[0], ANY
    return from_far(dep), HBM


class Halves:
    def __init__(self, mine, other):
        self.mine, self.other = mine, other


def rows_operands(source, name="e"):
    if isinstance(source, Rows):
        return {name: (source.array, source.spec())}
    half = pl.BlockSpec((HALF, D), lambda *i: (0, 0))
    return {name + MINE: (source.mine, half), name + OTHER: (source.other, half)}


MINE, OTHER = "_mine", "_other"


def half_rows(core):
    return pl.ds(pl.multiple_of(core * HALF, HALF), HALF)


def gather_rows(R, name, target):
    if hasattr(R, name):
        target[...] = getattr(R, name)[...].astype(target.dtype)
    else:
        target[half_rows(R.core[0]), :] = getattr(R, name + MINE)[...].astype(target.dtype)
        target[half_rows(1 - R.core[0]), :] = getattr(R, name + OTHER)[...].astype(target.dtype)


def part_rows(R, name, k, at=0, count=HALF):
    if hasattr(R, name):
        first = (1 - R.core[0] if k else R.core[0]) * HALF + at
        return getattr(R, name)[pl.ds(pl.multiple_of(first, STRIP), count), :].astype(F32)
    return getattr(R, name + (OTHER if k else MINE))[pl.ds(at, count), :].astype(F32)


STRIP = 32


def strips(rows, body):
    def step(c, _):
        body(pl.multiple_of(c * STRIP, STRIP))
        return 0

    lax.fori_loop(0, rows // STRIP, step, 0)


def ours(R, role):
    return R.flag[0] == role


def from_far(value):
    return pltpu.with_memory_space_constraint(value, pltpu.HBM)


TOKEN = (8, LANES)


SMEM = pl.BlockSpec(memory_space=pltpu.SMEM)
VMEM = pl.BlockSpec(memory_space=pltpu.VMEM)
ANY = pl.BlockSpec(memory_space=pl.ANY)
HBM = pl.BlockSpec(memory_space=pltpu.HBM)


def call(body, ins, outs, scratch, name, grid=(STEPS,), limit=VMEM_LIMIT):
    names = [*ins, *outs, *scratch]

    def kernel(*refs):
        body(SimpleNamespace(**dict(zip(names, refs))))

    values = pl.pallas_call(
        kernel,
        grid=grid,
        in_specs=[v[1] for v in ins.values()],
        out_specs=[v[1] for v in outs.values()],
        out_shape=tuple(v[0] for v in outs.values()),
        scratch_shapes=list(scratch.values()),
        compiler_params=pltpu.CompilerParams(
            dimension_semantics=("arbitrary",) * len(grid), vmem_limit_bytes=limit
        ),
        cost_estimate=COST,
        name=name,
    )(*[v[0] for v in ins.values()])
    return dict(zip(outs, values))


def scan_scratch():
    return dict(
        keep_s=pltpu.VMEM((3, T, LANES), F32),
        dt_s=pltpu.VMEM((STEPS, T, LANES), F32),
        cum_s=pltpu.VMEM((STEPS, T, LANES), F32),
        cumt_s=pltpu.VMEM((STEPS, 8, T), F32),
        hp_s=pltpu.VMEM((STEPS + 1, 8, LANES), F32),
        acc_s=pltpu.VMEM((T, D), F32),
    )


def forward_kernel(micro, R):
    step = pl.program_id(0)

    @pl.when(step == 0)
    def _():
        if not hasattr(R, "u"):
            gather_rows(R, "u", R.u_s)
        u = (R.u if hasattr(R, "u") else R.u_s)[...].astype(F32)
        s_zero = lax.rsqrt(jnp.mean(u * u, axis=1, keepdims=True) + EPS)
        low = (u * s_zero * R.norm[...]).astype(BF16)
        R.r_s[...] = low
        R.rt[...] = low.T
        keeps = keep_masks(R.lens, micro)
        for k in range(3):
            R.keep_s[k] = keeps[k]
        bcr = dot(low, R.bc[...])
        R.bcr[...] = bcr
        dtr = dot_nt(low, R.dt[...])
        R.dtr[...] = dtr
        total = conv(bcr, rows_of(R.cbc, 4), R.bbc[...], [wide(k, 2 * NS) for k in keeps])
        act = total * sigmoid(total)
        score = dot_nt(act[:, NS:].astype(BF16), act[:, :NS].astype(BF16)) * tri_mask(R.lens, micro)
        R.score_s[...] = score
        R.scoret[...] = score.T
        hp = spread_heads(R.hp, R.hp_s)
        dt = softplus(dtr + hp[0:1, :])
        rates = dt * (-jnp.exp(hp[1:2, :]))
        cums = position_sums(lower_ones(False), rates)
        R.cums[...] = cums
        spread_steps(dt, cums, R.dt_s, R.cum_s, R.cumt_s)
        R.acc_s[...] = jnp.zeros_like(R.acc_s)
        R.sq[...] = jnp.zeros_like(R.sq)

    keeps = [wide(R.keep_s[k]) for k in range(3)]
    low_z = dot(R.r_s[...], R.zx[0]).astype(BF16)
    low_x = dot(R.r_s[...], R.zx[1]).astype(BF16)
    R.z[...] = low_z
    R.x[...] = low_x
    z = low_z.astype(F32)
    x = low_x.astype(F32)
    total = conv(x, rows_of(R.cx, 4), R.bx[...], keeps)
    xc = total * sigmoid(total)
    cums = R.cum_s[step]
    cumt = R.cumt_s[step]
    xt = (xc * per_channel(R.dt_s[step])).astype(BF16)
    R.xt[...] = xt
    top = jnp.zeros((HALF, W), F32)
    bottom = jnp.zeros((HALF, W), F32)
    for k in range(PER):
        mine = head_lanes(xt, k)
        col = cums[:, k : k + 1]
        row = cumt[k : k + 1, :]
        mix = R.score_s[0:HALF, 0:HALF] * jnp.exp(jnp.minimum(col[:HALF] - row[:, :HALF], 0.0))
        top = top + dot(mix.astype(BF16), mine[:HALF])
        mix = R.score_s[HALF:T, :] * jnp.exp(jnp.minimum(col[HALF:] - row, 0.0))
        bottom = bottom + dot(mix.astype(BF16), mine)
    y = jnp.concatenate([top, bottom], axis=0) + skip_row(R.hp_s, step) * xc
    R.y[...] = y
    g = y * (z * sigmoid(z))
    squares = g * g
    for k in range(W // LANES):
        R.sq[...] += squares[:, k * LANES : (k + 1) * LANES]
    R.acc_s[...] += dot((g * R.gate[...]).astype(BF16), R.out[...])

    @pl.when(step == STEPS - 1)
    def _():
        R.part0[...] = R.acc_s[:HALF, :].astype(BF16)
        R.part1[...] = R.acc_s[HALF:, :].astype(BF16)
        R.token[...] = jnp.zeros(TOKEN, F32)


def small_operands(wts):
    return dict(
        bc=(wts.bc, full((D, 2 * NS))),
        dt=(wts.dt, full((LANES, D))),
        cx=(from_far(wts.cx), cols(4)),
        bx=(from_far(wts.bx), cols(1)),
        cbc=(from_far(wts.cbc), full((4, 2 * NS))),
        bbc=(from_far(wts.bbc), full((1, 2 * NS))),
        hp=(from_far(wts.hp), full(wts.hp.shape)),
    )


def forward(micro, role, flag, lens, core, u, wts, dep):
    def kernel(R):
        @pl.when(R.flag[0] != role)
        def _():
            for ref in (R.part0, R.part1, R.sq, R.token):
                ref[...] = jnp.zeros_like(ref)

        pl.when(ours(R, role))(lambda: forward_kernel(micro, R))

    ins = rows_operands(u, "u") | dict(
        flag=(flag, SMEM),
        core=(core, SMEM),
        lens=(lens, SMEM),
        norm=(from_far(wts.norm), full((1, D))),
        zx=(from_far(wts.zx), pl.BlockSpec((2, D, W), lambda i: (0, 0, i))),
        out=(from_far(wts.out), pl.BlockSpec((W, D), lambda i: (i, 0))),
        gate=(from_far(wts.gate), cols(1)),
        **small_operands(wts),
        dep=order(dep),
    )
    outs = dict(
        rt=(far((D, T), BF16), full((D, T))),
        z=(far((T, C), BF16), cols(T)),
        x=(far((T, C), BF16), cols(T)),
        y=(far((T, C), F32), cols(T)),
        bcr=(far((T, 2 * NS), F32), full((T, 2 * NS))),
        dtr=(far((T, LANES), F32), full((T, LANES))),
        part0=(shape_of((HALF, D), BF16), full((HALF, D))),
        part1=(shape_of((HALF, D), BF16), full((HALF, D))),
        sq=(shape_of((T, LANES), F32), full((T, LANES))),
        xt=(far((T, C), BF16), cols(T)),
        scoret=(far((T, T), F32), full((T, T))),
        cums=(far((T, LANES), F32), full((T, LANES))),
        token=(far(TOKEN, F32), full(TOKEN)),
    )
    scratch = scan_scratch() | dict(
        r_s=pltpu.VMEM((T, D), BF16),
        u_s=pltpu.VMEM((T, D), BF16),
        score_s=pltpu.VMEM((T, T), F32),
    )
    return call(kernel, ins, outs, scratch, "layer_forward")


def touch_kernel(*refs):
    refs[-1][...] = jnp.zeros(TOKEN, F32)


def touch(*values):
    return pl.pallas_call(
        touch_kernel,
        in_specs=[ANY] * len(values),
        out_specs=VMEM,
        out_shape=shape_of(TOKEN, F32),
        compiler_params=pltpu.CompilerParams(vmem_limit_bytes=SMALL_LIMIT),
        cost_estimate=COST,
        name="touch",
    )(*values)


def scale_of(sq0_ref, sq1_ref):
    squares = jnp.sum(sq0_ref[...] + sq1_ref[...], axis=1, keepdims=True)
    return lax.rsqrt(squares / DI + EPS)


def join_rows(mine, others):
    halves = [a[...].astype(F32) + b[...].astype(F32) for a, b in zip(mine, others)]
    return jnp.concatenate(halves, axis=0)


def join(flag, core, keep, dep, first):
    def second(R):
        gather_rows(R, "u", R.res)
        for k, (own, other) in enumerate(((R.p0, R.o0), (R.p1, R.o1))):

            def strip(at):
                here, span = pl.ds(at, STRIP), pl.ds(pl.multiple_of(k * HALF + at, STRIP), STRIP)
                squares = jnp.sum(R.sq0[span, :] + R.sq1[span, :], axis=1, keepdims=True)
                scale = lax.rsqrt(squares / DI + EPS)
                total = own[here, :].astype(F32) + other[here, :].astype(F32)
                R.res[span, :] = R.res[span, :] + scale * total

            strips(HALF, strip)

    def body(R):
        if not first:
            return second(R)
        scale = scale_of(R.sq0, R.sq1)
        total = join_rows((R.p0, R.p1), (R.o0, R.o1))
        gather_rows(R, "u", R.res)
        res = R.res[...] + scale * total
        R.res[...] = res.astype(BF16).astype(F32)
        R.low[...] = R.res[half_rows(R.core[0]), :].astype(BF16)
        R.total[...] = total.astype(BF16)
        R.scale[...] = jnp.broadcast_to(scale, (T, LANES))

    def kernel(R):
        R.token[...] = jnp.zeros(TOKEN, F32)
        pl.when(ours(R, 0 if first else 1))(lambda: body(R))

    ins = rows_operands(keep.u, "u") | dict(
        flag=(flag, SMEM),
        core=(core, SMEM),
        p0=(keep.part[0], VMEM),
        p1=(keep.part[1], VMEM),
        o0=(keep.other[0], VMEM),
        o1=(keep.other[1], VMEM),
        sq0=(keep.sq, VMEM),
        sq1=(keep.other_sq, VMEM),
        dep=order(dep),
    )
    outs = dict(res=(far((T, D), F32), full((T, D))), token=(far(TOKEN, F32), full(TOKEN)))
    if first:
        outs |= dict(
            low=(shape_of((HALF, D), BF16), VMEM),
            total=(far((T, D), BF16), full((T, D))),
            scale=(far((T, LANES), F32), full((T, LANES))),
        )
    return call(kernel, ins, outs, {}, "join_output", grid=(1,), limit=SMALL_LIMIT)


def gate_begin(R):
    gather_rows(R, "e", R.e_s)
    e = R.e_s[...].astype(F32)
    if hasattr(R, "total"):
        scale = R.scale[:, 0:1]
        total = R.total[...].astype(F32)
    else:
        scale = scale_of(R.sq0, R.sq1)
        total = join_rows((R.p0, R.p1), (R.o0, R.o1))
    inner = jnp.sum(e * total, axis=1, keepdims=True)
    R.scale_s[...] = jnp.broadcast_to(scale, (T, LANES))
    R.inner_s[...] = jnp.broadcast_to(inner * (scale * scale * scale) / DI, (T, LANES))
    R.et[...] = R.e_s[...].T


def gate_block(R):
    scale = wide(R.scale_s[...])
    z = R.z[...].astype(F32)
    y = R.y[...]
    gg = R.gate[...]
    dn = dot_nt(R.e_s[...], R.out[...])
    sig = sigmoid(z)
    act = z * sig
    g = y * act
    normed = g * scale
    R.n[...] = (normed * gg).astype(BF16)
    dg = scale * (gg * dn) - g * wide(R.inner_s[...])
    R.dz[...] = (dg * y * (sig * (1.0 + z * (1.0 - sig)))).astype(BF16)
    return y, (dg * act).astype(BF16), jnp.sum(normed * dn, axis=0, keepdims=True)


def scan_begin(micro, R):
    keeps = keep_masks(R.lens, micro)
    for k in range(3):
        R.keep_s[k] = keeps[k]
    hp = spread_heads(R.hp, R.hp_s)
    spread_steps(softplus(R.dtr[...] + hp[0:1, :]), R.cums[...], R.dt_s, R.cum_s, R.cumt_s)
    for ref in (R.acc_s, R.dscore_s, R.dcum_s, R.ddt_s, R.dskip_s):
        ref[...] = jnp.zeros_like(ref)


def scan_block(R, step, y, dyb, ggrad):
    keeps = [wide(R.keep_s[k]) for k in range(3)]
    taps = rows_of(R.cx, 4)
    x = R.x[...].astype(F32)
    total = conv(x, taps, R.bx[...], keeps)
    sig = sigmoid(total)
    xc = total * sig
    cums = R.cum_s[step]
    cumt = R.cumt_s[step]
    dtb = per_channel(R.dt_s[step])
    xt = R.xt[...]
    skip = skip_row(R.hp_s, step)
    inside = y - skip * xc
    top = jnp.zeros((HALF, W), F32)
    bottom = jnp.zeros((HALF, W), F32)
    for k in range(PER):
        my_dy = head_lanes(dyb, k)
        my_x = head_lanes(xt, k)
        col = cums[:, k : k + 1]
        row = cumt[k : k + 1, :]
        decay = jnp.exp(jnp.minimum(row - col[:HALF], 0.0))
        mix = R.scoret[0:HALF, :] * decay
        top = top + dot(mix.astype(BF16), my_dy)
        R.dscore_s[0:HALF, :] += dot_nt(my_x[:HALF], dyb) * decay
        decay = jnp.exp(jnp.minimum(row[:, HALF:] - col[HALF:], 0.0))
        mix = R.scoret[HALF:T, HALF:T] * decay
        bottom = bottom + dot(mix.astype(BF16), my_dy[HALF:])
        R.dscore_s[HALF:T, HALF:T] += dot_nt(my_x[HALF:], dyb[HALF:]) * decay
    dxt = jnp.concatenate([top, bottom], axis=0)
    chan = (lax.broadcasted_iota(jnp.int32, (W, LANES), 0) >> 6) + PER * step
    lane = lax.broadcasted_iota(jnp.int32, (W, LANES), 1)
    group = (chan == lane).astype(F32)
    dy = dyb.astype(F32)
    dxc = dtb * dxt + skip * dy
    dskip = jnp.broadcast_to(jnp.sum(dy * xc, axis=0, keepdims=True), (16, W))
    sums = group_sums([dy * inside - xt.astype(F32) * dxt, xc * dxt, dskip], group)
    R.dcum_s[...] += sums[0]
    R.ddt_s[...] += sums[1]
    R.dskip_s[...] += sums[2][:8]
    dtotal = dxc * (sig * (1.0 + total * (1.0 - sig)))
    dx, grads, dbias = conv_back(dtotal, x, taps, keeps)
    here = pl.ds(pl.multiple_of(step * W, W), W)
    for k, value in enumerate(grads + [dbias, ggrad]):
        R.pack[k : k + 1, here] = value
    low = dx.astype(BF16)
    R.dx[...] = low
    R.acc_s[...] += dot_nt(R.dz[...], R.zx[0]) + dot_nt(low, R.zx[1])


def scan_end(micro, R):
    keeps = [wide(R.keep_s[k], 2 * NS) for k in range(3)]
    bcr = R.bcr[...]
    taps = rows_of(R.cbc, 4)
    total = conv(bcr, taps, R.bbc[...], keeps)
    sig = sigmoid(total)
    act = total * sig
    dscore = R.dscore_s[...] * tri_mask(R.lens, micro, True)
    db = dot(dscore.astype(BF16), act[:, NS:].astype(BF16))
    dc = dot(dscore.T.astype(BF16), act[:, :NS].astype(BF16))
    dact = jnp.concatenate([db, dc], axis=1)
    dtotal = dact * (sig * (1.0 + total * (1.0 - sig)))
    dbc, grads, dbias = conv_back(dtotal, bcr, taps, keeps)
    for k, value in enumerate(grads + [dbias]):
        R.pack[7:8, 2 * NS * k : 2 * NS * (k + 1)] = value
    hp = R.hp_s[STEPS]
    pre = R.dtr[...] + hp[0:1, :]
    decay_rate = -jnp.exp(hp[1:2, :])
    dt = softplus(pre)
    drates = position_sums(lower_ones(True), R.dcum_s[...])
    heads = R.hp.shape[2]
    lane = lax.broadcasted_iota(jnp.int32, (T, LANES), 1)
    ddt = (R.ddt_s[...] + drates * decay_rate) * sigmoid(pre)
    ddt = jnp.where(lane < heads, ddt, 0.0)
    shift = jnp.sum(ddt, axis=0, keepdims=True)
    decay = jnp.sum(drates * dt, axis=0, keepdims=True) * decay_rate
    decay = jnp.where(lane[0:1] < heads, decay, 0.0)
    both = jnp.concatenate([shift, decay, R.dskip_s[2:8, :]], axis=0)
    tile = both[0:1] + pltpu.roll(both, 32, 1)[1:2] + pltpu.roll(both, 64, 1)[2:3]
    R.pack[7:8, 10 * NS : 11 * NS] = tile
    R.pack[7:8, 11 * NS :] = jnp.zeros((1, NS), F32)
    low_bc = dbc.astype(BF16)
    low_dt = ddt.astype(BF16)
    R.bcdt[:, : 2 * NS] = low_bc
    R.bcdt[:, 2 * NS :] = low_dt
    out = R.acc_s[...] + dot_nt(low_bc, R.bc[...]) + dot(low_dt, R.dt[...])
    R.acc_s[...] = out
    R.mine[...] = R.acc_s[half_rows(R.core[0]), :].astype(BF16)
    R.theirs[...] = R.acc_s[half_rows(1 - R.core[0]), :].astype(BF16)
    gather_rows(R, "u", R.u_s)
    u = R.u_s[...].astype(F32)
    s_zero = lax.rsqrt(jnp.mean(u * u, axis=1, keepdims=True) + EPS)
    R.pack[6:7, :] = jnp.sum(u * s_zero * out, axis=0, keepdims=True)
    R.token[...] = jnp.zeros(TOKEN, F32)


def gate_operands(e, keep, wts):
    ins = rows_operands(e) | dict(
        z=(from_far(keep.z), cols(T)),
        y=(from_far(keep.y), cols(T)),
        gate=(from_far(wts.gate), cols(1)),
        out=(from_far(wts.out), pl.BlockSpec((W, D), lambda i: (i, 0))),
    )
    if hasattr(keep, "total"):
        return ins | dict(
            total=(from_far(keep.total), full((T, D))), scale=(from_far(keep.scale), full((T, LANES)))
        )
    part, other = keep.part, keep.other
    ins |= dict(
        p0=(part[0], full((HALF, D))),
        p1=(part[1], full((HALF, D))),
        o0=(other[0], full((HALF, D))),
        o1=(other[1], full((HALF, D))),
        sq0=(keep.sq, full((T, LANES))),
        sq1=(keep.other_sq, full((T, LANES))),
    )
    return ins


def gate_results():
    return dict(
        et=(far((D, T), BF16), full((D, T))),
        n=(far((T, C), BF16), cols(T)),
        dz=(far((T, C), BF16), cols(T)),
    )


GATE_SCRATCH = dict(
    e_s=pltpu.VMEM((T, D), BF16), scale_s=pltpu.VMEM((T, LANES), F32), inner_s=pltpu.VMEM((T, LANES), F32))


def scan_operands(lens, core, keep, wts):
    return rows_operands(keep.u, "u") | dict(
        lens=(lens, SMEM),
        core=(core, SMEM),
        x=(from_far(keep.x), cols(T)),
        xt=(from_far(keep.xt), cols(T)),
        bcr=(from_far(keep.bcr), full((T, 2 * NS))),
        dtr=(from_far(keep.dtr), full((T, LANES))),
        scoret=(from_far(keep.scoret), full((T, T))),
        cums=(from_far(keep.cums), full((T, LANES))),
        zx=(from_far(wts.zx), pl.BlockSpec((2, D, W), lambda i: (0, 0, i))),
        **small_operands(wts),
    )


def scan_results():
    return dict(
        dx=(far((T, C), BF16), cols(T)),
        bcdt=(far((T, 3 * LANES), BF16), full((T, 3 * LANES))),
        mine=(shape_of((HALF, D), BF16), full((HALF, D))),
        theirs=(shape_of((HALF, D), BF16), full((HALF, D))),
        pack=(far((PACK, C), F32), full((PACK, C))),
        token=(far(TOKEN, F32), full(TOKEN)),
    )


def back_scratch():
    return scan_scratch() | dict(
        dscore_s=pltpu.VMEM((T, T), F32),
        dcum_s=pltpu.VMEM((T, LANES), F32),
        ddt_s=pltpu.VMEM((T, LANES), F32),
        dskip_s=pltpu.VMEM((8, LANES), F32),
        u_s=pltpu.VMEM((T, D), BF16),
    )


def gate_back(flag, core, e, keep, wts, dep):
    def body(R):
        pl.when(pl.program_id(0) == 0)(lambda: gate_begin(R))
        _, R.dy[...], R.ggrad[...] = gate_block(R)

    ins = gate_operands(e, keep, wts) | dict(flag=(flag, SMEM), core=(core, SMEM), dep=order(dep))
    outs = gate_results() | dict(dy=(far((T, C), BF16), cols(T)), ggrad=(far((1, C), F32), cols(1)))
    return call(
        lambda R: pl.when(ours(R, 0))(lambda: body(R)), ins, outs, GATE_SCRATCH, "gate_backward"
    )


def no_rows(R):
    for ref in (R.mine, R.theirs, R.token):
        ref[...] = jnp.zeros_like(ref)


def scan_back(micro, flag, lens, core, keep, wts, dep):
    def body(R):
        step = pl.program_id(0)
        pl.when(step == 0)(lambda: scan_begin(micro, R))
        scan_block(R, step, R.y[...], R.dy[...], R.ggrad[...])
        pl.when(step == STEPS - 1)(lambda: scan_end(micro, R))

    def kernel(R):
        pl.when(R.flag[0] != 0)(lambda: no_rows(R))
        pl.when(ours(R, 0))(lambda: body(R))

    ins = scan_operands(lens, core, keep, wts) | dict(
        flag=(flag, SMEM),
        y=(from_far(keep.y), cols(T)),
        dy=(from_far(keep.dy), cols(T)),
        dz=(from_far(keep.dz), cols(T)),
        ggrad=(from_far(keep.ggrad), cols(1)),
        dep=order(dep),
    )
    return call(kernel, ins, scan_results(), back_scratch(), "scan_backward")


def layer_back(micro, role, flag, lens, core, e, keep, wts, dep):
    def body(R):
        step = pl.program_id(0)

        @pl.when(step == 0)
        def _():
            gate_begin(R)
            scan_begin(micro, R)

        scan_block(R, step, *gate_block(R))
        pl.when(step == STEPS - 1)(lambda: scan_end(micro, R))

    def kernel(R):
        pl.when(R.flag[0] != role)(lambda: no_rows(R))
        pl.when(ours(R, role))(lambda: body(R))

    ins = dict(flag=(flag, SMEM), **gate_operands(e, keep, wts), **scan_operands(lens, core, keep, wts))
    return call(
        kernel,
        ins | dict(dep=order(dep)),
        gate_results() | scan_results(),
        back_scratch() | GATE_SCRATCH,
        "layer_backward",
    )


def input_rows(R, e, u, dr):
    s_zero = lax.rsqrt(jnp.mean(u * u, axis=1, keepdims=True) + EPS)
    gained = R.norm[...] * dr
    shared = s_zero * s_zero * s_zero * jnp.mean(u * gained, axis=1, keepdims=True)
    return e + s_zero * gained - u * shared


def input_send(flag, core, keep, wts):
    def body(R):
        dr = R.mine[...].astype(F32) + R.came[...].astype(F32)
        R.low[...] = input_rows(R, part_rows(R, "e", 0), part_rows(R, "u", 0), dr).astype(BF16)

    def kernel(R):
        R.token[...] = jnp.zeros(TOKEN, F32)
        pl.when(ours(R, 1))(lambda: body(R))

    ins = rows_operands(keep.e) | rows_operands(keep.u, "u") | dict(
        flag=(flag, SMEM),
        core=(core, SMEM),
        norm=(from_far(wts.norm), full((1, D))),
        mine=(keep.mine, VMEM),
        came=(keep.came, VMEM),
    )
    outs = dict(low=(shape_of((HALF, D), BF16), VMEM), token=(far(TOKEN, F32), full(TOKEN)))
    return call(kernel, ins, outs, {}, "input_send", grid=(1,), limit=SMALL_LIMIT)


def input_back(core, keep, wts, dep):
    def kernel(R):
        for k, (own, other) in enumerate(((R.mine, R.came), (R.theirs, R.left))):

            def strip(at):
                span = pl.ds(at, STRIP)
                dr = own[span, :].astype(F32) + other[span, :].astype(F32)
                e, u = part_rows(R, "e", k, at, STRIP), part_rows(R, "u", k, at, STRIP)
                first = (1 - R.core[0] if k else R.core[0]) * HALF + at
                R.du[pl.ds(pl.multiple_of(first, STRIP), STRIP), :] = input_rows(R, e, u, dr)

            strips(HALF, strip)
        R.token[...] = jnp.zeros(TOKEN, F32)

    ins = rows_operands(keep.e) | rows_operands(keep.u, "u") | dict(
        core=(core, SMEM),
        norm=(from_far(wts.norm), full((1, D))),
        mine=(keep.mine, full((HALF, D))),
        came=(keep.came, full((HALF, D))),
        theirs=(keep.theirs, full((HALF, D))),
        left=(keep.left, full((HALF, D))),
        dep=order(dep),
    )
    outs = dict(du=(far((T, D), F32), full((T, D))), token=(far(TOKEN, F32), full(TOKEN)))
    return call(kernel, ins, outs, {}, "input_backward", grid=(1,), limit=SMALL_LIMIT)


def hold(value, dep):
    def kernel(R):
        R.out[...] = R.value[...]

    ins = dict(value=(value, VMEM), dep=order(dep))
    outs = dict(out=(shape_of(value.shape, value.dtype), VMEM))
    return call(kernel, ins, outs, {}, "hold", grid=(1,), limit=SMALL_LIMIT)["out"]


def swap(value):
    return lax.ppermute(value, "tensor", [(0, 1), (1, 0)])


def relay_up(value):
    return lax.ppermute(value, "pipe", [(0, 1)])


def relay_down(value):
    return lax.ppermute(value, "pipe", [(1, 0)])


def partners():
    def make(fn):
        return [fn(i // 8, (i // 2) % 4, i % 2) for i in range(32)]

    def pack(y, x, z):
        return y * 8 + x * 2 + z

    def wrap(v):
        return (v + 1) % 4 if v % 2 else (v - 1) % 4

    return [
        make(lambda y, x, z: pack(y, x ^ 1, z)),
        make(lambda y, x, z: pack(y ^ 1, x, z)),
        make(lambda y, x, z: pack(y, wrap(x), z)),
        make(lambda y, x, z: pack(wrap(y), x, z)),
        make(lambda y, x, z: pack(y, x, z ^ 1)),
    ]


STREAMS = 5


LAST = ((0, 4), (0, 1), (2, 1), (2, 3), (3, 4))


def dims_of(stream, late):
    if late:
        return [(stream + k) % 5 for k in range(1, 4)] + list(LAST[stream])
    return [(stream + k) % 5 for k in range(5)]


def ends_first(s):
    return dims_of(s, 0)[4] == LAST[s][0]


def round_groups(which):
    dims = sorted({last[which] for last in LAST})
    return [(d, [s for s in range(5) if LAST[s][which] == d]) for d in dims]


def block_order(maps, stream, late=0):
    order = [maps[d] for d in dims_of(stream, late)]
    count = len(order[0])
    table = np.zeros((count, count), np.int32)
    for me in range(count):
        for p in range(count):
            owner = me
            for k, step in enumerate(order):
                if (p >> (len(order) - 1 - k)) & 1:
                    owner = step[owner]
            table[me, p] = owner
    return table


TILES_EARLY = [("et", "n", LANES * k) for k in range(C // LANES)] + [
    ("rt", "dz", LANES * k) for k in range(C // LANES)
]
TILES_LATE = [("rt", "dx", LANES * k) for k in range(C // LANES)] + [
    ("rt", "bcdt", LANES * k) for k in range(3)
]


def deal(tiles, sizes):
    return [tiles[sum(sizes[:s]) : sum(sizes[: s + 1])] for s in range(STREAMS)]


EARLY, LATE = deal(TILES_EARLY, (5, 5, 5, 4, 5)), deal(TILES_LATE, (3, 3, 3, 3, 3))
PACK = 8
PACK_ROWS = 2 * PACK * (C // LANES)
PACK_STREAM = 3


def runs(tiles):
    out = []
    for at, (left, right, first) in enumerate(tiles):
        if out and out[-1][:2] == [left, right] and out[-1][2] + LANES * out[-1][3] == first:
            out[-1][3] += 1
        else:
            out.append([left, right, first, 1, at])
    return out


class Loader:
    def __init__(self, flag_ref, names, sources, held, sem):
        self.flag, self.names, self.sources, self.held, self.sem = flag_ref, names, sources, held, sem
        self.waited = set()

    def copy(self, k, m, early):
        span = pl.ds(m * T, T)
        ref = self.held[k]
        slot = ref.at[:, span] if ref.shape[0] == D else ref.at[span, :]
        return pltpu.make_async_copy(self.sources[4 * k + 2 * early + m], slot, self.sem.at[2 * k + m])

    def start(self, name):
        k = self.names.index(name)
        for m in range(2):
            pl.when(self.flag[0] == 1)(lambda: self.copy(k, m, 0).start())
            pl.when(self.flag[0] == 0)(lambda: self.copy(k, m, 1).start())

    def get(self, name):
        k = self.names.index(name)
        if name not in self.waited:
            self.waited.add(name)
            for m in range(2):
                self.copy(k, m, 0).wait()
        return self.held[k]


def held_shapes(arrays):
    shapes = []
    for a in arrays:
        rows, columns = a[0].shape
        shapes.append(pltpu.VMEM((rows, 2 * columns) if rows == D else (2 * rows, columns), BF16))
    return shapes


def products(loader, lefts, tiles, blocks, owner_of, place):
    rows, half, chunk = D // blocks, D // 2, 384
    placed = []
    for left, right, first, count, at in runs(tiles):
        held, rhs = loader.get(left), loader.get(right)
        if left not in placed:
            placed.append(left)
            for p in range(blocks):
                start = pl.multiple_of(owner_of(p) * rows, 16)
                lefts[len(placed) - 1, p * rows : (p + 1) * rows, :] = held[pl.ds(start, rows), :]
        slot = placed.index(left)
        for side in range(2):
            for row in range(0, half, chunk):
                span = slice(side * half + row, side * half + row + chunk)
                value = dot(lefts[slot, span, :], rhs[:, first : first + LANES * count]).astype(BF16)
                for j in range(count):
                    place(side, at + j, row, value[:, j * LANES : (j + 1) * LANES])


def early_kernel(blocks, flag_ref, table_ref, *refs):
    names = ["et", "n", "rt", "dz"]
    sources, refs = refs[:16], refs[16:]
    outs, token_ref = refs[: 2 * STREAMS], refs[2 * STREAMS]
    held, lefts, in_sem = refs[2 * STREAMS + 1 :]
    loader = Loader(flag_ref, names, sources, held, in_sem)
    for name in names:
        loader.start(name)
    for s in range(STREAMS):

        def place(side, tile, row, value):
            outs[2 * s + side][tile, row : row + value.shape[0], :] = value

        def owner_of(p):
            return table_ref[flag_ref[1] + s * blocks + p]

        products(loader, lefts, EARLY[s], blocks, owner_of, place)
    token_ref[...] = jnp.zeros(TOKEN, F32)


def early_grads(flag, table, arrays, blocks):
    out = []
    for s in range(STREAMS):
        out += [near((len(EARLY[s]), D // 2, LANES), BF16)] * 2
    flat = pl.pallas_call(
        functools.partial(early_kernel, blocks),
        in_specs=[SMEM, SMEM] + [HBM] * 16,
        out_specs=[VMEM] * (len(out) + 1),
        out_shape=tuple(out) + (shape_of(TOKEN, F32),),
        scratch_shapes=[
            held_shapes(arrays),
            pltpu.VMEM((2, D, 2 * T), BF16),
            pltpu.SemaphoreType.DMA((8,)),
        ],
        compiler_params=pltpu.CompilerParams(vmem_limit_bytes=VMEM_LIMIT),
        cost_estimate=COST,
        name="grad_early",
    )(flag, table, *[from_far(v) for a in arrays for v in a])
    return list(flat[0:-1:2]), list(flat[1:-1:2]), flat[-1]


def total_rows(s, early, late):
    return len(EARLY[s]) * early + len(LATE[s]) * late + (PACK_ROWS if s == PACK_STREAM else 0)


def split_pair(value):
    high = value.astype(BF16)
    return jnp.concatenate([high, (value - high.astype(F32)).astype(BF16)], axis=0)


def join_pair(pair):
    wide_pair = pair.astype(F32)
    return wide_pair[:PACK] + wide_pair[PACK:]


def late_kernel(blocks, flag_ref, table_ref, *refs):
    names = ["rt", "dx", "bcdt"]
    sources, refs = refs[:12], refs[12:]
    packs, refs = refs[:4], refs[4:]
    keeps, gots, refs = refs[:STREAMS], refs[STREAMS : 2 * STREAMS], refs[2 * STREAMS :]
    outs, token_ref = refs[: 2 * STREAMS], refs[2 * STREAMS]
    held, lefts, in_sem = refs[2 * STREAMS + 1 :]
    loader = Loader(flag_ref, names, sources, held, in_sem)
    for name in names:
        loader.start(name)
    half = D // 2
    quarter = half // 2
    for s in range(STREAMS):
        for j in range(len(EARLY[s])):
            for side in range(2):
                span = slice(side * quarter, (side + 1) * quarter)
                total = keeps[s][j, span, :].astype(F32) + gots[s][j, span, :].astype(F32)
                outs[2 * s + side][j * quarter : (j + 1) * quarter, :] = total.astype(BF16)
    last = flag_ref[0] == 1
    total = jnp.where(last, packs[0][...] + packs[1][...], packs[2][...] + packs[3][...])
    for j in range(C // LANES):
        pair = split_pair(total[:, j * LANES : (j + 1) * LANES])
        at = total_rows(PACK_STREAM, quarter, half) - PACK_ROWS + 2 * PACK * j
        for side in range(2):
            outs[2 * PACK_STREAM + side][at : at + 2 * PACK, :] = pair
    for s in range(STREAMS):
        base = len(EARLY[s]) * quarter

        def place(side, tile, row, value):
            at = base + tile * half + row
            outs[2 * s + side][at : at + value.shape[0], :] = value

        def owner_of(p):
            return table_ref[flag_ref[1] + s * blocks + p]

        products(loader, lefts, LATE[s], blocks, owner_of, place)
    token_ref[...] = jnp.zeros(TOKEN, F32)


def late_grads(flag, table, arrays, blocks, packs, keeps, gots):
    out = []
    for s in range(STREAMS):
        out += [near((total_rows(s, D // 4, D // 2), LANES), BF16)] * 2
    flat = pl.pallas_call(
        functools.partial(late_kernel, blocks),
        in_specs=[SMEM, SMEM] + [HBM] * 12 + [VMEM] * (4 + 2 * STREAMS),
        out_specs=[VMEM] * (len(out) + 1),
        out_shape=tuple(out) + (shape_of(TOKEN, F32),),
        scratch_shapes=[
            held_shapes(arrays),
            pltpu.VMEM((1, D, 2 * T), BF16),
            pltpu.SemaphoreType.DMA((6,)),
        ],
        compiler_params=pltpu.CompilerParams(vmem_limit_bytes=VMEM_LIMIT),
        cost_estimate=COST,
        name="grad_late",
    )(
        flag,
        table,
        *[from_far(v) for a in arrays for v in a],
        *packs,
        *keeps,
        *gots,
    )
    return list(flat[0:-1:2]), list(flat[1:-1:2]), flat[-1]


def fold(s, keep, got, early, late, deps):
    def kernel(keep, got, *refs):
        next_keep, next_send, token = refs[len(pairs) :]
        at = to = 0
        for rows, tiles in ((early, EARLY[s]), (late, LATE[s])):
            for _ in tiles:
                next_send[to : to + rows // 2, :] = add(keep, got, at + rows // 2, rows // 2).astype(BF16)
                next_keep[to : to + rows // 2, :] = add(keep, got, at, rows // 2).astype(BF16)
                at += rows
                to += rows // 2
        if s == PACK_STREAM:
            add_packs((keep, at), (got, at), ((next_keep, to), (next_send, to)))
        token[...] = jnp.zeros(TOKEN, F32)

    pairs = [order(dep) for dep in deps]
    rows = total_rows(s, early // 2, late // 2)
    out = [near((rows, LANES), BF16), near((rows, LANES), BF16), near(TOKEN, F32)]
    return pl.pallas_call(
        kernel,
        in_specs=[VMEM] * 2 + [spec for _, spec in pairs],
        out_specs=[VMEM, VMEM, VMEM],
        out_shape=tuple(out),
        compiler_params=pltpu.CompilerParams(vmem_limit_bytes=SMALL_LIMIT),
        cost_estimate=COST,
        name="fold_grads",
    )(keep, got, *[value for value, _ in pairs])


def add(keep, got, at, rows, got_at=None):
    got_at = at if got_at is None else got_at
    return keep[at : at + rows, :].astype(F32) + got[got_at : got_at + rows, :].astype(F32)


def pack_sum(keep, keep_at, got, got_at, j):
    a = keep[keep_at + 2 * PACK * j : keep_at + 2 * PACK * (j + 1), :]
    b = got[got_at + 2 * PACK * j : got_at + 2 * PACK * (j + 1), :]
    return join_pair(a) + join_pair(b)


def add_packs(keep, got, targets):
    for j in range(C // LANES):
        pair = split_pair(pack_sum(*keep, *got, j))
        for ref, at in targets:
            ref[at + 2 * PACK * j : at + 2 * PACK * (j + 1), :] = pair


BLOCK = 48


def payload(s, which):
    early = BLOCK if ends_first(s) != bool(which) else 0
    late = BLOCK if which else 2 * BLOCK
    return len(EARLY[s]) * early, len(LATE[s]) * late, PACK_ROWS if s == PACK_STREAM else 0


def places(which):
    where, sizes = {}, []
    for g, (_, streams) in enumerate(round_groups(which)):
        at = 0
        for s in streams:
            where[s] = (g, at)
            at += sum(payload(s, which))
        sizes.append(at)
    return where, sizes


def keep_rows(s):
    early = len(EARLY[s]) * BLOCK
    return early if ends_first(s) else 2 * early, len(LATE[s]) * 2 * BLOCK, payload(s, 0)[2]


def third_kernel(*refs):
    refs = refs[: 2 * STREAMS] + refs[2 * STREAMS + 1 :]
    keeps, gots = refs[:STREAMS], refs[STREAMS : 2 * STREAMS]
    next_keeps, sends = refs[2 * STREAMS : 3 * STREAMS], refs[3 * STREAMS :]
    where, _ = places(0)
    for s in range(STREAMS):
        keep, got, out = keeps[s], gots[s], next_keeps[s]
        group, to = where[s]
        target = sends[group]
        early = len(EARLY[s]) * BLOCK
        at = 0
        for j in range(len(EARLY[s])):
            out[j * BLOCK : (j + 1) * BLOCK, :] = add(keep, got, at, BLOCK).astype(BF16)
            value = add(keep, got, at + BLOCK, BLOCK).astype(BF16)
            if ends_first(s):
                target[to + j * BLOCK : to + (j + 1) * BLOCK, :] = value
            else:
                out[early + j * BLOCK : early + (j + 1) * BLOCK, :] = value
            at += 2 * BLOCK
        base, to = keep_rows(s)[0], to + payload(s, 0)[0]
        half = 2 * BLOCK
        for j in range(len(LATE[s])):
            out[base + j * half : base + (j + 1) * half, :] = add(keep, got, at, half).astype(BF16)
            target[to + j * half : to + (j + 1) * half, :] = add(keep, got, at + half, half).astype(BF16)
            at += 2 * half
        if s == PACK_STREAM:
            spots = ((out, base + len(LATE[s]) * half), (target, to + len(LATE[s]) * half))
            add_packs((keep, at), (got, at), spots)


def fourth_kernel(*refs):
    groups = len(round_groups(0))
    refs = refs[: STREAMS + groups] + refs[STREAMS + groups + 1 :]
    keeps, gots = refs[:STREAMS], refs[STREAMS : STREAMS + groups]
    refs = refs[STREAMS + groups :]
    dones, next_keeps, sends = refs[:STREAMS], refs[STREAMS : 2 * STREAMS], refs[2 * STREAMS :]
    came, _ = places(0)
    where, _ = places(1)
    for s in range(STREAMS):
        keep, got, out = keeps[s], gots[came[s][0]], next_keeps[s]
        target, to = sends[where[s][0]], where[s][1]
        at = came[s][1]
        early = len(EARLY[s]) * BLOCK
        if ends_first(s):
            dones[s][...] = add(keep, got, 0, early, at)
        else:
            dones[s][...] = keep[:early, :].astype(F32)
            target[to : to + early, :] = keep[early : 2 * early, :]
        at, to, base = at + payload(s, 0)[0], to + payload(s, 1)[0], keep_rows(s)[0]
        for j in range(len(LATE[s])):
            first = base + 2 * BLOCK * j
            out[j * BLOCK : (j + 1) * BLOCK, :] = add(keep, got, first, BLOCK, at).astype(BF16)
            value = add(keep, got, first + BLOCK, BLOCK, at + BLOCK).astype(BF16)
            target[to + j * BLOCK : to + (j + 1) * BLOCK, :] = value
            at += 2 * BLOCK
        if s == PACK_STREAM:
            late = len(LATE[s]) * BLOCK
            add_packs((keep, base + 2 * late), (got, at), ((out, late), (target, to + late)))


def last_folds(kernel, operands, dep, shapes, name):
    return pl.pallas_call(
        kernel,
        in_specs=[VMEM] * len(operands) + [ANY],
        out_specs=[VMEM] * len(shapes),
        out_shape=tuple(near((rows, LANES), dtype) for rows, dtype in shapes),
        compiler_params=pltpu.CompilerParams(vmem_limit_bytes=SMALL_LIMIT),
        cost_estimate=COST,
        name=name,
    )(*operands, dep)


def fold_third(keeps, gots, dep):
    shapes = [(sum(keep_rows(s)), BF16) for s in range(STREAMS)]
    shapes += [(rows, BF16) for rows in places(0)[1]]
    flat = last_folds(third_kernel, [*keeps, *gots], dep, shapes, "fold_third")
    return flat[:STREAMS], flat[STREAMS:]


def fold_fourth(keeps, gots, dep):
    shapes = [(len(EARLY[s]) * BLOCK, F32) for s in range(STREAMS)]
    shapes += [(sum(payload(s, 1)[1:]), BF16) for s in range(STREAMS)]
    shapes += [(rows, BF16) for rows in places(1)[1]]
    flat = last_folds(fourth_kernel, [*keeps, *gots], dep, shapes, "fold_fourth")
    return flat[:STREAMS], flat[STREAMS : 2 * STREAMS], flat[2 * STREAMS :]


def end_kernel(rows, heads, core_ref, *refs):
    groups = len(round_groups(1))
    dones, keeps, gots = refs[:STREAMS], refs[STREAMS : 2 * STREAMS], refs[2 * STREAMS :][:groups]
    refs = refs[2 * STREAMS + groups :]
    out_ref, zx_ref, dt_ref, cx_ref, bx_ref, gate_ref, heads_ref = refs[:7]
    mine_ref, theirs_ref, shared_ref, bcdt_s = refs[7:]
    came, _ = places(1)

    def place(right, first, value):
        if right == "n":
            out_ref[:, first : first + LANES] = value
        elif right == "bcdt":
            bcdt_s[:, first : first + LANES] = value
        else:
            zx_ref[:, 0 if right == "dz" else 1, first : first + LANES] = value

    for s in range(STREAMS):
        got, at = gots[came[s][0]], came[s][1]
        for j, (_, right, first) in enumerate(EARLY[s]):
            value = dones[s][j * rows : (j + 1) * rows, :]
            if not ends_first(s):
                value = value + got[at : at + rows, :].astype(F32)
                at += rows
            place(right, first, value)
        for j, (_, right, first) in enumerate(LATE[s]):
            place(right, first, add(keeps[s], got, j * rows, rows, at))
            at += rows
        if s == PACK_STREAM:
            keep, keep_at = keeps[s], len(LATE[s]) * rows
            for j in range(C // LANES):
                lanes = slice(j * LANES, (j + 1) * LANES)
                value = pack_sum(keep, keep_at, got, at, j)
                cx_ref[:, lanes] = value[0:4]
                bx_ref[:, lanes] = value[4:5]
                gate_ref[:, lanes] = value[5:6]
                shared_ref[:, lanes] = value[6:8]
                if j == 10:
                    for k in range(3):
                        moved = pltpu.roll(value, (LANES - 32 * k) % LANES, 1) if k else value
                        heads_ref[k : k + 1, :] = moved[7:8, :heads]
    part = rows // 2
    mine_ref[...] = bcdt_s[pl.ds(pl.multiple_of(core_ref[0] * part, 8), part), : 2 * NS]
    theirs_ref[...] = bcdt_s[pl.ds(pl.multiple_of((1 - core_ref[0]) * part, 8), part), : 2 * NS]
    dt_ref[...] = bcdt_s[:, 2 * NS :].T[:heads, :]


def end(core, dones, keeps, gots, rows, heads):
    return pl.pallas_call(
        functools.partial(end_kernel, rows, heads),
        in_specs=[SMEM] + [VMEM] * (2 * STREAMS + len(gots)),
        out_specs=[VMEM] * 10,
        out_shape=(
            shape_of((rows, C), F32),
            shape_of((rows, 2, C), F32),
            shape_of((heads, rows), F32),
            shape_of((4, C), F32),
            shape_of((1, C), F32),
            shape_of((1, C), F32),
            shape_of((3, heads), F32),
            shape_of((rows // 2, 2 * NS), F32),
            shape_of((rows // 2, 2 * NS), F32),
            shape_of((2, C), F32),
        ),
        scratch_shapes=[pltpu.VMEM((rows, 3 * LANES), F32)],
        compiler_params=pltpu.CompilerParams(vmem_limit_bytes=SMALL_LIMIT),
        cost_estimate=COST,
        name="grad_end",
    )(core, *dones, *keeps, *gots)


def last_kernel(mine_ref, other_ref, shared_ref, other_shared_ref, bc_ref, norm_ref, conv_ref, bias_ref):
    bc_ref[...] = mine_ref[...] + other_ref[...]
    total = shared_ref[...] + other_shared_ref[...]
    norm_ref[...] = total[0:1]
    for k in range(4):
        conv_ref[k : k + 1, :] = total[1:2, 2 * NS * k : 2 * NS * (k + 1)]
    bias_ref[...] = total[1:2, 8 * NS : 10 * NS]


def last_sums(mine, other, shared, other_shared):
    return pl.pallas_call(
        last_kernel,
        in_specs=[VMEM] * 4,
        out_specs=[VMEM] * 4,
        out_shape=(
            shape_of(mine.shape, F32),
            shape_of((1, C), F32),
            shape_of((4, 2 * NS), F32),
            shape_of((1, 2 * NS), F32),
        ),
        compiler_params=pltpu.CompilerParams(vmem_limit_bytes=SMALL_LIMIT),
        cost_estimate=COST,
        name="last_sums",
    )(mine, other, shared, other_shared)


def pick_kernel(flag_ref, late0, late1, early0, early1, _, out_ref, token_ref, held, sem):
    for m, (late, early) in enumerate(((late0, early0), (late1, early1))):

        def start(source):
            pltpu.make_async_copy(source, held.at[m], sem.at[m]).start()

        pl.when(flag_ref[0] == 1)(lambda: start(late))
        pl.when(flag_ref[0] == 0)(lambda: start(early))
    for m in range(2):
        pltpu.make_async_copy(early0, held.at[m], sem.at[m]).wait()
        pltpu.make_async_copy(held.at[m], out_ref.at[m], sem.at[2 + m]).start()
    for m in range(2):
        pltpu.make_async_copy(held.at[m], out_ref.at[m], sem.at[2 + m]).wait()
    token_ref[...] = jnp.zeros(TOKEN, F32)


def pick(flag, late, early, dep):
    return pl.pallas_call(
        pick_kernel,
        in_specs=[SMEM] + [HBM] * 4 + [ANY],
        out_specs=[HBM, VMEM],
        out_shape=(far((2, T, D), F32), shape_of(TOKEN, F32)),
        scratch_shapes=[pltpu.VMEM((2, T, D), F32), pltpu.SemaphoreType.DMA((4,))],
        compiler_params=pltpu.CompilerParams(vmem_limit_bytes=SMALL_LIMIT),
        cost_estimate=COST,
        name="pick_section",
    )(flag, *[from_far(v) for v in (*late, *early)], dep)


def send(value, step):
    return lax.ppermute(value, "dp", [(i, to) for i, to in enumerate(step)])


def body(
    tokens,
    cotangent,
    lengths,
    norm_gain,
    w_zx,
    w_bc,
    w_dt,
    conv_x,
    bias_x,
    conv_bc,
    bias_bc,
    head_params,
    gate_gain,
    w_out,
):
    is_last = lax.axis_index("pipe") == 1
    core_at = lax.axis_index("tensor")
    heads = w_dt.shape[2]
    wts = SimpleNamespace(
        norm=norm_gain,
        zx=jnp.transpose(w_zx[0], (1, 0, 2)),
        bc=w_bc[0],
        dt=jnp.pad(w_dt[0].T, ((0, LANES - heads), (0, 0))),
        cx=conv_x[0],
        bx=bias_x,
        cbc=conv_bc[0],
        bbc=bias_bc,
        hp=jnp.transpose(head_params, (1, 0, 2)),
        gate=gate_gain,
        out=w_out[0],
    )

    flag = is_last.astype(jnp.int32).reshape(1)
    core = core_at.astype(jnp.int32).reshape(1)

    lens = lengths

    def run(m, role, u, dep):
        keep = SimpleNamespace(**forward(m, role, flag, lens, core, u, wts, dep))
        keep.u = u
        keep.part = (keep.part0, keep.part1)
        keep.other = tuple(swap(v) for v in keep.part)
        keep.other_sq = swap(keep.sq)
        return keep

    def backward(m, role, keep, e, dep):
        keep.e = e
        vars(keep).update(layer_back(m, role, flag, lens, core, e, keep, wts, dep))
        share(keep)

    def share(keep):
        keep.came, keep.left = swap(keep.theirs), swap(keep.mine)

    def send_down(keep):
        result = input_send(flag, core, keep, wts)
        return relay_down(result["low"]), result["token"]

    def finish(keep, dep):
        result = input_back(core, keep, wts, dep)
        keep.du = result["du"]
        return result["token"]

    keep_a = run(0, 0, Rows(tokens, 0), (lens,))
    vars(keep_a).update(join(flag, core, keep_a, (lens,), True))
    sent_a = relay_up(keep_a.low)
    keep_b = run(1, 0, Rows(tokens, 1), keep_a.token)
    vars(keep_b).update(join(flag, core, keep_b, (sent_a,), True))
    sent_b = relay_up(keep_b.low)
    keep_c = run(0, 1, Halves(sent_a, swap(sent_a)), keep_b.token)
    sent_b = hold(sent_b, keep_c.token)
    keep_d = run(1, 1, Halves(sent_b, swap(sent_b)), keep_c.token)
    backward(0, 1, keep_c, Rows(cotangent, 0), keep_d.token)
    sent_c, token = send_down(keep_c)
    backward(1, 1, keep_d, Rows(cotangent, 1), token)
    sent_d, token = send_down(keep_d)
    backward(0, 0, keep_a, Halves(sent_c, swap(sent_c)), token)
    sent_d = hold(sent_d, keep_a.token)
    keep_b.e = Halves(sent_d, swap(sent_d))
    vars(keep_b).update(gate_back(flag, core, keep_b.e, keep_b, wts, (touch(keep_a.came, *[keep.left for keep in (keep_a, keep_c, keep_d)]),)))

    dp = lax.axis_size("dp")
    maps = partners()
    me = lax.axis_index("dp")
    tables = [
        jnp.asarray(np.stack([block_order(maps, s, late) for s in range(STREAMS)], axis=1).reshape(-1))
        for late in range(2)
    ]
    flag = jnp.stack([is_last.astype(jnp.int32), me.astype(jnp.int32) * (STREAMS * dp)])

    def both(name):
        return tuple(getattr(keep, name) for keep in (keep_c, keep_d, keep_a, keep_b))

    arrays = [both(k) for k in ("et", "n", "rt", "dz")]
    keeps, sends, token = early_grads(flag, tables[0], arrays, dp)
    gots = [send(sends[s], maps[dims_of(s, 0)[0]]) for s in range(STREAMS)]
    vars(keep_b).update(scan_back(1, flag, lens, core, keep_b, wts, (token,)))
    share(keep_b)
    arrays = [both(k) for k in ("rt", "dx", "bcdt")]
    keeps, sends, token = late_grads(flag, tables[1], arrays, dp, both("pack"), keeps, gots)
    tokens_in = [finish(keep, (token,)) for keep in (keep_a, keep_b, keep_c, keep_d)]
    join_c = SimpleNamespace(**join(flag, core, keep_c, (token,), False))
    join_d = SimpleNamespace(**join(flag, core, keep_d, (token,), False))
    deps = [[*tokens_in, join_c.token, join_d.token]]
    section_out, token_a = pick(
        flag, (join_c.res, join_d.res), (keep_a.res, keep_b.res), token
    )
    section_grad, token_b = pick(flag, (keep_c.du, keep_d.du), (keep_a.du, keep_b.du), token)
    deps += [[]]
    early, late = D // 4, D // 2
    gots = [send(sends[s], maps[dims_of(s, 1)[0]]) for s in range(STREAMS)]
    token = None
    for k in range(1, 3):
        for s in range(STREAMS):
            after = [(token,)] if token is not None else []
            if s == 0:
                after += deps[k - 1]
            keeps[s], sends[s], token = fold(s, keeps[s], gots[s], early, late, after)
            gots[s] = send(sends[s], maps[dims_of(s, 1)[k]])
        early, late = early // 2, late // 2
    keeps, sends = fold_third(keeps, gots, token_a)
    gots = [send(v, maps[d]) for v, (d, _) in zip(sends, round_groups(0))]
    dones, keeps, sends = fold_fourth(keeps, gots, token_b)
    gots = [send(v, maps[d]) for v, (d, _) in zip(sends, round_groups(1))]
    g_out, g_zx, g_dt, g_cx, g_bx, g_gate, g_heads, mine, theirs, shared = end(
        core, dones, keeps, gots, D // dp, heads
    )
    g_bc, g_norm, g_cbc, g_bbc = last_sums(mine, swap(theirs), shared, swap(shared))
    return (
        section_out[None],
        section_grad[None],
        g_norm,
        g_zx[None],
        g_bc[None],
        g_dt.T[None],
        g_cx[None],
        g_bx,
        g_cbc[None],
        g_bbc,
        g_heads[None],
        g_gate,
        g_out.T[None],
    )


def solution(mesh):
    in_specs = (
        P(None, "dp", None),
        P(None, "dp", None),
        P(None, "dp", None),
        P("pipe", None),
        P("pipe", None, None, "tensor"),
        P("pipe", None, None),
        P("pipe", None, "tensor"),
        P("pipe", None, "tensor"),
        P("pipe", "tensor"),
        P("pipe", None, None),
        P("pipe", None),
        P("pipe", None, "tensor"),
        P("pipe", "tensor"),
        P("pipe", "tensor", None),
    )
    out_specs = (
        P("pipe", None, "dp", None),
        P("pipe", None, "dp", None),
        P("pipe", None),
        P("pipe", "dp", None, "tensor"),
        P("pipe", ("dp", "tensor"), None),
        P("pipe", "dp", "tensor"),
        P("pipe", None, "tensor"),
        P("pipe", "tensor"),
        P("pipe", None, None),
        P("pipe", None),
        P("pipe", None, "tensor"),
        P("pipe", "tensor"),
        P("pipe", "tensor", "dp"),
    )
    return jax.shard_map(body, mesh=mesh, in_specs=in_specs, out_specs=out_specs, check_vma=False)
```

```python
import functools
from types import SimpleNamespace

import jax
import jax.numpy as jnp
import numpy as np
from jax import lax
from jax.experimental import pallas as pl
from jax.experimental.pallas import tpu as pltpu
from jax.sharding import PartitionSpec as P

F32 = jnp.float32
BF16 = jnp.bfloat16
EPS = 1e-05
T = 256
D = 1536
C = 1536
W = 256
STEPS = C // W
HEAD = 64
PER = W // HEAD
NS = 128
DI = 3072
LANES = 128
HALF = T // 2
NT = (((1,), (1,)), ((), ()))
VMEM_LIMIT = 24 * 1024 * 1024
SMALL_LIMIT = 16 * 1024 * 1024
COST = pl.CostEstimate(flops=1, bytes_accessed=1, transcendentals=0)


def dot(a, b):
    return jnp.dot(a, b, preferred_element_type=F32)


def dot_nt(a, b):
    return lax.dot_general(a, b, NT, preferred_element_type=F32)


def group_sums(values, group):
    terms = []
    for value in values:
        high = value.astype(BF16)
        terms += [high, (value - high.astype(F32)).astype(BF16)]
    out = dot(jnp.concatenate(terms, axis=0), group.astype(BF16))
    at, sums = 0, []
    for value in values:
        rows = value.shape[0]
        sums.append(out[at : at + rows] + out[at + rows : at + 2 * rows])
        at += 2 * rows
    return sums


def position_sums(ones, value):
    high = value.astype(BF16)
    rest = value - high.astype(F32)
    middle = rest.astype(BF16)
    low = (rest - middle.astype(F32)).astype(BF16)
    out = dot(ones.astype(BF16), jnp.concatenate([high, middle, low], axis=1))
    width = value.shape[1]
    return out[:, :width] + (out[:, width : 2 * width] + out[:, 2 * width :])


def params(steps):
    return pltpu.CompilerParams(
        dimension_semantics=("arbitrary",) * steps, vmem_limit_bytes=VMEM_LIMIT
    )


def sigmoid(v):
    return 1.0 / (1.0 + jnp.exp(-v))


def seg_ids(len_ref, micro, pos):
    end = jnp.int32(0)
    seg = jnp.zeros(pos.shape, jnp.int32)
    for k in range(4):
        end = end + len_ref[micro, 0, k]
        seg = seg + (pos >= end).astype(jnp.int32)
    return seg


def keep_masks(len_ref, micro):
    pos = lax.broadcasted_iota(jnp.int32, (T, LANES), 0)
    seg = seg_ids(len_ref, micro, pos)
    out = []
    for back in range(1, 4):
        same = (seg_ids(len_ref, micro, pos - back) == seg) & (pos >= back)
        out.append(same.astype(F32))
    return out


def wide(mask, width=W):
    return jnp.concatenate([mask] * (width // LANES), axis=1)


def conv(v, taps, bias, keeps):
    total = bias + taps[3] * v
    for back in range(1, 4):
        total = total + taps[3 - back] * (pltpu.roll(v, back, 0) * keeps[back - 1])
    return total


def conv_back(dtotal, v, taps, keeps):
    dv = taps[3] * dtotal
    grads = [None] * 4
    grads[3] = jnp.sum(dtotal * v, axis=0, keepdims=True)
    for back in range(1, 4):
        masked = dtotal * keeps[back - 1]
        grads[3 - back] = jnp.sum(masked * pltpu.roll(v, back, 0), axis=0, keepdims=True)
        dv = dv + taps[3 - back] * pltpu.roll(masked, T - back, 0)
    return dv, grads, jnp.sum(dtotal, axis=0, keepdims=True)


def rows_of(ref, count):
    return [ref[k : k + 1, :] for k in range(count)]


def tri_mask(len_ref, micro, transposed=False):
    first = lax.broadcasted_iota(jnp.int32, (T, T), 0)
    second = lax.broadcasted_iota(jnp.int32, (T, T), 1)
    same = seg_ids(len_ref, micro, first) == seg_ids(len_ref, micro, second)
    order = (second >= first) if transposed else (first >= second)
    return (same & order).astype(F32)


def lower_ones(transposed):
    first = lax.broadcasted_iota(jnp.int32, (T, T), 0)
    second = lax.broadcasted_iota(jnp.int32, (T, T), 1)
    return ((second >= first) if transposed else (first >= second)).astype(F32)


def softplus(v):
    return jnp.maximum(v, 0.0) + jnp.log1p(jnp.exp(-jnp.abs(v)))


def spread_steps(dt, cums, dt_s, cum_s, cumt_s):
    turned = cums.T
    for i in range(STEPS):
        shift = (LANES - PER * i) % LANES
        dt_s[i] = pltpu.roll(dt, shift, 1) if shift else dt
        cum_s[i] = pltpu.roll(cums, shift, 1) if shift else cums
        cumt_s[i, 0:PER, :] = turned[PER * i : PER * (i + 1), :]


def head_lanes(value, k):
    lane = lax.broadcasted_iota(jnp.int32, value.shape, 1)
    return jnp.where((lane >= k * HEAD) & (lane < (k + 1) * HEAD), value, jnp.zeros_like(value))


def per_channel(dt):
    lane = lax.broadcasted_iota(jnp.int32, dt.shape, 1)
    tiles = []
    for p in range(PER // 2):
        tiles.append(
            jnp.where(
                lane < HEAD,
                jnp.broadcast_to(dt[:, 2 * p : 2 * p + 1], dt.shape),
                jnp.broadcast_to(dt[:, 2 * p + 1 : 2 * p + 2], dt.shape),
            )
        )
    return jnp.concatenate(tiles, axis=1)


def spread_heads(hp_ref, hp_s):
    count = hp_ref.shape[2]
    hp_s[STEPS] = jnp.zeros((8, LANES), F32)
    for k in range(3):
        hp_s[STEPS, k : k + 1, 0:count] = hp_ref[k]
    value = hp_s[STEPS]
    for i in range(STEPS):
        shift = (LANES - PER * i) % LANES
        hp_s[i] = pltpu.roll(value, shift, 1) if shift else value
    return value


def skip_row(hp_s, step):
    return per_channel(hp_s[step])[2:3, :]


def full(shape):
    return pl.BlockSpec(shape, lambda i: (0,) * len(shape))


def cols(rows):
    return pl.BlockSpec((rows, W), lambda i: (0, i))


def shape_of(shape, dtype):
    return jax.ShapeDtypeStruct(shape, dtype)


def far(shape, dtype):
    return pltpu.HBM(shape, dtype)


def near(shape, dtype):
    return pltpu.VMEM(shape, dtype)


class Rows:
    def __init__(self, array, m=None):
        self.array, self.m = array, m

    def spec(self):
        if self.m is None:
            return pl.BlockSpec((T, D), lambda *i: (0, 0))
        return pl.BlockSpec((None, T, D), lambda *i: (self.m, 0, 0))


def order(dep):
    if isinstance(dep, tuple):
        return dep[0], ANY
    return from_far(dep), HBM


class Halves:
    def __init__(self, mine, other):
        self.mine, self.other = mine, other


def rows_operands(source, name="e"):
    if isinstance(source, Rows):
        return {name: (source.array, source.spec())}
    half = pl.BlockSpec((HALF, D), lambda *i: (0, 0))
    return {name + MINE: (source.mine, half), name + OTHER: (source.other, half)}


MINE, OTHER = "_mine", "_other"


def half_rows(core):
    return pl.ds(pl.multiple_of(core * HALF, HALF), HALF)


def gather_rows(R, name, target):
    if hasattr(R, name):
        target[...] = getattr(R, name)[...].astype(target.dtype)
    else:
        target[half_rows(R.core[0]), :] = getattr(R, name + MINE)[...].astype(target.dtype)
        target[half_rows(1 - R.core[0]), :] = getattr(R, name + OTHER)[...].astype(target.dtype)


def part_rows(R, name, k, at=0, count=HALF):
    if hasattr(R, name):
        first = (1 - R.core[0] if k else R.core[0]) * HALF + at
        return getattr(R, name)[pl.ds(pl.multiple_of(first, STRIP), count), :].astype(F32)
    return getattr(R, name + (OTHER if k else MINE))[pl.ds(at, count), :].astype(F32)


STRIP = 32


def strips(rows, body):
    def step(c, _):
        body(pl.multiple_of(c * STRIP, STRIP))
        return 0

    lax.fori_loop(0, rows // STRIP, step, 0)


def ours(R, role):
    return R.flag[0] == role


def from_far(value):
    return pltpu.with_memory_space_constraint(value, pltpu.HBM)


TOKEN = (8, LANES)


SMEM = pl.BlockSpec(memory_space=pltpu.SMEM)
VMEM = pl.BlockSpec(memory_space=pltpu.VMEM)
ANY = pl.BlockSpec(memory_space=pl.ANY)
HBM = pl.BlockSpec(memory_space=pltpu.HBM)


def call(body, ins, outs, scratch, name, grid=(STEPS,), limit=VMEM_LIMIT):
    names = [*ins, *outs, *scratch]

    def kernel(*refs):
        body(SimpleNamespace(**dict(zip(names, refs))))

    values = pl.pallas_call(
        kernel,
        grid=grid,
        in_specs=[v[1] for v in ins.values()],
        out_specs=[v[1] for v in outs.values()],
        out_shape=tuple(v[0] for v in outs.values()),
        scratch_shapes=list(scratch.values()),
        compiler_params=pltpu.CompilerParams(
            dimension_semantics=("arbitrary",) * len(grid), vmem_limit_bytes=limit
        ),
        cost_estimate=COST,
        name=name,
    )(*[v[0] for v in ins.values()])
    return dict(zip(outs, values))


def scan_scratch():
    return dict(
        keep_s=pltpu.VMEM((3, T, LANES), F32),
        dt_s=pltpu.VMEM((STEPS, T, LANES), F32),
        cum_s=pltpu.VMEM((STEPS, T, LANES), F32),
        cumt_s=pltpu.VMEM((STEPS, 8, T), F32),
        hp_s=pltpu.VMEM((STEPS + 1, 8, LANES), F32),
        acc_s=pltpu.VMEM((T, D), F32),
    )


def forward_kernel(micro, R):
    step = pl.program_id(0)

    @pl.when(step == 0)
    def _():
        if not hasattr(R, "u"):
            gather_rows(R, "u", R.u_s)
        u = (R.u if hasattr(R, "u") else R.u_s)[...].astype(F32)
        s_zero = lax.rsqrt(jnp.mean(u * u, axis=1, keepdims=True) + EPS)
        low = (u * s_zero * R.norm[...]).astype(BF16)
        R.r_s[...] = low
        R.rt[...] = low.T
        keeps = keep_masks(R.lens, micro)
        for k in range(3):
            R.keep_s[k] = keeps[k]
        bcr = dot(low, R.bc[...])
        R.bcr[...] = bcr
        dtr = dot_nt(low, R.dt[...])
        R.dtr[...] = dtr
        total = conv(bcr, rows_of(R.cbc, 4), R.bbc[...], [wide(k, 2 * NS) for k in keeps])
        act = total * sigmoid(total)
        score = dot_nt(act[:, NS:].astype(BF16), act[:, :NS].astype(BF16)) * tri_mask(R.lens, micro)
        R.score_s[...] = score
        R.scoret[...] = score.T
        hp = spread_heads(R.hp, R.hp_s)
        dt = softplus(dtr + hp[0:1, :])
        rates = dt * (-jnp.exp(hp[1:2, :]))
        cums = position_sums(lower_ones(False), rates)
        R.cums[...] = cums
        spread_steps(dt, cums, R.dt_s, R.cum_s, R.cumt_s)
        R.acc_s[...] = jnp.zeros_like(R.acc_s)
        R.sq[...] = jnp.zeros_like(R.sq)

    keeps = [wide(R.keep_s[k]) for k in range(3)]
    low_z = dot(R.r_s[...], R.zx[0]).astype(BF16)
    low_x = dot(R.r_s[...], R.zx[1]).astype(BF16)
    R.z[...] = low_z
    R.x[...] = low_x
    z = low_z.astype(F32)
    x = low_x.astype(F32)
    total = conv(x, rows_of(R.cx, 4), R.bx[...], keeps)
    xc = total * sigmoid(total)
    cums = R.cum_s[step]
    cumt = R.cumt_s[step]
    xt = (xc * per_channel(R.dt_s[step])).astype(BF16)
    R.xt[...] = xt
    top = jnp.zeros((HALF, W), F32)
    bottom = jnp.zeros((HALF, W), F32)
    for k in range(PER):
        mine = head_lanes(xt, k)
        col = cums[:, k : k + 1]
        row = cumt[k : k + 1, :]
        mix = R.score_s[0:HALF, 0:HALF] * jnp.exp(jnp.minimum(col[:HALF] - row[:, :HALF], 0.0))
        top = top + dot(mix.astype(BF16), mine[:HALF])
        mix = R.score_s[HALF:T, :] * jnp.exp(jnp.minimum(col[HALF:] - row, 0.0))
        bottom = bottom + dot(mix.astype(BF16), mine)
    y = jnp.concatenate([top, bottom], axis=0) + skip_row(R.hp_s, step) * xc
    R.y[...] = y
    g = y * (z * sigmoid(z))
    squares = g * g
    for k in range(W // LANES):
        R.sq[...] += squares[:, k * LANES : (k + 1) * LANES]
    R.acc_s[...] += dot((g * R.gate[...]).astype(BF16), R.out[...])

    @pl.when(step == STEPS - 1)
    def _():
        R.part0[...] = R.acc_s[:HALF, :].astype(BF16)
        R.part1[...] = R.acc_s[HALF:, :].astype(BF16)
        R.token[...] = jnp.zeros(TOKEN, F32)


def small_operands(wts):
    return dict(
        bc=(wts.bc, full((D, 2 * NS))),
        dt=(wts.dt, full((LANES, D))),
        cx=(from_far(wts.cx), cols(4)),
        bx=(from_far(wts.bx), cols(1)),
        cbc=(from_far(wts.cbc), full((4, 2 * NS))),
        bbc=(from_far(wts.bbc), full((1, 2 * NS))),
        hp=(from_far(wts.hp), full(wts.hp.shape)),
    )


def forward(micro, role, flag, lens, core, u, wts, dep):
    def kernel(R):
        @pl.when(R.flag[0] != role)
        def _():
            for ref in (R.part0, R.part1, R.sq, R.token):
                ref[...] = jnp.zeros_like(ref)

        pl.when(ours(R, role))(lambda: forward_kernel(micro, R))

    ins = rows_operands(u, "u") | dict(
        flag=(flag, SMEM),
        core=(core, SMEM),
        lens=(lens, SMEM),
        norm=(from_far(wts.norm), full((1, D))),
        zx=(from_far(wts.zx), pl.BlockSpec((2, D, W), lambda i: (0, 0, i))),
        out=(from_far(wts.out), pl.BlockSpec((W, D), lambda i: (i, 0))),
        gate=(from_far(wts.gate), cols(1)),
        **small_operands(wts),
        dep=order(dep),
    )
    outs = dict(
        rt=(far((D, T), BF16), full((D, T))),
        z=(far((T, C), BF16), cols(T)),
        x=(far((T, C), BF16), cols(T)),
        y=(far((T, C), F32), cols(T)),
        bcr=(far((T, 2 * NS), F32), full((T, 2 * NS))),
        dtr=(far((T, LANES), F32), full((T, LANES))),
        part0=(shape_of((HALF, D), BF16), full((HALF, D))),
        part1=(shape_of((HALF, D), BF16), full((HALF, D))),
        sq=(shape_of((T, LANES), F32), full((T, LANES))),
        xt=(far((T, C), BF16), cols(T)),
        scoret=(far((T, T), F32), full((T, T))),
        cums=(far((T, LANES), F32), full((T, LANES))),
        token=(far(TOKEN, F32), full(TOKEN)),
    )
    scratch = scan_scratch() | dict(
        r_s=pltpu.VMEM((T, D), BF16),
        u_s=pltpu.VMEM((T, D), BF16),
        score_s=pltpu.VMEM((T, T), F32),
    )
    return call(kernel, ins, outs, scratch, "layer_forward")


def touch_kernel(*refs):
    refs[-1][...] = jnp.zeros(TOKEN, F32)


def touch(*values):
    return pl.pallas_call(
        touch_kernel,
        in_specs=[ANY] * len(values),
        out_specs=VMEM,
        out_shape=shape_of(TOKEN, F32),
        compiler_params=pltpu.CompilerParams(vmem_limit_bytes=SMALL_LIMIT),
        cost_estimate=COST,
        name="touch",
    )(*values)


def scale_of(sq0_ref, sq1_ref):
    squares = jnp.sum(sq0_ref[...] + sq1_ref[...], axis=1, keepdims=True)
    return lax.rsqrt(squares / DI + EPS)


def join_rows(mine, others):
    halves = [a[...].astype(F32) + b[...].astype(F32) for a, b in zip(mine, others)]
    return jnp.concatenate(halves, axis=0)


def join(flag, core, keep, dep, first):
    def second(R):
        gather_rows(R, "u", R.res)
        for k, (own, other) in enumerate(((R.p0, R.o0), (R.p1, R.o1))):

            def strip(at):
                here, span = pl.ds(at, STRIP), pl.ds(pl.multiple_of(k * HALF + at, STRIP), STRIP)
                squares = jnp.sum(R.sq0[span, :] + R.sq1[span, :], axis=1, keepdims=True)
                scale = lax.rsqrt(squares / DI + EPS)
                total = own[here, :].astype(F32) + other[here, :].astype(F32)
                R.res[span, :] = R.res[span, :] + scale * total

            strips(HALF, strip)

    def body(R):
        if not first:
            return second(R)
        scale = scale_of(R.sq0, R.sq1)
        total = join_rows((R.p0, R.p1), (R.o0, R.o1))
        gather_rows(R, "u", R.res)
        res = R.res[...] + scale * total
        R.res[...] = res.astype(BF16).astype(F32)
        R.low[...] = R.res[half_rows(R.core[0]), :].astype(BF16)
        R.total[...] = total.astype(BF16)
        R.scale[...] = jnp.broadcast_to(scale, (T, LANES))

    def kernel(R):
        R.token[...] = jnp.zeros(TOKEN, F32)
        pl.when(ours(R, 0 if first else 1))(lambda: body(R))

    ins = rows_operands(keep.u, "u") | dict(
        flag=(flag, SMEM),
        core=(core, SMEM),
        p0=(keep.part[0], VMEM),
        p1=(keep.part[1], VMEM),
        o0=(keep.other[0], VMEM),
        o1=(keep.other[1], VMEM),
        sq0=(keep.sq, VMEM),
        sq1=(keep.other_sq, VMEM),
        dep=order(dep),
    )
    outs = dict(res=(far((T, D), F32), full((T, D))), token=(far(TOKEN, F32), full(TOKEN)))
    if first:
        outs |= dict(
            low=(shape_of((HALF, D), BF16), VMEM),
            total=(far((T, D), BF16), full((T, D))),
            scale=(far((T, LANES), F32), full((T, LANES))),
        )
    return call(kernel, ins, outs, {}, "join_output", grid=(1,), limit=SMALL_LIMIT)


def gate_begin(R):
    gather_rows(R, "e", R.e_s)
    e = R.e_s[...].astype(F32)
    if hasattr(R, "total"):
        scale = R.scale[:, 0:1]
        total = R.total[...].astype(F32)
    else:
        scale = scale_of(R.sq0, R.sq1)
        total = join_rows((R.p0, R.p1), (R.o0, R.o1))
    inner = jnp.sum(e * total, axis=1, keepdims=True)
    R.scale_s[...] = jnp.broadcast_to(scale, (T, LANES))
    R.inner_s[...] = jnp.broadcast_to(inner * (scale * scale * scale) / DI, (T, LANES))
    R.et[...] = R.e_s[...].T


def gate_block(R):
    scale = wide(R.scale_s[...])
    z = R.z[...].astype(F32)
    y = R.y[...]
    gg = R.gate[...]
    dn = dot_nt(R.e_s[...], R.out[...])
    sig = sigmoid(z)
    act = z * sig
    g = y * act
    normed = g * scale
    R.n[...] = (normed * gg).astype(BF16)
    dg = scale * (gg * dn) - g * wide(R.inner_s[...])
    R.dz[...] = (dg * y * (sig * (1.0 + z * (1.0 - sig)))).astype(BF16)
    return y, (dg * act).astype(BF16), jnp.sum(normed * dn, axis=0, keepdims=True)


def scan_begin(micro, R):
    keeps = keep_masks(R.lens, micro)
    for k in range(3):
        R.keep_s[k] = keeps[k]
    hp = spread_heads(R.hp, R.hp_s)
    spread_steps(softplus(R.dtr[...] + hp[0:1, :]), R.cums[...], R.dt_s, R.cum_s, R.cumt_s)
    for ref in (R.acc_s, R.dscore_s, R.dcum_s, R.ddt_s, R.dskip_s):
        ref[...] = jnp.zeros_like(ref)


def scan_block(R, step, y, dyb, ggrad):
    keeps = [wide(R.keep_s[k]) for k in range(3)]
    taps = rows_of(R.cx, 4)
    x = R.x[...].astype(F32)
    total = conv(x, taps, R.bx[...], keeps)
    sig = sigmoid(total)
    xc = total * sig
    cums = R.cum_s[step]
    cumt = R.cumt_s[step]
    dtb = per_channel(R.dt_s[step])
    xt = R.xt[...]
    skip = skip_row(R.hp_s, step)
    inside = y - skip * xc
    top = jnp.zeros((HALF, W), F32)
    bottom = jnp.zeros((HALF, W), F32)
    for k in range(PER):
        my_dy = head_lanes(dyb, k)
        my_x = head_lanes(xt, k)
        col = cums[:, k : k + 1]
        row = cumt[k : k + 1, :]
        decay = jnp.exp(jnp.minimum(row - col[:HALF], 0.0))
        mix = R.scoret[0:HALF, :] * decay
        top = top + dot(mix.astype(BF16), my_dy)
        R.dscore_s[0:HALF, :] += dot_nt(my_x[:HALF], dyb) * decay
        decay = jnp.exp(jnp.minimum(row[:, HALF:] - col[HALF:], 0.0))
        mix = R.scoret[HALF:T, HALF:T] * decay
        bottom = bottom + dot(mix.astype(BF16), my_dy[HALF:])
        R.dscore_s[HALF:T, HALF:T] += dot_nt(my_x[HALF:], dyb[HALF:]) * decay
    dxt = jnp.concatenate([top, bottom], axis=0)
    chan = (lax.broadcasted_iota(jnp.int32, (W, LANES), 0) >> 6) + PER * step
    lane = lax.broadcasted_iota(jnp.int32, (W, LANES), 1)
    group = (chan == lane).astype(F32)
    dy = dyb.astype(F32)
    dxc = dtb * dxt + skip * dy
    dskip = jnp.broadcast_to(jnp.sum(dy * xc, axis=0, keepdims=True), (16, W))
    sums = group_sums([dy * inside - xt.astype(F32) * dxt, xc * dxt, dskip], group)
    R.dcum_s[...] += sums[0]
    R.ddt_s[...] += sums[1]
    R.dskip_s[...] += sums[2][:8]
    dtotal = dxc * (sig * (1.0 + total * (1.0 - sig)))
    dx, grads, dbias = conv_back(dtotal, x, taps, keeps)
    here = pl.ds(pl.multiple_of(step * W, W), W)
    for k, value in enumerate(grads + [dbias, ggrad]):
        R.pack[k : k + 1, here] = value
    low = dx.astype(BF16)
    R.dx[...] = low
    R.acc_s[...] += dot_nt(R.dz[...], R.zx[0]) + dot_nt(low, R.zx[1])


def scan_end(micro, R):
    keeps = [wide(R.keep_s[k], 2 * NS) for k in range(3)]
    bcr = R.bcr[...]
    taps = rows_of(R.cbc, 4)
    total = conv(bcr, taps, R.bbc[...], keeps)
    sig = sigmoid(total)
    act = total * sig
    dscore = R.dscore_s[...] * tri_mask(R.lens, micro, True)
    db = dot(dscore.astype(BF16), act[:, NS:].astype(BF16))
    dc = dot(dscore.T.astype(BF16), act[:, :NS].astype(BF16))
    dact = jnp.concatenate([db, dc], axis=1)
    dtotal = dact * (sig * (1.0 + total * (1.0 - sig)))
    dbc, grads, dbias = conv_back(dtotal, bcr, taps, keeps)
    for k, value in enumerate(grads + [dbias]):
        R.pack[7:8, 2 * NS * k : 2 * NS * (k + 1)] = value
    hp = R.hp_s[STEPS]
    pre = R.dtr[...] + hp[0:1, :]
    decay_rate = -jnp.exp(hp[1:2, :])
    dt = softplus(pre)
    drates = position_sums(lower_ones(True), R.dcum_s[...])
    heads = R.hp.shape[2]
    lane = lax.broadcasted_iota(jnp.int32, (T, LANES), 1)
    ddt = (R.ddt_s[...] + drates * decay_rate) * sigmoid(pre)
    ddt = jnp.where(lane < heads, ddt, 0.0)
    shift = jnp.sum(ddt, axis=0, keepdims=True)
    decay = jnp.sum(drates * dt, axis=0, keepdims=True) * decay_rate
    decay = jnp.where(lane[0:1] < heads, decay, 0.0)
    both = jnp.concatenate([shift, decay, R.dskip_s[2:8, :]], axis=0)
    tile = both[0:1] + pltpu.roll(both, 32, 1)[1:2] + pltpu.roll(both, 64, 1)[2:3]
    R.pack[7:8, 10 * NS : 11 * NS] = tile
    R.pack[7:8, 11 * NS :] = jnp.zeros((1, NS), F32)
    low_bc = dbc.astype(BF16)
    low_dt = ddt.astype(BF16)
    R.bcdt[:, : 2 * NS] = low_bc
    R.bcdt[:, 2 * NS :] = low_dt
    out = R.acc_s[...] + dot_nt(low_bc, R.bc[...]) + dot(low_dt, R.dt[...])
    R.acc_s[...] = out
    R.mine[...] = R.acc_s[half_rows(R.core[0]), :].astype(BF16)
    R.theirs[...] = R.acc_s[half_rows(1 - R.core[0]), :].astype(BF16)
    gather_rows(R, "u", R.u_s)
    u = R.u_s[...].astype(F32)
    s_zero = lax.rsqrt(jnp.mean(u * u, axis=1, keepdims=True) + EPS)
    R.pack[6:7, :] = jnp.sum(u * s_zero * out, axis=0, keepdims=True)
    R.token[...] = jnp.zeros(TOKEN, F32)


def gate_operands(e, keep, wts):
    ins = rows_operands(e) | dict(
        z=(from_far(keep.z), cols(T)),
        y=(from_far(keep.y), cols(T)),
        gate=(from_far(wts.gate), cols(1)),
        out=(from_far(wts.out), pl.BlockSpec((W, D), lambda i: (i, 0))),
    )
    if hasattr(keep, "total"):
        return ins | dict(
            total=(from_far(keep.total), full((T, D))), scale=(from_far(keep.scale), full((T, LANES)))
        )
    part, other = keep.part, keep.other
    ins |= dict(
        p0=(part[0], full((HALF, D))),
        p1=(part[1], full((HALF, D))),
        o0=(other[0], full((HALF, D))),
        o1=(other[1], full((HALF, D))),
        sq0=(keep.sq, full((T, LANES))),
        sq1=(keep.other_sq, full((T, LANES))),
    )
    return ins


def gate_results():
    return dict(
        et=(far((D, T), BF16), full((D, T))),
        n=(far((T, C), BF16), cols(T)),
        dz=(far((T, C), BF16), cols(T)),
    )


GATE_SCRATCH = dict(
    e_s=pltpu.VMEM((T, D), BF16), scale_s=pltpu.VMEM((T, LANES), F32), inner_s=pltpu.VMEM((T, LANES), F32))


def scan_operands(lens, core, keep, wts):
    return rows_operands(keep.u, "u") | dict(
        lens=(lens, SMEM),
        core=(core, SMEM),
        x=(from_far(keep.x), cols(T)),
        xt=(from_far(keep.xt), cols(T)),
        bcr=(from_far(keep.bcr), full((T, 2 * NS))),
        dtr=(from_far(keep.dtr), full((T, LANES))),
        scoret=(from_far(keep.scoret), full((T, T))),
        cums=(from_far(keep.cums), full((T, LANES))),
        zx=(from_far(wts.zx), pl.BlockSpec((2, D, W), lambda i: (0, 0, i))),
        **small_operands(wts),
    )


def scan_results():
    return dict(
        dx=(far((T, C), BF16), cols(T)),
        bcdt=(far((T, 3 * LANES), BF16), full((T, 3 * LANES))),
        mine=(shape_of((HALF, D), BF16), full((HALF, D))),
        theirs=(shape_of((HALF, D), BF16), full((HALF, D))),
        pack=(far((PACK, C), F32), full((PACK, C))),
        token=(far(TOKEN, F32), full(TOKEN)),
    )


def back_scratch():
    return scan_scratch() | dict(
        dscore_s=pltpu.VMEM((T, T), F32),
        dcum_s=pltpu.VMEM((T, LANES), F32),
        ddt_s=pltpu.VMEM((T, LANES), F32),
        dskip_s=pltpu.VMEM((8, LANES), F32),
        u_s=pltpu.VMEM((T, D), BF16),
    )


def gate_back(flag, core, e, keep, wts, dep):
    def body(R):
        pl.when(pl.program_id(0) == 0)(lambda: gate_begin(R))
        _, R.dy[...], R.ggrad[...] = gate_block(R)

    ins = gate_operands(e, keep, wts) | dict(flag=(flag, SMEM), core=(core, SMEM), dep=order(dep))
    outs = gate_results() | dict(dy=(far((T, C), BF16), cols(T)), ggrad=(far((1, C), F32), cols(1)))
    return call(
        lambda R: pl.when(ours(R, 0))(lambda: body(R)), ins, outs, GATE_SCRATCH, "gate_backward"
    )


def no_rows(R):
    for ref in (R.mine, R.theirs, R.token):
        ref[...] = jnp.zeros_like(ref)


def scan_back(micro, flag, lens, core, keep, wts, dep):
    def body(R):
        step = pl.program_id(0)
        pl.when(step == 0)(lambda: scan_begin(micro, R))
        scan_block(R, step, R.y[...], R.dy[...], R.ggrad[...])
        pl.when(step == STEPS - 1)(lambda: scan_end(micro, R))

    def kernel(R):
        pl.when(R.flag[0] != 0)(lambda: no_rows(R))
        pl.when(ours(R, 0))(lambda: body(R))

    ins = scan_operands(lens, core, keep, wts) | dict(
        flag=(flag, SMEM),
        y=(from_far(keep.y), cols(T)),
        dy=(from_far(keep.dy), cols(T)),
        dz=(from_far(keep.dz), cols(T)),
        ggrad=(from_far(keep.ggrad), cols(1)),
        dep=order(dep),
    )
    return call(kernel, ins, scan_results(), back_scratch(), "scan_backward")


def layer_back(micro, role, flag, lens, core, e, keep, wts, dep):
    def body(R):
        step = pl.program_id(0)

        @pl.when(step == 0)
        def _():
            gate_begin(R)
            scan_begin(micro, R)

        scan_block(R, step, *gate_block(R))
        pl.when(step == STEPS - 1)(lambda: scan_end(micro, R))

    def kernel(R):
        pl.when(R.flag[0] != role)(lambda: no_rows(R))
        pl.when(ours(R, role))(lambda: body(R))

    ins = dict(flag=(flag, SMEM), **gate_operands(e, keep, wts), **scan_operands(lens, core, keep, wts))
    return call(
        kernel,
        ins | dict(dep=order(dep)),
        gate_results() | scan_results(),
        back_scratch() | GATE_SCRATCH,
        "layer_backward",
    )


def input_rows(R, e, u, dr):
    s_zero = lax.rsqrt(jnp.mean(u * u, axis=1, keepdims=True) + EPS)
    gained = R.norm[...] * dr
    shared = s_zero * s_zero * s_zero * jnp.mean(u * gained, axis=1, keepdims=True)
    return e + s_zero * gained - u * shared


def input_send(flag, core, keep, wts):
    def body(R):
        dr = R.mine[...].astype(F32) + R.came[...].astype(F32)
        R.low[...] = input_rows(R, part_rows(R, "e", 0), part_rows(R, "u", 0), dr).astype(BF16)

    def kernel(R):
        R.token[...] = jnp.zeros(TOKEN, F32)
        pl.when(ours(R, 1))(lambda: body(R))

    ins = rows_operands(keep.e) | rows_operands(keep.u, "u") | dict(
        flag=(flag, SMEM),
        core=(core, SMEM),
        norm=(from_far(wts.norm), full((1, D))),
        mine=(keep.mine, VMEM),
        came=(keep.came, VMEM),
    )
    outs = dict(low=(shape_of((HALF, D), BF16), VMEM), token=(far(TOKEN, F32), full(TOKEN)))
    return call(kernel, ins, outs, {}, "input_send", grid=(1,), limit=SMALL_LIMIT)


def input_back(role, flag, core, keep, wts, dep):
    def body(R):
        for k, (own, other) in enumerate(((R.mine, R.came), (R.theirs, R.left))):

            def strip(at):
                span = pl.ds(at, STRIP)
                dr = own[span, :].astype(F32) + other[span, :].astype(F32)
                e, u = part_rows(R, "e", k, at, STRIP), part_rows(R, "u", k, at, STRIP)
                first = (1 - R.core[0] if k else R.core[0]) * HALF + at
                R.du[pl.ds(pl.multiple_of(first, STRIP), STRIP), :] = input_rows(R, e, u, dr)

            strips(HALF, strip)

    def kernel(R):
        R.token[...] = jnp.zeros(TOKEN, F32)
        pl.when(ours(R, role))(lambda: body(R))

    ins = rows_operands(keep.e) | rows_operands(keep.u, "u") | dict(
        flag=(flag, SMEM),
        core=(core, SMEM),
        norm=(from_far(wts.norm), full((1, D))),
        mine=(keep.mine, full((HALF, D))),
        came=(keep.came, full((HALF, D))),
        theirs=(keep.theirs, full((HALF, D))),
        left=(keep.left, full((HALF, D))),
        dep=order(dep),
    )
    outs = dict(du=(far((T, D), F32), full((T, D))), token=(far(TOKEN, F32), full(TOKEN)))
    return call(kernel, ins, outs, {}, "input_backward", grid=(1,), limit=SMALL_LIMIT)


def hold(value, dep):
    def kernel(R):
        R.out[...] = R.value[...]

    ins = dict(value=(value, VMEM), dep=order(dep))
    outs = dict(out=(shape_of(value.shape, value.dtype), VMEM))
    return call(kernel, ins, outs, {}, "hold", grid=(1,), limit=SMALL_LIMIT)["out"]


def swap(value):
    return lax.ppermute(value, "tensor", [(0, 1), (1, 0)])


def relay_up(value):
    return lax.ppermute(value, "pipe", [(0, 1)])


def relay_down(value):
    return lax.ppermute(value, "pipe", [(1, 0)])


def partners():
    def make(fn):
        return [fn(i // 8, (i // 2) % 4, i % 2) for i in range(32)]

    def pack(y, x, z):
        return y * 8 + x * 2 + z

    def wrap(v):
        return (v + 1) % 4 if v % 2 else (v - 1) % 4

    return [
        make(lambda y, x, z: pack(y, x ^ 1, z)),
        make(lambda y, x, z: pack(y ^ 1, x, z)),
        make(lambda y, x, z: pack(y, wrap(x), z)),
        make(lambda y, x, z: pack(wrap(y), x, z)),
        make(lambda y, x, z: pack(y, x, z ^ 1)),
    ]


STREAMS = 5


LAST = ((0, 4), (0, 1), (2, 1), (2, 3), (3, 4))


def dims_of(stream, late):
    if late:
        return [(stream + k) % 5 for k in range(1, 4)] + list(LAST[stream])
    return [(stream + k) % 5 for k in range(5)]


def ends_first(s):
    return dims_of(s, 0)[4] == LAST[s][0]


def round_groups(which):
    dims = sorted({last[which] for last in LAST})
    return [(d, [s for s in range(5) if LAST[s][which] == d]) for d in dims]


def block_order(maps, stream, late=0):
    order = [maps[d] for d in dims_of(stream, late)]
    count = len(order[0])
    table = np.zeros((count, count), np.int32)
    for me in range(count):
        for p in range(count):
            owner = me
            for k, step in enumerate(order):
                if (p >> (len(order) - 1 - k)) & 1:
                    owner = step[owner]
            table[me, p] = owner
    return table


TILES_EARLY = [("et", "n", LANES * k) for k in range(C // LANES)] + [
    ("rt", "dz", LANES * k) for k in range(C // LANES)
]
TILES_LATE = [("rt", "dx", LANES * k) for k in range(C // LANES)] + [
    ("rt", "bcdt", LANES * k) for k in range(3)
]


def deal(tiles, sizes):
    return [tiles[sum(sizes[:s]) : sum(sizes[: s + 1])] for s in range(STREAMS)]


EARLY, LATE = deal(TILES_EARLY, (5, 5, 5, 4, 5)), deal(TILES_LATE, (3, 3, 3, 3, 3))
PACK = 8
PACK_ROWS = 2 * PACK * (C // LANES)
PACK_STREAM = 3


def runs(tiles):
    out = []
    for at, (left, right, first) in enumerate(tiles):
        if out and out[-1][:2] == [left, right] and out[-1][2] + LANES * out[-1][3] == first:
            out[-1][3] += 1
        else:
            out.append([left, right, first, 1, at])
    return out


class Loader:
    def __init__(self, flag_ref, names, sources, held, sem):
        self.flag, self.names, self.sources, self.held, self.sem = flag_ref, names, sources, held, sem
        self.waited = set()

    def copy(self, k, m, early):
        span = pl.ds(m * T, T)
        ref = self.held[k]
        slot = ref.at[:, span] if ref.shape[0] == D else ref.at[span, :]
        return pltpu.make_async_copy(self.sources[4 * k + 2 * early + m], slot, self.sem.at[2 * k + m])

    def start(self, name):
        k = self.names.index(name)
        for m in range(2):
            pl.when(self.flag[0] == 1)(lambda: self.copy(k, m, 0).start())
            pl.when(self.flag[0] == 0)(lambda: self.copy(k, m, 1).start())

    def get(self, name):
        k = self.names.index(name)
        if name not in self.waited:
            self.waited.add(name)
            for m in range(2):
                self.copy(k, m, 0).wait()
        return self.held[k]


def held_shapes(arrays):
    shapes = []
    for a in arrays:
        rows, columns = a[0].shape
        shapes.append(pltpu.VMEM((rows, 2 * columns) if rows == D else (2 * rows, columns), BF16))
    return shapes


def products(loader, lefts, tiles, blocks, owner_of, place):
    rows, half, chunk = D // blocks, D // 2, 384
    placed = []
    for left, right, first, count, at in runs(tiles):
        held, rhs = loader.get(left), loader.get(right)
        if left not in placed:
            placed.append(left)
            for p in range(blocks):
                start = pl.multiple_of(owner_of(p) * rows, 16)
                lefts[len(placed) - 1, p * rows : (p + 1) * rows, :] = held[pl.ds(start, rows), :]
        slot = placed.index(left)
        for side in range(2):
            for row in range(0, half, chunk):
                span = slice(side * half + row, side * half + row + chunk)
                value = dot(lefts[slot, span, :], rhs[:, first : first + LANES * count]).astype(BF16)
                for j in range(count):
                    place(side, at + j, row, value[:, j * LANES : (j + 1) * LANES])


def early_kernel(blocks, flag_ref, table_ref, *refs):
    names = ["et", "n", "rt", "dz"]
    sources, refs = refs[:16], refs[16:]
    outs, token_ref = refs[: 2 * STREAMS], refs[2 * STREAMS]
    held, lefts, in_sem = refs[2 * STREAMS + 1 :]
    loader = Loader(flag_ref, names, sources, held, in_sem)
    for name in names:
        loader.start(name)
    for s in range(STREAMS):

        def place(side, tile, row, value):
            outs[2 * s + side][tile, row : row + value.shape[0], :] = value

        def owner_of(p):
            return table_ref[flag_ref[1] + s * blocks + p]

        products(loader, lefts, EARLY[s], blocks, owner_of, place)
    token_ref[...] = jnp.zeros(TOKEN, F32)


def early_grads(flag, table, arrays, blocks):
    out = []
    for s in range(STREAMS):
        out += [near((len(EARLY[s]), D // 2, LANES), BF16)] * 2
    flat = pl.pallas_call(
        functools.partial(early_kernel, blocks),
        in_specs=[SMEM, SMEM] + [HBM] * 16,
        out_specs=[VMEM] * (len(out) + 1),
        out_shape=tuple(out) + (shape_of(TOKEN, F32),),
        scratch_shapes=[
            held_shapes(arrays),
            pltpu.VMEM((2, D, 2 * T), BF16),
            pltpu.SemaphoreType.DMA((8,)),
        ],
        compiler_params=pltpu.CompilerParams(vmem_limit_bytes=VMEM_LIMIT),
        cost_estimate=COST,
        name="grad_early",
    )(flag, table, *[from_far(v) for a in arrays for v in a])
    return list(flat[0:-1:2]), list(flat[1:-1:2]), flat[-1]


def total_rows(s, early, late):
    return len(EARLY[s]) * early + len(LATE[s]) * late + (PACK_ROWS if s == PACK_STREAM else 0)


def split_pair(value):
    high = value.astype(BF16)
    return jnp.concatenate([high, (value - high.astype(F32)).astype(BF16)], axis=0)


def join_pair(pair):
    wide_pair = pair.astype(F32)
    return wide_pair[:PACK] + wide_pair[PACK:]


def late_kernel(blocks, flag_ref, table_ref, *refs):
    names = ["rt", "dx", "bcdt"]
    sources, refs = refs[:12], refs[12:]
    packs, refs = refs[:4], refs[4:]
    keeps, gots, refs = refs[:STREAMS], refs[STREAMS : 2 * STREAMS], refs[2 * STREAMS :]
    outs, token_ref = refs[: 2 * STREAMS], refs[2 * STREAMS]
    held, lefts, in_sem = refs[2 * STREAMS + 1 :]
    loader = Loader(flag_ref, names, sources, held, in_sem)
    for name in names:
        loader.start(name)
    half = D // 2
    quarter = half // 2
    for s in range(STREAMS):
        for j in range(len(EARLY[s])):
            for side in range(2):
                span = slice(side * quarter, (side + 1) * quarter)
                total = keeps[s][j, span, :].astype(F32) + gots[s][j, span, :].astype(F32)
                outs[2 * s + side][j * quarter : (j + 1) * quarter, :] = total.astype(BF16)
    last = flag_ref[0] == 1
    total = jnp.where(last, packs[0][...] + packs[1][...], packs[2][...] + packs[3][...])
    for j in range(C // LANES):
        pair = split_pair(total[:, j * LANES : (j + 1) * LANES])
        at = total_rows(PACK_STREAM, quarter, half) - PACK_ROWS + 2 * PACK * j
        for side in range(2):
            outs[2 * PACK_STREAM + side][at : at + 2 * PACK, :] = pair
    for s in range(STREAMS):
        base = len(EARLY[s]) * quarter

        def place(side, tile, row, value):
            at = base + tile * half + row
            outs[2 * s + side][at : at + value.shape[0], :] = value

        def owner_of(p):
            return table_ref[flag_ref[1] + s * blocks + p]

        products(loader, lefts, LATE[s], blocks, owner_of, place)
    token_ref[...] = jnp.zeros(TOKEN, F32)


def late_grads(flag, table, arrays, blocks, packs, keeps, gots):
    out = []
    for s in range(STREAMS):
        out += [near((total_rows(s, D // 4, D // 2), LANES), BF16)] * 2
    flat = pl.pallas_call(
        functools.partial(late_kernel, blocks),
        in_specs=[SMEM, SMEM] + [HBM] * 12 + [VMEM] * (4 + 2 * STREAMS),
        out_specs=[VMEM] * (len(out) + 1),
        out_shape=tuple(out) + (shape_of(TOKEN, F32),),
        scratch_shapes=[
            held_shapes(arrays),
            pltpu.VMEM((1, D, 2 * T), BF16),
            pltpu.SemaphoreType.DMA((6,)),
        ],
        compiler_params=pltpu.CompilerParams(vmem_limit_bytes=VMEM_LIMIT),
        cost_estimate=COST,
        name="grad_late",
    )(
        flag,
        table,
        *[from_far(v) for a in arrays for v in a],
        *packs,
        *keeps,
        *gots,
    )
    return list(flat[0:-1:2]), list(flat[1:-1:2]), flat[-1]


def fold(s, keep, got, early, late, deps):
    def kernel(keep, got, *refs):
        next_keep, next_send, token = refs[len(pairs) :]
        at = to = 0
        for rows, tiles in ((early, EARLY[s]), (late, LATE[s])):
            for _ in tiles:
                next_send[to : to + rows // 2, :] = add(keep, got, at + rows // 2, rows // 2).astype(BF16)
                next_keep[to : to + rows // 2, :] = add(keep, got, at, rows // 2).astype(BF16)
                at += rows
                to += rows // 2
        if s == PACK_STREAM:
            add_packs((keep, at), (got, at), ((next_keep, to), (next_send, to)))
        token[...] = jnp.zeros(TOKEN, F32)

    pairs = [order(dep) for dep in deps]
    rows = total_rows(s, early // 2, late // 2)
    out = [near((rows, LANES), BF16), near((rows, LANES), BF16), near(TOKEN, F32)]
    return pl.pallas_call(
        kernel,
        in_specs=[VMEM] * 2 + [spec for _, spec in pairs],
        out_specs=[VMEM, VMEM, VMEM],
        out_shape=tuple(out),
        compiler_params=pltpu.CompilerParams(vmem_limit_bytes=SMALL_LIMIT),
        cost_estimate=COST,
        name="fold_grads",
    )(keep, got, *[value for value, _ in pairs])


def add(keep, got, at, rows, got_at=None):
    got_at = at if got_at is None else got_at
    return keep[at : at + rows, :].astype(F32) + got[got_at : got_at + rows, :].astype(F32)


def pack_sum(keep, keep_at, got, got_at, j):
    a = keep[keep_at + 2 * PACK * j : keep_at + 2 * PACK * (j + 1), :]
    b = got[got_at + 2 * PACK * j : got_at + 2 * PACK * (j + 1), :]
    return join_pair(a) + join_pair(b)


def add_packs(keep, got, targets):
    for j in range(C // LANES):
        pair = split_pair(pack_sum(*keep, *got, j))
        for ref, at in targets:
            ref[at + 2 * PACK * j : at + 2 * PACK * (j + 1), :] = pair


BLOCK = 48


def payload(s, which):
    early = BLOCK if ends_first(s) != bool(which) else 0
    late = BLOCK if which else 2 * BLOCK
    return len(EARLY[s]) * early, len(LATE[s]) * late, PACK_ROWS if s == PACK_STREAM else 0


def places(which):
    where, sizes = {}, []
    for g, (_, streams) in enumerate(round_groups(which)):
        at = 0
        for s in streams:
            where[s] = (g, at)
            at += sum(payload(s, which))
        sizes.append(at)
    return where, sizes


def keep_rows(s):
    early = len(EARLY[s]) * BLOCK
    return early if ends_first(s) else 2 * early, len(LATE[s]) * 2 * BLOCK, payload(s, 0)[2]


def third_kernel(*refs):
    refs = refs[: 2 * STREAMS] + refs[2 * STREAMS + 1 :]
    keeps, gots = refs[:STREAMS], refs[STREAMS : 2 * STREAMS]
    next_keeps, sends = refs[2 * STREAMS : 3 * STREAMS], refs[3 * STREAMS :]
    where, _ = places(0)
    for s in range(STREAMS):
        keep, got, out = keeps[s], gots[s], next_keeps[s]
        group, to = where[s]
        target = sends[group]
        early = len(EARLY[s]) * BLOCK
        at = 0
        for j in range(len(EARLY[s])):
            out[j * BLOCK : (j + 1) * BLOCK, :] = add(keep, got, at, BLOCK).astype(BF16)
            value = add(keep, got, at + BLOCK, BLOCK).astype(BF16)
            if ends_first(s):
                target[to + j * BLOCK : to + (j + 1) * BLOCK, :] = value
            else:
                out[early + j * BLOCK : early + (j + 1) * BLOCK, :] = value
            at += 2 * BLOCK
        base, to = keep_rows(s)[0], to + payload(s, 0)[0]
        half = 2 * BLOCK
        for j in range(len(LATE[s])):
            out[base + j * half : base + (j + 1) * half, :] = add(keep, got, at, half).astype(BF16)
            target[to + j * half : to + (j + 1) * half, :] = add(keep, got, at + half, half).astype(BF16)
            at += 2 * half
        if s == PACK_STREAM:
            spots = ((out, base + len(LATE[s]) * half), (target, to + len(LATE[s]) * half))
            add_packs((keep, at), (got, at), spots)


def fourth_kernel(*refs):
    groups = len(round_groups(0))
    refs = refs[: STREAMS + groups] + refs[STREAMS + groups + 1 :]
    keeps, gots = refs[:STREAMS], refs[STREAMS : STREAMS + groups]
    refs = refs[STREAMS + groups :]
    dones, next_keeps, sends = refs[:STREAMS], refs[STREAMS : 2 * STREAMS], refs[2 * STREAMS :]
    came, _ = places(0)
    where, _ = places(1)
    for s in range(STREAMS):
        keep, got, out = keeps[s], gots[came[s][0]], next_keeps[s]
        target, to = sends[where[s][0]], where[s][1]
        at = came[s][1]
        early = len(EARLY[s]) * BLOCK
        if ends_first(s):
            dones[s][...] = add(keep, got, 0, early, at)
        else:
            dones[s][...] = keep[:early, :].astype(F32)
            target[to : to + early, :] = keep[early : 2 * early, :]
        at, to, base = at + payload(s, 0)[0], to + payload(s, 1)[0], keep_rows(s)[0]
        for j in range(len(LATE[s])):
            first = base + 2 * BLOCK * j
            out[j * BLOCK : (j + 1) * BLOCK, :] = add(keep, got, first, BLOCK, at).astype(BF16)
            value = add(keep, got, first + BLOCK, BLOCK, at + BLOCK).astype(BF16)
            target[to + j * BLOCK : to + (j + 1) * BLOCK, :] = value
            at += 2 * BLOCK
        if s == PACK_STREAM:
            late = len(LATE[s]) * BLOCK
            add_packs((keep, base + 2 * late), (got, at), ((out, late), (target, to + late)))


def last_folds(kernel, operands, dep, shapes, name):
    return pl.pallas_call(
        kernel,
        in_specs=[VMEM] * len(operands) + [ANY],
        out_specs=[VMEM] * len(shapes),
        out_shape=tuple(near((rows, LANES), dtype) for rows, dtype in shapes),
        compiler_params=pltpu.CompilerParams(vmem_limit_bytes=SMALL_LIMIT),
        cost_estimate=COST,
        name=name,
    )(*operands, dep)


def fold_third(keeps, gots, dep):
    shapes = [(sum(keep_rows(s)), BF16) for s in range(STREAMS)]
    shapes += [(rows, BF16) for rows in places(0)[1]]
    flat = last_folds(third_kernel, [*keeps, *gots], dep, shapes, "fold_third")
    return flat[:STREAMS], flat[STREAMS:]


def fold_fourth(keeps, gots, dep):
    shapes = [(len(EARLY[s]) * BLOCK, F32) for s in range(STREAMS)]
    shapes += [(sum(payload(s, 1)[1:]), BF16) for s in range(STREAMS)]
    shapes += [(rows, BF16) for rows in places(1)[1]]
    flat = last_folds(fourth_kernel, [*keeps, *gots], dep, shapes, "fold_fourth")
    return flat[:STREAMS], flat[STREAMS : 2 * STREAMS], flat[2 * STREAMS :]


def end_kernel(rows, heads, core_ref, *refs):
    groups = len(round_groups(1))
    dones, keeps, gots = refs[:STREAMS], refs[STREAMS : 2 * STREAMS], refs[2 * STREAMS :][:groups]
    refs = refs[2 * STREAMS + groups :]
    out_ref, zx_ref, dt_ref, cx_ref, bx_ref, gate_ref, heads_ref = refs[:7]
    mine_ref, theirs_ref, shared_ref, bcdt_s = refs[7:]
    came, _ = places(1)

    def place(right, first, value):
        if right == "n":
            out_ref[:, first : first + LANES] = value
        elif right == "bcdt":
            bcdt_s[:, first : first + LANES] = value
        else:
            zx_ref[:, 0 if right == "dz" else 1, first : first + LANES] = value

    for s in range(STREAMS):
        got, at = gots[came[s][0]], came[s][1]
        for j, (_, right, first) in enumerate(EARLY[s]):
            value = dones[s][j * rows : (j + 1) * rows, :]
            if not ends_first(s):
                value = value + got[at : at + rows, :].astype(F32)
                at += rows
            place(right, first, value)
        for j, (_, right, first) in enumerate(LATE[s]):
            place(right, first, add(keeps[s], got, j * rows, rows, at))
            at += rows
        if s == PACK_STREAM:
            keep, keep_at = keeps[s], len(LATE[s]) * rows
            for j in range(C // LANES):
                lanes = slice(j * LANES, (j + 1) * LANES)
                value = pack_sum(keep, keep_at, got, at, j)
                cx_ref[:, lanes] = value[0:4]
                bx_ref[:, lanes] = value[4:5]
                gate_ref[:, lanes] = value[5:6]
                shared_ref[:, lanes] = value[6:8]
                if j == 10:
                    for k in range(3):
                        moved = pltpu.roll(value, (LANES - 32 * k) % LANES, 1) if k else value
                        heads_ref[k : k + 1, :] = moved[7:8, :heads]
    part = rows // 2
    mine_ref[...] = bcdt_s[pl.ds(pl.multiple_of(core_ref[0] * part, 8), part), : 2 * NS]
    theirs_ref[...] = bcdt_s[pl.ds(pl.multiple_of((1 - core_ref[0]) * part, 8), part), : 2 * NS]
    dt_ref[...] = bcdt_s[:, 2 * NS :].T[:heads, :]


def end(core, dones, keeps, gots, rows, heads):
    return pl.pallas_call(
        functools.partial(end_kernel, rows, heads),
        in_specs=[SMEM] + [VMEM] * (2 * STREAMS + len(gots)),
        out_specs=[VMEM] * 10,
        out_shape=(
            shape_of((rows, C), F32),
            shape_of((rows, 2, C), F32),
            shape_of((heads, rows), F32),
            shape_of((4, C), F32),
            shape_of((1, C), F32),
            shape_of((1, C), F32),
            shape_of((3, heads), F32),
            shape_of((rows // 2, 2 * NS), F32),
            shape_of((rows // 2, 2 * NS), F32),
            shape_of((2, C), F32),
        ),
        scratch_shapes=[pltpu.VMEM((rows, 3 * LANES), F32)],
        compiler_params=pltpu.CompilerParams(vmem_limit_bytes=SMALL_LIMIT),
        cost_estimate=COST,
        name="grad_end",
    )(core, *dones, *keeps, *gots)


def last_kernel(mine_ref, other_ref, shared_ref, other_shared_ref, bc_ref, norm_ref, conv_ref, bias_ref):
    bc_ref[...] = mine_ref[...] + other_ref[...]
    total = shared_ref[...] + other_shared_ref[...]
    norm_ref[...] = total[0:1]
    for k in range(4):
        conv_ref[k : k + 1, :] = total[1:2, 2 * NS * k : 2 * NS * (k + 1)]
    bias_ref[...] = total[1:2, 8 * NS : 10 * NS]


def last_sums(mine, other, shared, other_shared):
    return pl.pallas_call(
        last_kernel,
        in_specs=[VMEM] * 4,
        out_specs=[VMEM] * 4,
        out_shape=(
            shape_of(mine.shape, F32),
            shape_of((1, C), F32),
            shape_of((4, 2 * NS), F32),
            shape_of((1, 2 * NS), F32),
        ),
        compiler_params=pltpu.CompilerParams(vmem_limit_bytes=SMALL_LIMIT),
        cost_estimate=COST,
        name="last_sums",
    )(mine, other, shared, other_shared)


def pick_kernel(flag_ref, late0, late1, early0, early1, _, out_ref, token_ref, held, sem):
    for m, (late, early) in enumerate(((late0, early0), (late1, early1))):

        def start(source):
            pltpu.make_async_copy(source, held.at[m], sem.at[m]).start()

        pl.when(flag_ref[0] == 1)(lambda: start(late))
        pl.when(flag_ref[0] == 0)(lambda: start(early))
    for m in range(2):
        pltpu.make_async_copy(early0, held.at[m], sem.at[m]).wait()
        pltpu.make_async_copy(held.at[m], out_ref.at[m], sem.at[2 + m]).start()
    for m in range(2):
        pltpu.make_async_copy(held.at[m], out_ref.at[m], sem.at[2 + m]).wait()
    token_ref[...] = jnp.zeros(TOKEN, F32)


def pick(flag, late, early, dep):
    return pl.pallas_call(
        pick_kernel,
        in_specs=[SMEM] + [HBM] * 4 + [ANY],
        out_specs=[HBM, VMEM],
        out_shape=(far((2, T, D), F32), shape_of(TOKEN, F32)),
        scratch_shapes=[pltpu.VMEM((2, T, D), F32), pltpu.SemaphoreType.DMA((4,))],
        compiler_params=pltpu.CompilerParams(vmem_limit_bytes=SMALL_LIMIT),
        cost_estimate=COST,
        name="pick_section",
    )(flag, *[from_far(v) for v in (*late, *early)], dep)


def send(value, step):
    return lax.ppermute(value, "dp", [(i, to) for i, to in enumerate(step)])


def body(
    tokens,
    cotangent,
    lengths,
    norm_gain,
    w_zx,
    w_bc,
    w_dt,
    conv_x,
    bias_x,
    conv_bc,
    bias_bc,
    head_params,
    gate_gain,
    w_out,
):
    is_last = lax.axis_index("pipe") == 1
    core_at = lax.axis_index("tensor")
    heads = w_dt.shape[2]
    wts = SimpleNamespace(
        norm=norm_gain,
        zx=jnp.transpose(w_zx[0], (1, 0, 2)),
        bc=w_bc[0],
        dt=jnp.pad(w_dt[0].T, ((0, LANES - heads), (0, 0))),
        cx=conv_x[0],
        bx=bias_x,
        cbc=conv_bc[0],
        bbc=bias_bc,
        hp=jnp.transpose(head_params, (1, 0, 2)),
        gate=gate_gain,
        out=w_out[0],
    )

    flag = is_last.astype(jnp.int32).reshape(1)
    core = core_at.astype(jnp.int32).reshape(1)

    lens = lengths

    def run(m, role, u, dep):
        keep = SimpleNamespace(**forward(m, role, flag, lens, core, u, wts, dep))
        keep.u = u
        keep.part = (keep.part0, keep.part1)
        keep.other = tuple(swap(v) for v in keep.part)
        keep.other_sq = swap(keep.sq)
        return keep

    def backward(m, role, keep, e, dep):
        keep.e = e
        vars(keep).update(layer_back(m, role, flag, lens, core, e, keep, wts, dep))
        share(keep)

    def share(keep):
        keep.came, keep.left = swap(keep.theirs), swap(keep.mine)

    def send_down(keep):
        result = input_send(flag, core, keep, wts)
        return relay_down(result["low"]), result["token"]

    def finish(role, keep, dep):
        result = input_back(role, flag, core, keep, wts, dep)
        keep.du = result["du"]
        return result["token"]

    keep_a = run(0, 0, Rows(tokens, 0), (lens,))
    vars(keep_a).update(join(flag, core, keep_a, (lens,), True))
    sent_a = relay_up(keep_a.low)
    keep_b = run(1, 0, Rows(tokens, 1), keep_a.token)
    vars(keep_b).update(join(flag, core, keep_b, (sent_a,), True))
    sent_b = relay_up(keep_b.low)
    keep_c = run(0, 1, Halves(sent_a, swap(sent_a)), keep_b.token)
    sent_b = hold(sent_b, keep_c.token)
    keep_d = run(1, 1, Halves(sent_b, swap(sent_b)), keep_c.token)
    backward(0, 1, keep_c, Rows(cotangent, 0), keep_d.token)
    sent_c, token = send_down(keep_c)
    backward(1, 1, keep_d, Rows(cotangent, 1), token)
    sent_d, token = send_down(keep_d)
    backward(0, 0, keep_a, Halves(sent_c, swap(sent_c)), token)
    sent_d = hold(sent_d, keep_a.token)
    keep_b.e = Halves(sent_d, swap(sent_d))
    vars(keep_b).update(gate_back(flag, core, keep_b.e, keep_b, wts, (touch(keep_a.came, *[keep.left for keep in (keep_a, keep_c, keep_d)]),)))

    dp = lax.axis_size("dp")
    maps = partners()
    me = lax.axis_index("dp")
    tables = [
        jnp.asarray(np.stack([block_order(maps, s, late) for s in range(STREAMS)], axis=1).reshape(-1))
        for late in range(2)
    ]
    flag = jnp.stack([is_last.astype(jnp.int32), me.astype(jnp.int32) * (STREAMS * dp)])

    def both(name):
        return tuple(getattr(keep, name) for keep in (keep_c, keep_d, keep_a, keep_b))

    arrays = [both(k) for k in ("et", "n", "rt", "dz")]
    keeps, sends, token = early_grads(flag, tables[0], arrays, dp)
    gots = [send(sends[s], maps[dims_of(s, 0)[0]]) for s in range(STREAMS)]
    vars(keep_b).update(scan_back(1, flag, lens, core, keep_b, wts, (token,)))
    share(keep_b)
    arrays = [both(k) for k in ("rt", "dx", "bcdt")]
    keeps, sends, token = late_grads(flag, tables[1], arrays, dp, both("pack"), keeps, gots)
    layers = ((0, keep_a), (0, keep_b), (1, keep_c), (1, keep_d))
    tokens_in = [finish(role, keep, (token,)) for role, keep in layers]
    join_c = SimpleNamespace(**join(flag, core, keep_c, (token,), False))
    join_d = SimpleNamespace(**join(flag, core, keep_d, (token,), False))
    deps = [[*tokens_in, join_c.token, join_d.token]]
    section_out, token_a = pick(
        flag, (join_c.res, join_d.res), (keep_a.res, keep_b.res), token
    )
    section_grad, token_b = pick(flag, (keep_c.du, keep_d.du), (keep_a.du, keep_b.du), token)
    deps += [[]]
    early, late = D // 4, D // 2
    gots = [send(sends[s], maps[dims_of(s, 1)[0]]) for s in range(STREAMS)]
    token = None
    for k in range(1, 3):
        for s in range(STREAMS):
            after = [(token,)] if token is not None else []
            if s == 0:
                after += deps[k - 1]
            keeps[s], sends[s], token = fold(s, keeps[s], gots[s], early, late, after)
            gots[s] = send(sends[s], maps[dims_of(s, 1)[k]])
        early, late = early // 2, late // 2
    keeps, sends = fold_third(keeps, gots, token_a)
    gots = [send(v, maps[d]) for v, (d, _) in zip(sends, round_groups(0))]
    dones, keeps, sends = fold_fourth(keeps, gots, token_b)
    gots = [send(v, maps[d]) for v, (d, _) in zip(sends, round_groups(1))]
    g_out, g_zx, g_dt, g_cx, g_bx, g_gate, g_heads, mine, theirs, shared = end(
        core, dones, keeps, gots, D // dp, heads
    )
    g_bc, g_norm, g_cbc, g_bbc = last_sums(mine, swap(theirs), shared, swap(shared))
    return (
        section_out[None],
        section_grad[None],
        g_norm,
        g_zx[None],
        g_bc[None],
        g_dt.T[None],
        g_cx[None],
        g_bx,
        g_cbc[None],
        g_bbc,
        g_heads[None],
        g_gate,
        g_out.T[None],
    )


def solution(mesh):
    in_specs = (
        P(None, "dp", None),
        P(None, "dp", None),
        P(None, "dp", None),
        P("pipe", None),
        P("pipe", None, None, "tensor"),
        P("pipe", None, None),
        P("pipe", None, "tensor"),
        P("pipe", None, "tensor"),
        P("pipe", "tensor"),
        P("pipe", None, None),
        P("pipe", None),
        P("pipe", None, "tensor"),
        P("pipe", "tensor"),
        P("pipe", "tensor", None),
    )
    out_specs = (
        P("pipe", None, "dp", None),
        P("pipe", None, "dp", None),
        P("pipe", None),
        P("pipe", "dp", None, "tensor"),
        P("pipe", ("dp", "tensor"), None),
        P("pipe", "dp", "tensor"),
        P("pipe", None, "tensor"),
        P("pipe", "tensor"),
        P("pipe", None, None),
        P("pipe", None),
        P("pipe", None, "tensor"),
        P("pipe", "tensor"),
        P("pipe", "tensor", "dp"),
    )
    return jax.shard_map(body, mesh=mesh, in_specs=in_specs, out_specs=out_specs, check_vma=False)
```
